32 devices in a mesh: seq: 16 (over z, y, x), state: 2 (over core).
Axes of the slice: x: 2, y: 2, z: 4, core: 2. Of those that a mesh axis runs over, the one named last changes fastest.
Arguments:
- tokens: bfloat16 [4, 4096, 512], P(None, 'seq', 'state'), may hold values from -6 to 6
- batchnorm_gain: bfloat16 [2, 512], P(None, 'state'), may hold values from 0.5 to 1.5
- batchnorm_bias: bfloat16 [2, 512], P(None, 'state'), may hold values from -3 to 3
- in_proj: bfloat16 [2, 512, 2, 256], P(None, None, None, 'state'), may hold values from -0.25 to 0.25
- out_proj: bfloat16 [2, 2, 256, 512], P(None, None, 'state'), may hold values from -0.25 to 0.25
- rate_log: bfloat16 [2, 256], P(None, 'state'), may hold values from -13 to -2
- angle_log: bfloat16 [2, 256], P(None, 'state'), may hold values from -4.59375 to 1
- skip_gain: bfloat16 [2, 512], P(None, 'state'), may hold values from -4 to 4
- glu_lin: bfloat16 [2, 512, 512], P(None, None, 'state'), may hold values from -0.25 to 0.25
- glu_gate: bfloat16 [2, 512, 512], P(None, None, 'state'), may hold values from -0.25 to 0.25
- positions: int32 [4, 16], replicated, may hold values from 0 to 4095, as said below
- cotangent: bfloat16 [4, 4096, 512], P(None, 'seq', 'state'), may hold values from -6 to 6
Outputs:
- block_out: bfloat16 [4, 4096, 512], P(None, 'seq', 'state')
- input_grad: float32 [4, 4096, 512], P(None, 'seq', 'state')
- norm_gain_gradient: float32 [2, 512], P(None, 'state')
- bias_grad: float32 [2, 512], P(None, 'state')
- in_grad: float32 [2, 512, 2, 256], P(None, None, None, 'state')
- out_grad: float32 [2, 2, 256, 512], P(None, None, 'state')
- rate_grad: float32 [2, 256], P(None, 'state')
- angle_grad: float32 [2, 256], P(None, 'state')
- skip_grad: float32 [2, 512], P(None, 'state')
- lin_grad: float32 [2, 512, 512], P(None, None, 'state')
- gate_grad: float32 [2, 512, 512], P(None, None, 'state')
The draws below stay inside these ranges and needn't reach their ends.
Inputs may be any that keep to these rules, and one draw needn't show every extreme that they name: Each row lists 16 positions at which a document starts, in order, the first 0; repeats may occur. In one row all are 0.
All inputs are finite; a program needn't handle non-finite values.
Results may differ from the reference program's by a relative error of at most 0.02.
Values may be sent and summed in bfloat16 or wider, within the bound.
No kernel may reach another device: no remote copies, remote signals or barrier semaphores. Data moves between devices by JAX's collectives and lax.ppermute only.
A program may use at most 128 MiB of HBM per device.

```python
from functools import partial
import jax
import jax.numpy as jnp
from jax import lax

D = 512
N = 256
ROWS = 4
DOCS = 16
LENGTH = 4096


def draw_rate_log(key, part):
    key = jax.random.fold_in(key, 7)
    chooser_key, slow_key, fast_key = jax.random.split(key, 3)
    slow_share = 0.5
    chooser = jax.random.uniform(chooser_key, (2, N), jnp.float32)
    slow_rate = jnp.log(0.3 / LENGTH) + jax.random.uniform(slow_key, (2, N), jnp.float32) * jnp.log(2.0 / 0.3)
    fast_rate = jnp.log(1.0 / 50.0) + jax.random.uniform(fast_key, (2, N), jnp.float32) * jnp.log(2.5)
    return jnp.where(chooser < slow_share, slow_rate, fast_rate).astype(jnp.bfloat16)


def draw_positions(key, part):
    key = jax.random.fold_in(key, 13)
    perm_key, row_key = jax.random.split(key)
    row_keys = jax.random.split(perm_key, ROWS)
    shuffled = jax.vmap(lambda one_key: jax.random.permutation(one_key, LENGTH - 1))(row_keys)
    picked = jnp.sort(shuffled[:, :DOCS - 1] + 1, axis=1).astype(jnp.int32)
    starts = jnp.concatenate([jnp.zeros((ROWS, 1), jnp.int32), picked], axis=1)
    whole_row = jax.random.randint(row_key, (), 0, ROWS)
    row_ids = jnp.arange(ROWS, dtype=jnp.int32)[:, None]
    column_ids = jnp.arange(DOCS, dtype=jnp.int32)[None, :]
    starts = jnp.where(row_ids == whole_row, 0, starts)
    last_row = (whole_row + 1) % ROWS
    starts = jnp.where((row_ids == last_row) & (column_ids == DOCS - 1), LENGTH - 1, starts)
    return starts.astype(jnp.int32)


def level_of(stream_key, extent, cuts, smallest, largest):
    def one(axis_at, blocks):
        heights = jax.random.uniform(jax.random.fold_in(jax.random.fold_in(stream_key, 6), axis_at), (blocks,), jnp.float32, smallest / len(cuts), largest / len(cuts))
        return jnp.repeat(jnp.exp(heights), extent[axis_at] // blocks).reshape((-1,) + (1,) * (len(extent) - axis_at - 1))

    factor_of = one(*cuts[0])
    for cut in cuts[1:]:
        factor_of = factor_of * one(*cut)
    return factor_of


def gaussian(stream_key, dims, width, bound, shards=(), kind=jnp.bfloat16):
    drawn = width * jax.random.normal(stream_key, dims, jnp.float32)
    if shards:
        drawn = drawn * level_of(stream_key, dims, shards, -0.22, 0.18)
    return jnp.clip(drawn, -bound, bound).astype(kind)


def setup_inputs(seed: int = 0) -> dict:
    key_of = jax.random.split(jax.random.key(seed), 13)
    tokens = gaussian(key_of[0], (ROWS, LENGTH, D), 1.0, 6.0, ((1, 16), (2, 2)))
    batchnorm_gain = jnp.clip(1.0 + 0.1 * jax.random.normal(key_of[1], (2, D), jnp.float32), 0.5, 1.5).astype(jnp.bfloat16)
    batchnorm_bias = gaussian(key_of[2], (2, D), 0.5, 3.0, ((1, 2),))
    in_proj = gaussian(key_of[3], (2, D, 2, N), D ** -0.5, 0.25, ((3, 2),))
    out_proj = gaussian(key_of[4], (2, 2, N, D), (2 * N) ** -0.5, 0.25, ((2, 2),))
    rate_log = draw_rate_log(jax.random.fold_in(key_of[12], 71), 0)
    angle_log = jnp.clip(-4.59375 + 5.59375 * jax.random.uniform(key_of[6], (2, N), jnp.float32) ** level_of(key_of[6], (2, N), ((1, 2),), -0.2, 0.2), -4.59375, 1.0).astype(jnp.bfloat16)
    skip_gain = gaussian(key_of[7], (2, D), 1.0, 4.0, ((1, 2),))
    glu_lin = gaussian(key_of[8], (2, D, D), D ** -0.5, 0.25, ((2, 2),))
    glu_gate = gaussian(key_of[9], (2, D, D), D ** -0.5, 0.25, ((2, 2),))
    positions = draw_positions(jax.random.fold_in(key_of[12], 71), 0)
    cotangent = gaussian(key_of[11], (ROWS, LENGTH, D), 1.0, 6.0, ((1, 16), (2, 2)))
    return dict(tokens=tokens, batchnorm_gain=batchnorm_gain, batchnorm_bias=batchnorm_bias, in_proj=in_proj, out_proj=out_proj, rate_log=rate_log, angle_log=angle_log, skip_gain=skip_gain, glu_lin=glu_lin, glu_gate=glu_gate, positions=positions, cotangent=cotangent)


@jax.custom_vjp
def low(v):
    return lax.optimization_barrier(v.astype(jnp.bfloat16)).astype(jnp.float32)

@jax.custom_vjp
def low_back(v):
    return v

def low_keep(v):
    return (low(v), None)

def low_pass(kept, grad):
    return (grad,)

def back_keep(v):
    return (v, None)

def back_low(kept, grad):
    return (low(grad),)
low.defvjp(low_keep, low_pass)
low_back.defvjp(back_keep, back_low)
norm_eps = 1e-05
block_len = 64

def dot_high(left, right):
    return jnp.dot(left, right, precision=lax.Precision.HIGHEST, preferred_element_type=jnp.float32)

def decay_terms(rate_log, angle_log):
    rate_now = jnp.exp(rate_log)
    modulus = jnp.exp(-rate_now)
    angle_now = jnp.exp(angle_log)
    return (modulus * jnp.cos(angle_now), modulus * jnp.sin(angle_now), jnp.sqrt(1.0 - modulus * modulus))

def compose(earlier, latter):
    early_ar, early_ai, early_br, early_bi = earlier
    late_ar, late_ai, late_br, late_bi = latter
    return (late_ar * early_ar - late_ai * early_ai, late_ar * early_ai + late_ai * early_ar, late_ar * early_br - late_ai * early_bi + late_br, late_ar * early_bi + late_ai * early_br + late_bi)

def run_row(coef_re, coef_im, drive_re, drive_im, reverse):
    pieces = tuple((member.reshape(LENGTH // block_len, block_len, N) for member in (coef_re, coef_im, drive_re, drive_im)))

    def advance(carried_along, block_part):
        acc_re, acc_im, part_re, part_im = lax.associative_scan(compose, block_part, reverse=reverse, axis=0)
        out_re = part_re + acc_re * carried_along[0] - acc_im * carried_along[1]
        out_im = part_im + acc_re * carried_along[1] + acc_im * carried_along[0]
        edge_at = 0 if reverse else block_len - 1
        return ((out_re[edge_at], out_im[edge_at]), (out_re, out_im))
    initial = (jnp.zeros((N,), jnp.float32), jnp.zeros((N,), jnp.float32))
    final_carry, stacked = lax.scan(jax.checkpoint(advance), initial, pieces, reverse=reverse)
    return (stacked[0].reshape(LENGTH, N), stacked[1].reshape(LENGTH, N))

def block_row(params, row_inputs, reverse):
    batch_mean, reciprocal_deviation, batchnorm_gain, batchnorm_bias, in_proj, out_proj, rate_log, angle_log, skip_gain, glu_lin, glu_gate = params
    block_inputs, keep_here = row_inputs
    normed_rows = (block_inputs - batch_mean) * reciprocal_deviation * batchnorm_gain + batchnorm_bias
    normed_low = low(normed_rows)
    projected = low_back(dot_high(normed_low, in_proj.reshape(D, 2 * N)))
    lam_re, lam_im, scale_in = decay_terms(rate_log, angle_log)
    h_re, h_im = run_row(lam_re * keep_here, lam_im * keep_here, scale_in * projected[:, :N], scale_in * projected[:, N:], reverse)
    states_low = low(jnp.concatenate([h_re, h_im], axis=1))
    mixed_output = low_back(dot_high(states_low, out_proj.reshape(2 * N, D))) + skip_gain * normed_rows
    active = low(jax.nn.gelu(mixed_output, approximate=True))
    linear = low_back(dot_high(active, glu_lin))
    gating = low_back(dot_high(active, glu_gate))
    return block_inputs + linear * jax.nn.sigmoid(gating)

def run_block(block_inputs, weights, keep_mask, reverse):
    batch_mean = lax.optimization_barrier(jnp.mean(block_inputs, axis=(0, 1)))
    reciprocal_deviation = lax.rsqrt(lax.optimization_barrier(jnp.mean(block_inputs * block_inputs, axis=(0, 1))) - batch_mean * batch_mean + norm_eps)
    params = (batch_mean, reciprocal_deviation) + tuple(weights)
    row_fn = jax.checkpoint(partial(block_row, reverse=reverse))
    return lax.map(lambda row_inputs: row_fn(params, row_inputs), (block_inputs, keep_mask))

def reference(tokens, batchnorm_gain, batchnorm_bias, in_proj, out_proj, rate_log, angle_log, skip_gain, glu_lin, glu_gate, positions, cotangent):
    times = jnp.arange(LENGTH, dtype=jnp.int32)
    hit_now = jnp.any(positions[:, None, :] == times[None, :, None], axis=2)
    hit_next = jnp.any(positions[:, None, :] == times[None, :, None] + 1, axis=2)
    mask_fwd = jnp.where(hit_now, 0.0, 1.0).astype(jnp.float32)[:, :, None]
    mask_bwd = jnp.where(hit_next, 0.0, 1.0).astype(jnp.float32)[:, :, None]
    weights = tuple((member.astype(jnp.float32) for member in (batchnorm_gain, batchnorm_bias, in_proj, out_proj, rate_log, angle_log, skip_gain, glu_lin, glu_gate)))

    def forward(block_inputs, *params):
        first_out = run_block(block_inputs, tuple((member[0] for member in params)), mask_fwd, False)
        return run_block(first_out, tuple((member[1] for member in params)), mask_bwd, True)
    result, pullback = jax.vjp(forward, tokens.astype(jnp.float32), *weights)
    grads = pullback(cotangent.astype(jnp.float32))
    return (result.astype(jnp.bfloat16), grads[0], grads[1], grads[2], grads[3], grads[4], grads[5], grads[6], grads[7], grads[8], grads[9])
```

```python
import functools

import jax
import jax.numpy as jnp
from jax import lax
from jax.experimental import pallas as pl
from jax.experimental.pallas import tpu as pltpu
from jax.sharding import PartitionSpec as P

f32, bf16 = jnp.float32, jnp.bfloat16
norm_eps = 1e-05
CHUNKS = 8
SLAB = 2 * CHUNKS


def mm(a, b):
    return jnp.dot(a, b, preferred_element_type=f32)


def mm_nt(a, b):
    return lax.dot_general(a, b, (((1,), (1,)), ((), ())), preferred_element_type=f32)


def mm_tn(a, b):
    return lax.dot_general(a, b, (((0,), (0,)), ((), ())), preferred_element_type=f32)


def wide(row):
    return jnp.broadcast_to(row, (CHUNKS, 128))


def cmul(ar, ai, br, bi):
    return ar * br - ai * bi, ar * bi + ai * br


def row_of_tiles(tiles):
    return jnp.concatenate([tiles[i : i + 1, :] for i in range(tiles.shape[0])], axis=1)


def channel_row(core, own, oth, at):
    mine, other = own[at : at + 2, :], oth[at : at + 2, :]
    low = jnp.where(core == 0, mine, other)
    high = jnp.where(core == 0, other, mine)
    return jnp.concatenate([low[0:1], low[1:2], high[0:1], high[1:2]], axis=1)


def own_cols(core, width):
    return pl.ds(pl.multiple_of(core * width, width), width)


def oth_cols(core, width):
    return pl.ds(pl.multiple_of((1 - core) * width, width), width)


def scan(drive, lams, keep_ref, which, steps, reverse, start, visit):
    order = range(steps - 1, -1, -1) if reverse else range(steps)
    state = dict(start)
    for s in order:
        for row in range(2):
            at = s * SLAB + row * CHUNKS
            keep = keep_ref[which, at : at + CHUNKS, :]
            for half in range(2):
                lr, li = lams[half]
                hr, hi = state[half, row]
                hr, hi = keep * hr, keep * hi
                dr, di = drive(s, row, half)
                state[half, row] = (lr * hr - li * hi + dr, lr * hi + li * hr + di)
        visit(s, state, keep_ref)
    return state


def keep_products(keep_ref, which, steps):
    out = []
    for row in range(2):
        total = keep_ref[which, row * CHUNKS : (row + 1) * CHUNKS, :]
        for s in range(1, steps):
            at = s * SLAB + row * CHUNKS
            total = total * keep_ref[which, at : at + CHUNKS, :]
        out.append(total)
    return out


def chunk_scan(ends, keeps, powers, reverse, comp_ref, packed):
    index = lax.broadcasted_iota(jnp.int32, (CHUNKS, 128), 0)

    def shifted(value, by, fill):
        turned = pltpu.roll(value, CHUNKS - by if reverse else by, 0)
        valid = index < CHUNKS - by if reverse else index >= by
        return jnp.where(valid, turned, fill)

    for half in range(2):
        for row in range(2):
            er, ei = ends[half, row]
            pr, pi = powers[half][0] * keeps[row], powers[half][1] * keeps[row]
            for by in (1, 2, 4):
                tr, ti = cmul(pr, pi, shifted(er, by, 0.0), shifted(ei, by, 0.0))
                er, ei = er + tr, ei + ti
                pr, pi = cmul(pr, pi, shifted(pr, by, 1.0), shifted(pi, by, 0.0))
            edge = 0 if reverse else CHUNKS - 1
            q = row * 2 + half
            packed[q : q + 1, :] = er[edge : edge + 1, :]
            packed[4 + q : 5 + q, :] = ei[edge : edge + 1, :]
            base = (half * 2 + row) * 4
            comp_ref[base] = shifted(er, 1, 0.0)
            comp_ref[base + 1] = shifted(ei, 1, 0.0)
            comp_ref[base + 2] = shifted(pr, 1, 1.0)
            comp_ref[base + 3] = shifted(pi, 1, 0.0)


def device_carry(me, peers, got_ref, dk_ref, which, own, oth, base, conj, reverse, packed):
    index = lax.broadcasted_iota(jnp.int32, (CHUNKS, 128), 0)
    is_own = index % 2 == 0
    sign = jnp.where(index < 4, -1.0, 1.0) * (-1.0 if conj else 1.0)
    ar = jnp.where(is_own, wide(own[base + 11 : base + 12, :]), wide(oth[base + 11 : base + 12, :]))
    ai = jnp.where(is_own, wide(own[base + 12 : base + 13, :]), wide(oth[base + 12 : base + 13, :]))
    ai = ai * sign

    def step(k, held):
        at = peers - 1 - k if reverse else k
        reached = at > me if reverse else at < me
        new = dk_ref[which, at] * (ar * held + ai * pltpu.roll(held, 4, 0)) + got_ref[at]
        return jnp.where(reached, new, held)

    packed[...] = lax.fori_loop(0, peers, step, jnp.zeros((8, 128), f32), unroll=peers <= 16)


def entries(comp_ref, packed):
    start = {}
    for half in range(2):
        for row in range(2):
            base, q = (half * 2 + row) * 4, row * 2 + half
            hr, hi = wide(packed[q : q + 1, :]), wide(packed[4 + q : 5 + q, :])
            tr, ti = cmul(comp_ref[base + 2], comp_ref[base + 3], hr, hi)
            start[half, row] = (comp_ref[base] + tr, comp_ref[base + 1] + ti)
    return start


def decay(own, oth, base, at, conj=False):
    sign = -1.0 if conj else 1.0
    return [(wide(r[base + at : base + at + 1, :]), sign * wide(r[base + at + 1 : base + at + 2, :])) for r in (own, oth)]


def scales(own, oth, base):
    return [wide(r[base + 8 : base + 9, :]) for r in (own, oth)]


def nothing(*_):
    return None


def zeros_start():
    zero = jnp.zeros((CHUNKS, 128), f32)
    return {(half, row): (zero, zero) for half in range(2) for row in range(2)}


def part(s, row):
    at = s * SLAB + row * CHUNKS
    return slice(at, at + CHUNKS)


def cols(half, im):
    at = half * 256 + im * 128
    return slice(at, at + 128)


def spread(out_ref, packed):
    out_ref[...] = jnp.broadcast_to(packed[...][None], out_ref.shape)


def prep_kernel(peers, steps, info, pos, tokens, gain, bias, skip, rate_log, angle_log, stats, small, keep, dk, perm):
    seq, core = info[0], info[1]
    rows, span, _ = tokens.shape
    docs = pos.shape[1]
    s1 = s2 = 0.0
    for r in range(rows):
        x = tokens[r].astype(f32)
        s1 = s1 + jnp.sum(x, axis=0, keepdims=True)
        s2 = s2 + jnp.sum(x * x, axis=0, keepdims=True)
    for i in range(2):
        stats[0, i : i + 1, :] = s1[:, 128 * i : 128 * (i + 1)]
        stats[0, 2 + i : 3 + i, :] = s2[:, 128 * i : 128 * (i + 1)]
    stats[...] = jnp.broadcast_to(stats[0][None], stats.shape)

    small[...] = jnp.zeros_like(small)
    for k in range(2):
        at = 16 * k
        for j, ref in enumerate((gain, bias, skip)):
            v = ref[...].astype(f32)
            small[at + 2 * j : at + 2 * j + 1, :] = v[k : k + 1, :128]
            small[at + 2 * j + 1 : at + 2 * j + 2, :] = v[k : k + 1, 128:]
        rate = jnp.exp(rate_log[...].astype(f32)[k : k + 1, :])
        angle = jnp.exp(angle_log[...].astype(f32)[k : k + 1, :])
        modulus = jnp.exp(-rate)
        lr, li = modulus * jnp.cos(angle), modulus * jnp.sin(angle)
        small[at + 6 : at + 7, :] = lr
        small[at + 7 : at + 8, :] = li
        small[at + 8 : at + 9, :] = jnp.sqrt(1.0 - modulus * modulus)
        power = 1
        while power < span:
            lr, li = cmul(lr, li, lr, li)
            power *= 2
            if power == steps:
                small[at + 9 : at + 10, :] = lr
                small[at + 10 : at + 11, :] = li
        small[at + 11 : at + 12, :] = lr
        small[at + 12 : at + 13, :] = li

    chunk = lax.broadcasted_iota(jnp.int32, (CHUNKS, 128), 0) * steps + seq * span
    for row in range(2):
        targets = [pos[core * 2 + row, d] - chunk for d in range(docs)]
        for s in range(steps + 1):
            hit = targets[0] == s
            for t in targets[1:]:
                hit = jnp.logical_or(hit, t == s)
            value = jnp.where(hit, 0.0, 1.0)
            at = s * SLAB + row * CHUNKS
            if s < steps:
                keep[0, at : at + CHUNKS, :] = value
            if s >= 1:
                keep[1, at - SLAB : at - SLAB + CHUNKS, :] = value

    first_row = (lax.broadcasted_iota(jnp.int32, (CHUNKS, 128), 0) // 2) % 2 == 0
    owners = ([], [])
    for d in range(docs):
        a, b = pos[core * 2, d], pos[core * 2 + 1, d]
        owners[0].append(jnp.where(first_row, a // span, b // span))
        owners[1].append(jnp.where(first_row, (a + span - 1) // span - 1, (b + span - 1) // span - 1))

    def mark(j, _):
        for m in range(2):
            hit = owners[m][0] == j
            for o in owners[m][1:]:
                hit = jnp.logical_or(hit, o == j)
            dk[m, j] = jnp.where(hit, 0.0, 1.0)
        return 0

    lax.fori_loop(0, peers, mark, 0)

    count = perm.shape[0]
    p = lax.broadcasted_iota(jnp.int32, (count, count), 0)
    q = lax.broadcasted_iota(jnp.int32, (count, count), 1)
    source = ((p >> 3) & 1) * span + (p & 7) * steps + (p >> 4)
    perm[...] = jnp.where(q == source, 1.0, 0.0).astype(bf16)


def norm_rows(total, squares, count, core, own, oth, base, nrm):
    mean = total / count
    inv = lax.rsqrt(squares / count - mean * mean + norm_eps)
    nrm[0:1, :] = mean
    nrm[1:2, :] = inv
    nrm[2:3, :] = channel_row(core, own, oth, base)
    nrm[3:4, :] = channel_row(core, own, oth, base + 2)
    nrm[4:5, :] = channel_row(core, own, oth, base + 4)
    nrm[5:8, :] = jnp.zeros_like(nrm[5:8, :])


def normalized(x, nrm):
    xhat = (x - nrm[0:1, :]) * nrm[1:2, :]
    return xhat, xhat * nrm[2:3, :] + nrm[3:4, :]


def project_and_scan(steps, base, which, reverse, own, oth, keep, win_own, win_oth, nl, proj, comp, summ, packed):
    proj[:, :256] = mm(nl[...], win_own[...])
    proj[:, 256:] = mm(nl[...], win_oth[...])
    lams, sc = decay(own, oth, base, 6), scales(own, oth, base)

    def drive(s, row, half):
        return sc[half] * proj[part(s, row), cols(half, 0)], sc[half] * proj[part(s, row), cols(half, 1)]

    ends = scan(drive, lams, keep, which, steps, reverse, zeros_start(), nothing)
    chunk_scan(ends, keep_products(keep, which, steps), decay(own, oth, base, 9), reverse, comp, packed)
    spread(summ, packed)


def enter_first_kernel(peers, steps, count, info, got, x_own, x_oth, perm, own, oth, keep, win_own, win_oth,
                       xp, nl, proj, comp, summ, nrm, packed):
    core = info[1]
    sums = got[0:2]
    for j in range(1, peers):
        sums = sums + got[2 * j : 2 * j + 2]
    total = jnp.concatenate([sums[0, 0:1], sums[0, 1:2], sums[1, 0:1], sums[1, 1:2]], axis=1)
    squares = jnp.concatenate([sums[0, 2:3], sums[0, 3:4], sums[1, 2:3], sums[1, 3:4]], axis=1)
    norm_rows(total, squares, count, core, own, oth, 0, nrm)
    xp[:, own_cols(core, 256)] = mm(perm[...], x_own[...]).astype(bf16)
    xp[:, oth_cols(core, 256)] = mm(perm[...], x_oth[...]).astype(bf16)
    _, normed = normalized(xp[...].astype(f32), nrm)
    nl[...] = normed.astype(bf16)
    project_and_scan(steps, 0, 0, False, own, oth, keep, win_own, win_oth, nl, proj, comp, summ, packed)


def sum_peers(got):
    total = got[0]
    for j in range(1, got.shape[0]):
        total = total + got[j]
    return total


def enter_second_kernel(peers, steps, count, info, got, x, own, oth, keep, win_own, win_oth,
                        nl, proj, comp, summ, nrm, packed):
    core = info[1]
    sums = sum_peers(got)
    norm_rows(row_of_tiles(sums[0:4]), row_of_tiles(sums[4:8]), count, core, own, oth, 16, nrm)
    _, normed = normalized(x[...], nrm)
    nl[...] = normed.astype(bf16)
    project_and_scan(steps, 16, 1, True, own, oth, keep, win_own, win_oth, nl, proj, comp, summ, packed)


def states_of(peers, steps, base, which, reverse, info, got, comp, dk, own, oth, keep, proj, hx, sl, packed):
    device_carry(info[0], peers, got, dk, which, own, oth, base, False, reverse, packed)
    start = entries(comp, packed)
    lams, sc = decay(own, oth, base, 6), scales(own, oth, base)
    shift = 0 if reverse else 1
    first = steps if reverse else 0
    for (half, row), (hr, hi) in start.items():
        hx[part(first, row), cols(half, 0)] = hr
        hx[part(first, row), cols(half, 1)] = hi

    def drive(s, row, half):
        return sc[half] * proj[part(s, row), cols(half, 0)], sc[half] * proj[part(s, row), cols(half, 1)]

    def visit(s, state, _):
        for half in range(2):
            for im in range(2):
                both = jnp.concatenate([state[half, row][im] for row in range(2)], axis=0)
                at = (s + shift) * SLAB
                hx[at : at + SLAB, cols(half, im)] = both
                sl[s * SLAB : (s + 1) * SLAB, cols(half, im)] = both.astype(bf16)

    scan(drive, lams, keep, which, steps, reverse, start, visit)


def mix_and_gate(core, x, nrm, sl, wout_own, wout_oth, lin_own, lin_oth, gate_own, gate_oth, gp, act, sig, qv, y):
    _, normed = normalized(x[...].astype(f32), nrm)
    mixed = mm(sl[:, :256], wout_own[...]) + mm(sl[:, 256:], wout_oth[...]) + nrm[4:5, :] * normed
    c = 0.7978845608028654
    sq = mixed * mixed
    t = jnp.tanh(c * (mixed + 0.044715 * sq * mixed))
    act[...] = (0.5 * mixed * (1.0 + t)).astype(bf16)
    gp[...] = 0.5 * (1.0 + t) + 0.5 * mixed * (1.0 - t * t) * (c * (1.0 + 3 * 0.044715 * sq))
    for w_lin, w_gate, at in ((lin_own, gate_own, own_cols(core, 256)), (lin_oth, gate_oth, oth_cols(core, 256))):
        linear = mm(act[...], w_lin[...])
        gating = mm(act[...], w_gate[...])
        sg = 0.5 + 0.5 * jnp.tanh(0.5 * gating)
        out = linear * sg
        sig[:, at] = sg
        qv[:, at] = out * (1.0 - sg)
        y[:, at] = x[:, at].astype(f32) + out


def leave_first_kernel(peers, steps, info, got, comp, dk, own, oth, keep, proj, x, nrm, wout_own, wout_oth,
                       lin_own, lin_oth, gate_own, gate_oth, hx, sl, gp, act, sig, qv, y, stats, packed):
    states_of(peers, steps, 0, 0, False, info, got, comp, dk, own, oth, keep, proj, hx, sl, packed)
    mix_and_gate(info[1], x, nrm, sl, wout_own, wout_oth, lin_own, lin_oth, gate_own, gate_oth, gp, act, sig, qv, y)
    out = y[...]
    pack_two(jnp.sum(out, axis=0, keepdims=True), jnp.sum(out * out, axis=0, keepdims=True), packed)
    spread(stats, packed)


def pack_two(a, b, packed):
    for i in range(4):
        packed[i : i + 1, :] = a[:, 128 * i : 128 * (i + 1)]
        packed[4 + i : 5 + i, :] = b[:, 128 * i : 128 * (i + 1)]


def glu_backward(steps, base, adj_which, adj_reverse, core, d_out, nrm, x, sl, gp, act, sig, qv, own, oth, keep, wout_own, wout_oth,
                 lin_own, lin_oth, gate_own, gate_oth, g_own, g_oth, skip_row, dmix, dst, comp, summ, packed, dl, dg, dml):
    dl[...] = (d_out * sig[...]).astype(bf16)
    dg[...] = (d_out * qv[...]).astype(bf16)
    mine, other = own_cols(core, 256), oth_cols(core, 256)
    d_active = (mm_nt(dl[:, mine], lin_own[...]) + mm_nt(dg[:, mine], gate_own[...])
                + mm_nt(dl[:, other], lin_oth[...]) + mm_nt(dg[:, other], gate_oth[...]))
    d_mixed = d_active * gp[...]
    dmix[...] = d_mixed
    _, normed = normalized(x[...].astype(f32), nrm)
    skip_row[0:1, :] = jnp.sum(d_mixed * normed, axis=0, keepdims=True)
    dml[...] = d_mixed.astype(bf16)
    dst[:, :256] = mm_nt(dml[...], wout_own[...])
    dst[:, 256:] = mm_nt(dml[...], wout_oth[...])
    lams = decay(own, oth, base, 6, conj=True)

    def drive(s, row, half):
        return dst[part(s, row), cols(half, 0)], dst[part(s, row), cols(half, 1)]

    ends = scan(drive, lams, keep, adj_which, steps, adj_reverse, zeros_start(), nothing)
    chunk_scan(ends, keep_products(keep, adj_which, steps), decay(own, oth, base, 9, conj=True), adj_reverse, comp, packed)
    spread(summ, packed)
    g_own[0:512, :] = mm_tn(act[...], dl[:, mine])
    g_oth[0:512, :] = mm_tn(act[...], dl[:, other]).astype(bf16)
    g_own[512:1024, :] = mm_tn(act[...], dg[:, mine])
    g_oth[512:1024, :] = mm_tn(act[...], dg[:, other]).astype(bf16)
    out_grad = mm_tn(sl[...], dml[...])
    for i in range(2):
        g_own[1024 + 256 * i : 1280 + 256 * i, :] = out_grad[:256, 256 * i : 256 * (i + 1)]
        g_oth[1024 + 256 * i : 1280 + 256 * i, :] = out_grad[256:, 256 * i : 256 * (i + 1)].astype(bf16)


def turn_kernel(peers, steps, info, got, comp_in, dk, own, oth, keep, proj, x, nrm, wout_own, wout_oth,
                lin_own, lin_oth, gate_own, gate_oth, perm, cot_own, cot_oth,
                hx, bo_own, bo_oth, d_out, g_own, g_oth, skip_row, dmix, dst, comp, summ,
                packed, sl, gp, act, sig, qv, y, dl, dg, dml):
    core = info[1]
    states_of(peers, steps, 16, 1, True, info, got, comp_in, dk, own, oth, keep, proj, hx, sl, packed)
    mix_and_gate(core, x, nrm, sl, wout_own, wout_oth, lin_own, lin_oth, gate_own, gate_oth, gp, act, sig, qv, y)
    low = y[...].astype(bf16)
    natural = mm_tn(perm[...], low)
    y[...] = natural
    bo_own[...] = y[:, own_cols(core, 256)].astype(bf16)
    bo_oth[...] = y[:, oth_cols(core, 256)].astype(bf16)
    d_out[:, own_cols(core, 256)] = mm(perm[...], cot_own[...])
    d_out[:, oth_cols(core, 256)] = mm(perm[...], cot_oth[...])
    glu_backward(steps, 16, 0, False, core, d_out[...], nrm, x, sl, gp, act, sig, qv, own, oth, keep, wout_own, wout_oth,
                 lin_own, lin_oth, gate_own, gate_oth, g_own, g_oth, skip_row, dmix, dst, comp, summ, packed, dl, dg, dml)


def adjoint_part(peers, steps, base, keep_which, adj_which, adj_reverse, info, got, comp, dk, own, oth, keep, proj, x, nrm, nl,
                 hx, dst, dmix, win_own, win_oth, skip_row, g_own, g_oth, small_own, small_oth, at, packed, dp):
    core = info[1]
    device_carry(info[0], peers, got, dk, adj_which, own, oth, base, True, adj_reverse, packed)
    start = entries(comp, packed)
    lams, sc = decay(own, oth, base, 6, conj=True), scales(own, oth, base)
    zero = jnp.zeros((CHUNKS, 128), f32)
    acc = {half: [zero, zero, zero] for half in range(2)}
    shift = 0 if adj_reverse else 1

    def drive(s, row, half):
        return dst[part(s, row), cols(half, 0)], dst[part(s, row), cols(half, 1)]

    def visit(s, state, _):
        for half in range(2):
            for row in range(2):
                ar, ai = state[half, row]
                pr, pi = hx[part(s + shift, row), cols(half, 0)], hx[part(s + shift, row), cols(half, 1)]
                keep_here = keep[keep_which, part(s, row), :]
                acc[half][0] = acc[half][0] + keep_here * (ar * pr + ai * pi)
                acc[half][1] = acc[half][1] + keep_here * (ai * pr - ar * pi)
                acc[half][2] = acc[half][2] + (ar * proj[part(s, row), cols(half, 0)] + ai * proj[part(s, row), cols(half, 1)])
            for im in range(2):
                both = jnp.concatenate([sc[half] * state[half, row][im] for row in range(2)], axis=0)
                dp[s * SLAB : (s + 1) * SLAB, cols(half, im)] = both.astype(bf16)

    scan(drive, lams, keep, adj_which, steps, adj_reverse, start, visit)

    d_normed = dmix[...] * nrm[4:5, :] + mm_nt(dp[:, :256], win_own[...]) + mm_nt(dp[:, 256:], win_oth[...])
    xhat, _ = normalized(x[...].astype(f32), nrm)
    bias_row = jnp.sum(d_normed, axis=0, keepdims=True)
    gain_row = jnp.sum(d_normed * xhat, axis=0, keepdims=True)
    pack_two(bias_row, gain_row, packed)

    for ref, half, flip in ((small_own, 0, 0), (small_oth, 1, 1)):
        ref[at : at + 16, :] = jnp.zeros((16, 128), f32)
        for j, row in enumerate((skip_row[0:1, :], bias_row, gain_row)):
            low = (core == 0) if flip == 0 else (core == 1)
            pick = jnp.where(low, row[:, :256], row[:, 256:])
            ref[at + 2 * j : at + 2 * j + 1, :] = pick[:, :128]
            ref[at + 2 * j + 1 : at + 2 * j + 2, :] = pick[:, 128:]
        for j in range(3):
            ref[at + 6 + j : at + 7 + j, :] = jnp.sum(acc[half][j], axis=0, keepdims=True)

    g_own[...] = mm_tn(nl[...], dp[:, :256])
    g_oth[...] = mm_tn(nl[...], dp[:, 256:]).astype(bf16)
    return d_normed


def adjoint_second_kernel(peers, steps, info, got, comp, dk, own, oth, keep, proj, x, nrm, nl, hx, dst, dmix, win_own, win_oth, skip_row,
                          g_own, g_oth, small_own, small_oth, dn, stats, packed, dp):
    dn[...] = adjoint_part(peers, steps, 16, 1, 0, False, info, got, comp, dk, own, oth, keep, proj, x, nrm, nl,
                           hx, dst, dmix, win_own, win_oth, skip_row, g_own, g_oth, small_own, small_oth, 0, packed, dp)
    spread(stats, packed)


def back_first_kernel(steps, count, info, got, dn, x2, nrm2, d_out2, own, oth, keep, x, nrm, sl, gp, act, sig, qv,
                      wout_own, wout_oth, lin_own, lin_oth, gate_own, gate_oth,
                      d_out, g_own, g_oth, skip_row, dmix, dst, comp, summ, packed, dl, dg, dml):
    sums = sum_peers(got)
    bias_row, gain_row = row_of_tiles(sums[0:4]), row_of_tiles(sums[4:8])
    xhat, _ = normalized(x2[...], nrm2)
    gain = nrm2[2:3, :]
    d_in = d_out2[...] + nrm2[1:2, :] * (dn[...] * gain - gain * bias_row / count - xhat * (gain * gain_row / count))
    d_out[...] = d_in
    glu_backward(steps, 0, 1, True, info[1], d_in, nrm, x, sl, gp, act, sig, qv, own, oth, keep, wout_own, wout_oth,
                 lin_own, lin_oth, gate_own, gate_oth, g_own, g_oth, skip_row, dmix, dst, comp, summ, packed, dl, dg, dml)


def adjoint_first_kernel(peers, steps, info, got, comp, dk, own, oth, keep, proj, x, nrm, nl, hx, dst, dmix, win_own, win_oth, skip_row,
                         d_out, perm, small1_own, small1_oth,
                         g_own, g_oth, small_own, small_oth, a_own, a_oth, packed, dp, tmp):
    core = info[1]
    d_normed = adjoint_part(peers, steps, 0, 0, 1, True, info, got, comp, dk, own, oth, keep, proj, x, nrm, nl,
                            hx, dst, dmix, win_own, win_oth, skip_row, g_own, g_oth, small_own, small_oth, 0, packed, dp)
    small_own[16:32, :] = small1_own[...]
    small_oth[16:32, :] = small1_oth[...]
    partial = d_out[...] + nrm[1:2, :] * nrm[2:3, :] * d_normed
    tmp[...] = mm_tn(perm[...], partial.astype(bf16))
    a_own[...] = tmp[:, own_cols(core, 256)].astype(bf16)
    a_oth[...] = tmp[:, oth_cols(core, 256)].astype(bf16)


def finish_kernel(count, info, got, a_mine, a_other, tokens, nrm, rate_log, angle_log,
                  d_in, ngg, bias, skip, rate_grad, angle_grad, packed, held):
    core = info[1]
    packed[...] = sum_peers(got)
    for k in range(2):
        at = 16 * k
        for ref, j in ((skip, 0), (bias, 2), (ngg, 4)):
            ref[k : k + 1, :128] = packed[at + j : at + j + 1, :]
            ref[k : k + 1, 128:] = packed[at + j + 1 : at + j + 2, :]
        rate = jnp.exp(rate_log[...].astype(f32)[k : k + 1, :])
        angle = jnp.exp(angle_log[...].astype(f32)[k : k + 1, :])
        modulus = jnp.exp(-rate)
        scale = jnp.sqrt(1.0 - modulus * modulus)
        cos, sin = jnp.cos(angle), jnp.sin(angle)
        dr, di, ds = (packed[at + j : at + j + 1, :] for j in (6, 7, 8))
        g_mod = dr * cos + di * sin - ds * modulus / scale
        rate_grad[k : k + 1, :] = -g_mod * modulus * rate
        angle_grad[k : k + 1, :] = modulus * (di * cos - dr * sin) * angle
    mine = nrm[:, own_cols(core, 256)]
    mean, inv, gain = mine[0:1, :], mine[1:2, :], mine[2:3, :]
    bias_row, gain_row = bias[0:1, :], ngg[0:1, :]
    flat = inv * gain / count
    for r in range(4):
        held_rows = jnp.where(core == r // 2, a_mine[r % 2].astype(f32), a_other[r % 2].astype(f32))
        xhat = (tokens[r].astype(f32) - mean) * inv
        d_in[r] = held_rows - flat * (bias_row + xhat * gain_row)


def swap(value):
    return lax.ppermute(value, "state", [(0, 1), (1, 0)])


def to_all(value):
    axes = ("seq", "state") if value.shape[0] != lax.axis_size("seq") else "seq"
    return lax.all_to_all(value, axes, 0, 0)


def partner(value, mask):
    size = lax.axis_size("seq")
    return lax.ppermute(value, "seq", [(i, i ^ mask) for i in range(size)])


def halves_down(value, masks):
    me = lax.axis_index("seq")
    for m in masks:
        half = value.shape[0] // 2
        bit = (me // m) % 2
        mine = lax.dynamic_slice_in_dim(value, bit * half, half, 0)
        other = lax.dynamic_slice_in_dim(value, (1 - bit) * half, half, 0)
        value = (mine.astype(f32) + partner(other, m).astype(f32)).astype(bf16)
    return value


def halves_up(value, masks):
    me = lax.axis_index("seq")
    for m in reversed(masks):
        bit = (me // m) % 2
        got = partner(value, m)
        value = jnp.concatenate([jnp.where(bit == 0, value, got), jnp.where(bit == 0, got, value)], axis=0)
    return value


def sum_over_seq(value):
    masks = []
    m = 1
    while m < lax.axis_size("seq"):
        masks.append(m)
        m *= 2
    turned = masks[len(masks) // 2 :] + masks[: len(masks) // 2]
    half = value.shape[0] // 2
    parts = [halves_up(halves_down(v, ms), ms) for v, ms in ((value[:half], masks), (value[half:], turned))]
    return jnp.concatenate(parts, axis=0)


def run(kernel, outs, args, scratch=(), n_smem=1):
    return pl.pallas_call(
        kernel,
        out_shape=[jax.ShapeDtypeStruct(s, d) for s, d in outs],
        in_specs=[pl.BlockSpec(memory_space=pltpu.SMEM)] * n_smem + [pl.BlockSpec(memory_space=pltpu.VMEM)] * (len(args) - n_smem),
        out_specs=[pl.BlockSpec(memory_space=pltpu.VMEM)] * len(outs),
        scratch_shapes=[pltpu.VMEM(s, d) for s, d in scratch],
        compiler_params=pltpu.CompilerParams(vmem_limit_bytes=48 * 2**20),
    )(*args)


def body(tokens, gain, bias, in_proj, out_proj, rate_log, angle_log, skip, glu_lin, glu_gate, positions, cotangent):
    peers = lax.axis_size("seq")
    seq, core = lax.axis_index("seq"), lax.axis_index("state")
    rows, span, width = tokens.shape
    steps = span // CHUNKS
    n = 2 * span
    count = float(rows * span * peers)
    info = jnp.stack([seq, core]).astype(jnp.int32)
    packed = ((8, 128), f32)

    def cut(value):
        value = value.reshape(2, 2 * span, width)
        return (lax.dynamic_index_in_dim(value, core, 0, False), swap(lax.dynamic_index_in_dim(value, 1 - core, 0, False)))

    x_own, x_oth = cut(tokens)
    cot_own, cot_oth = cut(cotangent)
    w_in = in_proj.reshape(2, 512, 256)
    w_out = out_proj.reshape(2, 256, 512)
    in_oth, out_oth, lin_oth, gate_oth = (swap(w) for w in (w_in, w_out, glu_lin, glu_gate))

    stats, own, keep, dk, perm = run(
        functools.partial(prep_kernel, peers, steps),
        [((2 * peers, 4, 128), f32), ((32, 128), f32), ((2, n, 128), f32), ((2, peers, 8, 128), f32), ((n, n), bf16)],
        (info, positions, tokens, gain, bias, skip, rate_log, angle_log), n_smem=2)
    oth = swap(own)

    scan_outs = [((n, 512), bf16), ((n, 512), f32), ((16, 8, 128), f32), ((peers, 8, 128), f32), ((8, 512), f32)]
    xp, nl0, proj0, comp, summ, nrm0 = run(
        functools.partial(enter_first_kernel, peers, steps, count), [((n, 512), bf16)] + scan_outs,
        (info, to_all(stats), x_own, x_oth, perm, own, oth, keep, w_in[0], in_oth[0]), [packed])
    hx0, sl0, gp0, act0, sig0, qv0, y0, stats = run(
        functools.partial(leave_first_kernel, peers, steps),
        [((n + SLAB, 512), f32), ((n, 512), bf16), ((n, 512), f32), ((n, 512), bf16), ((n, 512), f32), ((n, 512), f32), ((n, 512), f32),
         ((2 * peers, 8, 128), f32)],
        (info, to_all(summ), comp, dk, own, oth, keep, proj0, xp, nrm0, w_out[0], out_oth[0], glu_lin[0], lin_oth[0], glu_gate[0], gate_oth[0]),
        [packed])
    nl1, proj1, comp, summ, nrm1 = run(
        functools.partial(enter_second_kernel, peers, steps, count), scan_outs,
        (info, to_all(stats), y0, own, oth, keep, w_in[1], in_oth[1]), [packed])
    grad_outs = [((1536, 256), f32), ((1536, 256), bf16), ((8, 512), f32), ((n, 512), f32), ((n, 512), f32), ((16, 8, 128), f32),
                 ((peers, 8, 128), f32)]
    low = ((n, 512), bf16)
    full = ((n, 512), f32)
    hx1, bo_own, bo_oth, d_out1, g1_own, g1_oth, skip1, dmix, dst, comp, summ = run(
        functools.partial(turn_kernel, peers, steps),
        [((n + SLAB, 512), f32), ((n, 256), bf16), ((n, 256), bf16), full] + grad_outs,
        (info, to_all(summ), comp, dk, own, oth, keep, proj1, y0, nrm1, w_out[1], out_oth[1], glu_lin[1], lin_oth[1], glu_gate[1], gate_oth[1],
         perm, cot_own, cot_oth),
        [packed, low, full, low, full, full, full, low, low, low])
    bo_got = swap(bo_oth)
    adj_outs = [((512, 256), f32), ((512, 256), bf16)]
    i1_own, i1_oth, s1_own, s1_oth, dn, stats = run(
        functools.partial(adjoint_second_kernel, peers, steps),
        adj_outs + [((16, 128), f32), ((16, 128), f32), full, ((2 * peers, 8, 128), f32)],
        (info, to_all(summ), comp, dk, own, oth, keep, proj1, y0, nrm1, nl1, hx1, dst, dmix, w_in[1], in_oth[1], skip1),
        [packed, low])
    d_out0, g0_own, g0_oth, skip0, dmix, dst, comp, summ = run(
        functools.partial(back_first_kernel, steps, count),
        [full] + grad_outs,
        (info, to_all(stats), dn, y0, nrm1, d_out1, own, oth, keep, xp, nrm0, sl0, gp0, act0, sig0, qv0,
         w_out[0], out_oth[0], glu_lin[0], lin_oth[0], glu_gate[0], gate_oth[0]),
        [packed, low, low, low])
    i0_own, i0_oth, s_own, s_oth, a_own, a_oth = run(
        functools.partial(adjoint_first_kernel, peers, steps),
        adj_outs + [((32, 128), f32), ((32, 128), f32), ((n, 256), bf16), ((n, 256), bf16)],
        (info, to_all(summ), comp, dk, own, oth, keep, proj0, xp, nrm0, nl0, hx0, dst, dmix, w_in[0], in_oth[0], skip0,
         d_out0, perm, s1_own, s1_oth),
        [packed, low, full])
    a_got = swap(a_oth)
    s_all = s_own + swap(s_oth)
    got = to_all(jnp.broadcast_to(s_all[None], (peers, 32, 128)))
    pair = (2, span, width)
    d_in, ngg, bias_grad, skip_grad, rate_grad, angle_grad = run(
        functools.partial(finish_kernel, count),
        [((rows, span, width), f32), ((2, 256), f32), ((2, 256), f32), ((2, 256), f32), ((2, 128), f32), ((2, 128), f32)],
        (info, got, a_own.reshape(pair), a_got.reshape(pair), tokens, nrm0, rate_log, angle_log),
        [((32, 128), f32), ((8, 256), f32)])

    def weight_sum(g_own, g_oth, i_own, i_oth):
        mine = jnp.concatenate([g_own, i_own], axis=0)
        return sum_over_seq((mine + swap(jnp.concatenate([g_oth, i_oth], axis=0)).astype(f32)).astype(bf16))

    total1 = weight_sum(g1_own, g1_oth, i1_own, i1_oth).astype(f32)
    total0 = weight_sum(g0_own, g0_oth, i0_own, i0_oth).astype(f32)
    both = jnp.stack([total0, total1])
    lin_grad, gate_grad = both[:, :512], both[:, 512:1024]
    out_grad = jnp.concatenate([both[:, 1024:1280], both[:, 1280:1536]], axis=2).reshape(2, 2, 128, 512)
    in_grad = both[:, 1536:].reshape(2, 512, 2, 128)
    mine, other = bo_own.reshape(pair), bo_got.reshape(pair)
    block_out = jnp.concatenate([jnp.where(core == 0, mine, other), jnp.where(core == 0, other, mine)], axis=0)
    return (block_out, d_in, ngg, bias_grad, in_grad, out_grad, rate_grad, angle_grad, skip_grad, lin_grad, gate_grad)


def solution(mesh):
    placed = (
        P(None, "seq", "state"),
        P(None, "state"),
        P(None, "state"),
        P(None, None, None, "state"),
        P(None, None, "state", None),
        P(None, "state"),
        P(None, "state"),
        P(None, "state"),
        P(None, None, "state"),
        P(None, None, "state"),
        P(),
        P(None, "seq", "state"),
    )
    return jax.shard_map(
        body,
        mesh=mesh,
        in_specs=placed,
        out_specs=(
            P(None, "seq", "state"),
            P(None, "seq", "state"),
            P(None, "state"),
            P(None, "state"),
            P(None, None, None, "state"),
            P(None, None, "state", None),
            P(None, "state"),
            P(None, "state"),
            P(None, "state"),
            P(None, None, "state"),
            P(None, None, "state"),
        ),
        check_vma=False,
    )
```

```python
import functools

import jax
import jax.numpy as jnp
from jax import lax
from jax.experimental import pallas as pl
from jax.experimental.pallas import tpu as pltpu
from jax.sharding import PartitionSpec as P

f32, bf16 = jnp.float32, jnp.bfloat16
norm_eps = 1e-05
CHUNKS = 8
SLAB = 2 * CHUNKS


def mm(a, b):
    return jnp.dot(a, b, preferred_element_type=f32)


def mm_nt(a, b):
    return lax.dot_general(a, b, (((1,), (1,)), ((), ())), preferred_element_type=f32)


def mm_tn(a, b):
    return lax.dot_general(a, b, (((0,), (0,)), ((), ())), preferred_element_type=f32)


def wide(row):
    return jnp.broadcast_to(row, (CHUNKS, 128))


def cmul(ar, ai, br, bi):
    return ar * br - ai * bi, ar * bi + ai * br


def row_of_tiles(tiles):
    return jnp.concatenate([tiles[i : i + 1, :] for i in range(tiles.shape[0])], axis=1)


def channel_row(core, own, oth, at):
    mine, other = own[at : at + 2, :], oth[at : at + 2, :]
    low = jnp.where(core == 0, mine, other)
    high = jnp.where(core == 0, other, mine)
    return jnp.concatenate([low[0:1], low[1:2], high[0:1], high[1:2]], axis=1)


def own_cols(core, width):
    return pl.ds(pl.multiple_of(core * width, width), width)


def oth_cols(core, width):
    return pl.ds(pl.multiple_of((1 - core) * width, width), width)


def scan(drive, lams, keep_ref, which, steps, reverse, start, visit):
    order = range(steps - 1, -1, -1) if reverse else range(steps)
    state = dict(start)
    for s in order:
        for row in range(2):
            at = s * SLAB + row * CHUNKS
            keep = keep_ref[which, at : at + CHUNKS, :]
            for half in range(2):
                lr, li = lams[half]
                hr, hi = state[half, row]
                hr, hi = keep * hr, keep * hi
                dr, di = drive(s, row, half)
                state[half, row] = (lr * hr - li * hi + dr, lr * hi + li * hr + di)
        visit(s, state, keep_ref)
    return state


def keep_products(keep_ref, which, steps):
    out = []
    for row in range(2):
        total = keep_ref[which, row * CHUNKS : (row + 1) * CHUNKS, :]
        for s in range(1, steps):
            at = s * SLAB + row * CHUNKS
            total = total * keep_ref[which, at : at + CHUNKS, :]
        out.append(total)
    return out


def chunk_scan(ends, keeps, powers, reverse, comp_ref, packed):
    index = lax.broadcasted_iota(jnp.int32, (CHUNKS, 128), 0)

    def shifted(value, by, fill):
        turned = pltpu.roll(value, CHUNKS - by if reverse else by, 0)
        valid = index < CHUNKS - by if reverse else index >= by
        return jnp.where(valid, turned, fill)

    for half in range(2):
        for row in range(2):
            er, ei = ends[half, row]
            pr, pi = powers[half][0] * keeps[row], powers[half][1] * keeps[row]
            for by in (1, 2, 4):
                tr, ti = cmul(pr, pi, shifted(er, by, 0.0), shifted(ei, by, 0.0))
                er, ei = er + tr, ei + ti
                pr, pi = cmul(pr, pi, shifted(pr, by, 1.0), shifted(pi, by, 0.0))
            edge = 0 if reverse else CHUNKS - 1
            q = row * 2 + half
            packed[q : q + 1, :] = er[edge : edge + 1, :]
            packed[4 + q : 5 + q, :] = ei[edge : edge + 1, :]
            base = (half * 2 + row) * 4
            comp_ref[base] = shifted(er, 1, 0.0)
            comp_ref[base + 1] = shifted(ei, 1, 0.0)
            comp_ref[base + 2] = shifted(pr, 1, 1.0)
            comp_ref[base + 3] = shifted(pi, 1, 0.0)


def device_carry(me, peers, got, held, dk_ref, which, own, oth, base, conj, reverse, packed):
    got_ref = arrange(got, held)
    index = lax.broadcasted_iota(jnp.int32, (CHUNKS, 128), 0)
    is_own = index % 2 == 0
    sign = jnp.where(index < 4, -1.0, 1.0) * (-1.0 if conj else 1.0)
    ar = jnp.where(is_own, wide(own[base + 11 : base + 12, :]), wide(oth[base + 11 : base + 12, :]))
    ai = jnp.where(is_own, wide(own[base + 12 : base + 13, :]), wide(oth[base + 12 : base + 13, :]))
    ai = ai * sign

    def step(k, held):
        at = peers - 1 - k if reverse else k
        reached = at > me if reverse else at < me
        new = dk_ref[which, at] * (ar * held + ai * pltpu.roll(held, 4, 0)) + got_ref[at]
        return jnp.where(reached, new, held)

    packed[...] = lax.fori_loop(0, peers, step, jnp.zeros((8, 128), f32), unroll=peers <= 16)


def entries(comp_ref, packed):
    start = {}
    for half in range(2):
        for row in range(2):
            base, q = (half * 2 + row) * 4, row * 2 + half
            hr, hi = wide(packed[q : q + 1, :]), wide(packed[4 + q : 5 + q, :])
            tr, ti = cmul(comp_ref[base + 2], comp_ref[base + 3], hr, hi)
            start[half, row] = (comp_ref[base] + tr, comp_ref[base + 1] + ti)
    return start


def decay(own, oth, base, at, conj=False):
    sign = -1.0 if conj else 1.0
    return [(wide(r[base + at : base + at + 1, :]), sign * wide(r[base + at + 1 : base + at + 2, :])) for r in (own, oth)]


def scales(own, oth, base):
    return [wide(r[base + 8 : base + 9, :]) for r in (own, oth)]


def nothing(*_):
    return None


def zeros_start():
    zero = jnp.zeros((CHUNKS, 128), f32)
    return {(half, row): (zero, zero) for half in range(2) for row in range(2)}


def part(s, row):
    at = s * SLAB + row * CHUNKS
    return slice(at, at + CHUNKS)


def cols(half, im):
    at = half * 256 + im * 128
    return slice(at, at + 128)


def flat_rows(ref):
    value = ref[...]
    return value.reshape(value.shape[0] * value.shape[1], value.shape[2])


def spread(out_ref, packed):
    value = packed[...]
    out_ref[...] = value if len(out_ref.shape) == 2 else jnp.broadcast_to(value[None], out_ref.shape)


def arrange(got, held):
    if len(got) == 1:
        return got[0]
    me = place()[0]
    for m, block in enumerate(got):
        for e in range(4):
            held[(((me >> 2) ^ m) << 2) + ((me & 3) ^ e)] = block[e]
    return held


def place():
    return lax.axis_index("seq"), lax.axis_index("state")


def prep_kernel(peers, steps, pos, tokens, gain, bias, skip, rate_log, angle_log, stats, small, keep, dk, perm):
    seq, core = place()
    rows, span, _ = tokens.shape
    docs = pos.shape[1]

    count = perm.shape[0]
    p = lax.broadcasted_iota(jnp.int32, (count, count), 0)
    q = lax.broadcasted_iota(jnp.int32, (count, count), 1)
    source = ((p >> 3) & 1) * span + (p & 7) * steps + (p >> 4)
    perm[...] = jnp.where(q == source, 1.0, 0.0).astype(bf16)
    s1 = s2 = 0.0
    for r in range(rows):
        x = tokens[r].astype(f32)
        s1 = s1 + jnp.sum(x, axis=0, keepdims=True)
        s2 = s2 + jnp.sum(x * x, axis=0, keepdims=True)
    for i in range(2):
        stats[0, i : i + 1, :] = s1[:, 128 * i : 128 * (i + 1)]
        stats[0, 2 + i : 3 + i, :] = s2[:, 128 * i : 128 * (i + 1)]
    stats[...] = jnp.broadcast_to(stats[0][None], stats.shape)

    small[...] = jnp.zeros_like(small)
    for k in range(2):
        at = 16 * k
        for j, ref in enumerate((gain, bias, skip)):
            v = ref[...].astype(f32)
            small[at + 2 * j : at + 2 * j + 1, :] = v[k : k + 1, :128]
            small[at + 2 * j + 1 : at + 2 * j + 2, :] = v[k : k + 1, 128:]
        rate = jnp.exp(rate_log[...].astype(f32)[k : k + 1, :])
        angle = jnp.exp(angle_log[...].astype(f32)[k : k + 1, :])
        modulus = jnp.exp(-rate)
        lr, li = modulus * jnp.cos(angle), modulus * jnp.sin(angle)
        small[at + 6 : at + 7, :] = lr
        small[at + 7 : at + 8, :] = li
        small[at + 8 : at + 9, :] = jnp.sqrt(1.0 - modulus * modulus)
        power = 1
        while power < span:
            lr, li = cmul(lr, li, lr, li)
            power *= 2
            if power == steps:
                small[at + 9 : at + 10, :] = lr
                small[at + 10 : at + 11, :] = li
        small[at + 11 : at + 12, :] = lr
        small[at + 12 : at + 13, :] = li

    chunk = lax.broadcasted_iota(jnp.int32, (CHUNKS, 128), 0) * steps + seq * span
    for row in range(2):
        targets = [pos[core * 2 + row, d] - chunk for d in range(docs)]
        for s in range(steps + 1):
            hit = targets[0] == s
            for t in targets[1:]:
                hit = jnp.logical_or(hit, t == s)
            value = jnp.where(hit, 0.0, 1.0)
            at = s * SLAB + row * CHUNKS
            if s < steps:
                keep[0, at : at + CHUNKS, :] = value
            if s >= 1:
                keep[1, at - SLAB : at - SLAB + CHUNKS, :] = value

    first_row = (lax.broadcasted_iota(jnp.int32, (CHUNKS, 128), 0) // 2) % 2 == 0
    owners = ([], [])
    for d in range(docs):
        a, b = pos[core * 2, d], pos[core * 2 + 1, d]
        owners[0].append(jnp.where(first_row, a // span, b // span))
        owners[1].append(jnp.where(first_row, (a + span - 1) // span - 1, (b + span - 1) // span - 1))

    def mark(j, _):
        for m in range(2):
            hit = owners[m][0] == j
            for o in owners[m][1:]:
                hit = jnp.logical_or(hit, o == j)
            dk[m, j] = jnp.where(hit, 0.0, 1.0)
        return 0

    lax.fori_loop(0, peers, mark, 0)


def norm_rows(total, squares, count, core, own, oth, base, nrm):
    mean = total / count
    inv = lax.rsqrt(squares / count - mean * mean + norm_eps)
    nrm[0:1, :] = mean
    nrm[1:2, :] = inv
    nrm[2:3, :] = channel_row(core, own, oth, base)
    nrm[3:4, :] = channel_row(core, own, oth, base + 2)
    nrm[4:5, :] = channel_row(core, own, oth, base + 4)
    nrm[5:8, :] = jnp.zeros_like(nrm[5:8, :])


def normalized(x, nrm):
    xhat = (x - nrm[0:1, :]) * nrm[1:2, :]
    return xhat, xhat * nrm[2:3, :] + nrm[3:4, :]


def project_and_scan(steps, base, which, reverse, own, oth, keep, win_own, win_oth, nl, proj, comp, summ, packed):
    proj[:, :256] = mm(nl[...], win_own[...])
    proj[:, 256:] = mm(nl[...], win_oth[...])
    lams, sc = decay(own, oth, base, 6), scales(own, oth, base)

    def drive(s, row, half):
        return sc[half] * proj[part(s, row), cols(half, 0)], sc[half] * proj[part(s, row), cols(half, 1)]

    ends = scan(drive, lams, keep, which, steps, reverse, zeros_start(), nothing)
    chunk_scan(ends, keep_products(keep, which, steps), decay(own, oth, base, 9), reverse, comp, packed)
    spread(summ, packed)


def enter_first_kernel(peers, steps, count, got, x_own, x_oth, perm, own, oth, keep, win_own, win_oth,
                       xp, nl, proj, comp, summ, nrm, packed):
    _, core = place()
    sums = got[0:2]
    for j in range(1, peers):
        sums = sums + got[2 * j : 2 * j + 2]
    total = jnp.concatenate([sums[0, 0:1], sums[0, 1:2], sums[1, 0:1], sums[1, 1:2]], axis=1)
    squares = jnp.concatenate([sums[0, 2:3], sums[0, 3:4], sums[1, 2:3], sums[1, 3:4]], axis=1)
    norm_rows(total, squares, count, core, own, oth, 0, nrm)
    xp[:, own_cols(core, 256)] = mm(perm[...], flat_rows(x_own)).astype(bf16)
    xp[:, oth_cols(core, 256)] = mm(perm[...], flat_rows(x_oth)).astype(bf16)
    _, normed = normalized(xp[...].astype(f32), nrm)
    xp.send()
    nl[...] = normed.astype(bf16)
    nl.send()
    project_and_scan(steps, 0, 0, False, own, oth, keep, win_own, win_oth, nl, proj, comp, summ, packed)


def sum_peers(got):
    if len(got) == 1 and len(got[0].shape) == 3:
        got = [got[0].at[j] for j in range(got[0].shape[0])]
    total = got[0][...]
    for part in got[1:]:
        total = total + part[...]
    return total


def enter_second_kernel(peers, steps, count, got, x, own, oth, keep, win_own, win_oth,
                        nl, proj, comp, summ, nrm, packed):
    _, core = place()
    sums = sum_peers(got)
    norm_rows(row_of_tiles(sums[0:4]), row_of_tiles(sums[4:8]), count, core, own, oth, 16, nrm)
    _, normed = normalized(x[...], nrm)
    nl[...] = normed.astype(bf16)
    project_and_scan(steps, 16, 1, True, own, oth, keep, win_own, win_oth, nl, proj, comp, summ, packed)


def states_of(peers, steps, base, which, reverse, got, comp, dk, own, oth, keep, proj, cin, sl, packed, held):
    device_carry(place()[0], peers, got, held, dk, which, own, oth, base, False, reverse, packed)
    start = entries(comp, packed)
    lams, sc = decay(own, oth, base, 6), scales(own, oth, base)
    for (half, row), (hr, hi) in start.items():
        cin[part(0, row), cols(half, 0)] = hr
        cin[part(0, row), cols(half, 1)] = hi

    def drive(s, row, half):
        return sc[half] * proj[part(s, row), cols(half, 0)], sc[half] * proj[part(s, row), cols(half, 1)]

    def visit(s, state, _):
        for half in range(2):
            for im in range(2):
                both = jnp.concatenate([state[half, row][im] for row in range(2)], axis=0)
                sl[s * SLAB : (s + 1) * SLAB, cols(half, im)] = both.astype(bf16)

    scan(drive, lams, keep, which, steps, reverse, start, visit)
    send(sl)


def send(ref):
    if isinstance(ref, Drained):
        ref.send()


def mix_and_gate(core, x, nrm, sl, wout_own, wout_oth, lin_own, lin_oth, gate_own, gate_oth, gp, act, sig, qv, y):
    _, normed = normalized(x[...].astype(f32), nrm)
    mixed = mm(sl[:, :256], wout_own[...]) + mm(sl[:, 256:], wout_oth[...]) + nrm[4:5, :] * normed
    c = 0.7978845608028654
    sq = mixed * mixed
    t = jnp.tanh(c * (mixed + 0.044715 * sq * mixed))
    act[...] = (0.5 * mixed * (1.0 + t)).astype(bf16)
    send(act)
    gp[...] = (0.5 * (1.0 + t) + 0.5 * mixed * (1.0 - t * t) * (c * (1.0 + 3 * 0.044715 * sq))).astype(gp.dtype)
    send(gp)
    for w_lin, w_gate, at in ((lin_own, gate_own, own_cols(core, 256)), (lin_oth, gate_oth, oth_cols(core, 256))):
        linear = mm(act[...], w_lin[...])
        gating = mm(act[...], w_gate[...])
        sg = 0.5 + 0.5 * jnp.tanh(0.5 * gating)
        out = linear * sg
        sig[:, at] = sg.astype(sig.dtype)
        qv[:, at] = (out * (1.0 - sg)).astype(qv.dtype)
        y[:, at] = x[:, at].astype(f32) + out
    send(sig)
    send(qv)


def leave_first_kernel(peers, steps, got, comp, dk, own, oth, keep, proj, x, nrm, wout_own, wout_oth,
                       lin_own, lin_oth, gate_own, gate_oth, cin, sl, gp, act, sig, qv, y, stats, packed, held):
    states_of(peers, steps, 0, 0, False, got, comp, dk, own, oth, keep, proj, cin, sl, packed, held)
    mix_and_gate(place()[1], x, nrm, sl, wout_own, wout_oth, lin_own, lin_oth, gate_own, gate_oth, gp, act, sig, qv, y)
    out = y[...]
    pack_two(jnp.sum(out, axis=0, keepdims=True), jnp.sum(out * out, axis=0, keepdims=True), packed)
    spread(stats, packed)


def pack_two(a, b, packed):
    for i in range(4):
        packed[i : i + 1, :] = a[:, 128 * i : 128 * (i + 1)]
        packed[4 + i : 5 + i, :] = b[:, 128 * i : 128 * (i + 1)]


def glu_backward(steps, base, adj_which, adj_reverse, core, d_out, nrm, x, gp, sig, qv, own, oth, keep, wout_own, wout_oth,
                 lin_own, lin_oth, gate_own, gate_oth, skip_row, dst, comp, summ, packed, dl, dg, dml):
    dl[...] = (d_out * sig[...].astype(f32)).astype(bf16)
    dg[...] = (d_out * qv[...].astype(f32)).astype(bf16)
    mine, other = own_cols(core, 256), oth_cols(core, 256)
    d_active = (mm_nt(dl[:, mine], lin_own[...]) + mm_nt(dg[:, mine], gate_own[...])
                + mm_nt(dl[:, other], lin_oth[...]) + mm_nt(dg[:, other], gate_oth[...]))
    d_mixed = d_active * gp[...].astype(f32)
    _, normed = normalized(x[...].astype(f32), nrm)
    skip_row[0:1, :] = jnp.sum(d_mixed * normed, axis=0, keepdims=True)
    dml[...] = d_mixed.astype(bf16)
    dst[:, :256] = mm_nt(dml[...], wout_own[...])
    dst[:, 256:] = mm_nt(dml[...], wout_oth[...])
    lams = decay(own, oth, base, 6, conj=True)

    def drive(s, row, half):
        return dst[part(s, row), cols(half, 0)], dst[part(s, row), cols(half, 1)]

    ends = scan(drive, lams, keep, adj_which, steps, adj_reverse, zeros_start(), nothing)
    chunk_scan(ends, keep_products(keep, adj_which, steps), decay(own, oth, base, 9, conj=True), adj_reverse, comp, packed)
    spread(summ, packed)


def mixer_grads(act, dl, dg, sl, dml, g_own, g_oth):
    _, core = place()
    mine, other = own_cols(core, 256), oth_cols(core, 256)
    g_own[0:512, :] = mm_tn(act[...], dl[:, mine])
    g_oth[0:512, :] = mm_tn(act[...], dl[:, other]).astype(bf16)
    g_own[512:1024, :] = mm_tn(act[...], dg[:, mine])
    g_oth[512:1024, :] = mm_tn(act[...], dg[:, other]).astype(bf16)
    out_grad = mm_tn(sl[...], dml[...])
    for i in range(2):
        g_own[1024 + 256 * i : 1280 + 256 * i, :] = out_grad[:256, 256 * i : 256 * (i + 1)]
        g_oth[1024 + 256 * i : 1280 + 256 * i, :] = out_grad[256:, 256 * i : 256 * (i + 1)].astype(bf16)


def in_grads(nl, dp, g_own, g_oth):
    g_own[...] = mm_tn(nl[...], dp[:, :256])
    g_oth[...] = mm_tn(nl[...], dp[:, 256:]).astype(bf16)


def turn_kernel(peers, steps, got, comp_in, dk, own, oth, keep, proj, x, nrm, wout_own, wout_oth,
                lin_own, lin_oth, gate_own, gate_oth, perm, cot_own, cot_oth,
                cin, bo_own, bo_oth, d_out, act, dl, dg, sl, dml, skip_row, dst, comp, summ,
                packed, held, gp, sig, qv, y):
    _, core = place()
    states_of(peers, steps, 16, 1, True, got, comp_in, dk, own, oth, keep, proj, cin, sl, packed, held)
    mix_and_gate(core, x, nrm, sl, wout_own, wout_oth, lin_own, lin_oth, gate_own, gate_oth, gp, act, sig, qv, y)
    low = y[...].astype(bf16)
    natural = mm_tn(perm[...], low)
    y[...] = natural
    bo_own[...] = y[:, own_cols(core, 256)].astype(bf16)
    bo_oth[...] = y[:, oth_cols(core, 256)].astype(bf16)
    send(bo_own)
    send(bo_oth)
    d_out[:, own_cols(core, 256)] = mm(perm[...], flat_rows(cot_own)).astype(bf16)
    d_out[:, oth_cols(core, 256)] = mm(perm[...], flat_rows(cot_oth)).astype(bf16)
    glu_backward(steps, 16, 0, False, core, d_out[...].astype(f32), nrm, x, gp, sig, qv, own, oth, keep, wout_own, wout_oth,
                 lin_own, lin_oth, gate_own, gate_oth, skip_row, dst, comp, summ, packed, dl, dg, dml)


def adjoint_part(peers, steps, base, keep_which, adj_which, adj_reverse, got, comp, dk, own, oth, keep, nl, x, nrm,
                 cin, sl, dst, dml, win_own, win_oth, skip_row, small_own, small_oth, at, packed, held, proj, dp):
    _, core = place()
    device_carry(place()[0], peers, got, held, dk, adj_which, own, oth, base, True, adj_reverse, packed)
    start = entries(comp, packed)
    lams, sc = decay(own, oth, base, 6, conj=True), scales(own, oth, base)
    zero = jnp.zeros((CHUNKS, 128), f32)
    acc = {half: [zero, zero, zero] for half in range(2)}
    proj[:, :256] = mm(nl[...], win_own[...])
    proj[:, 256:] = mm(nl[...], win_oth[...])

    def prior(s, half, im):
        before = s - 1 if adj_reverse else s + 1
        if 0 <= before < steps:
            return sl[before * SLAB : (before + 1) * SLAB, cols(half, im)].astype(f32)
        return cin[:, cols(half, im)]

    def drive(s, row, half):
        return dst[part(s, row), cols(half, 0)], dst[part(s, row), cols(half, 1)]

    def visit(s, state, _):
        for half in range(2):
            prior_re, prior_im = prior(s, half, 0), prior(s, half, 1)
            for row in range(2):
                ar, ai = state[half, row]
                pr, pi = prior_re[part(0, row)], prior_im[part(0, row)]
                keep_here = keep[keep_which, part(s, row), :]
                acc[half][0] = acc[half][0] + keep_here * (ar * pr + ai * pi)
                acc[half][1] = acc[half][1] + keep_here * (ai * pr - ar * pi)
                acc[half][2] = acc[half][2] + (ar * proj[part(s, row), cols(half, 0)] + ai * proj[part(s, row), cols(half, 1)])
            for im in range(2):
                both = jnp.concatenate([sc[half] * state[half, row][im] for row in range(2)], axis=0)
                dp[s * SLAB : (s + 1) * SLAB, cols(half, im)] = both.astype(bf16)

    scan(drive, lams, keep, adj_which, steps, adj_reverse, start, visit)

    d_normed = dml[...].astype(f32) * nrm[4:5, :] + mm_nt(dp[:, :256], win_own[...]) + mm_nt(dp[:, 256:], win_oth[...])
    xhat, _ = normalized(x[...].astype(f32), nrm)
    bias_row = jnp.sum(d_normed, axis=0, keepdims=True)
    gain_row = jnp.sum(d_normed * xhat, axis=0, keepdims=True)
    pack_two(bias_row, gain_row, packed)

    for ref, half, flip in ((small_own, 0, 0), (small_oth, 1, 1)):
        ref[at : at + 16, :] = jnp.zeros((16, 128), f32)
        for j, row in enumerate((skip_row[0:1, :], bias_row, gain_row)):
            low = (core == 0) if flip == 0 else (core == 1)
            pick = jnp.where(low, row[:, :256], row[:, 256:])
            ref[at + 2 * j : at + 2 * j + 1, :] = pick[:, :128]
            ref[at + 2 * j + 1 : at + 2 * j + 2, :] = pick[:, 128:]
        for j in range(3):
            ref[at + 6 + j : at + 7 + j, :] = jnp.sum(acc[half][j], axis=0, keepdims=True)
    return d_normed


def adjoint_second_kernel(peers, steps, got, comp, dk, own, oth, keep, nl, x, nrm, cin, sl, dst, dml, win_own, win_oth, skip_row, act, dl, dg,
                          g_own, g_oth, small_own, small_oth, dn, stats, packed, held, proj, dp):
    dn[...] = adjoint_part(peers, steps, 16, 1, 0, False, got, comp, dk, own, oth, keep, nl, x, nrm,
                           cin, sl, dst, dml, win_own, win_oth, skip_row, small_own, small_oth, 0, packed, held, proj, dp)
    spread(stats, packed)
    mixer_grads(act, dl, dg, sl, dml, g_own, g_oth)
    in_grads(nl, dp, g_own.at[1536:], g_oth.at[1536:])


def back_first_kernel(steps, count, got, dn, x2, nrm2, d_out2, own, oth, keep, x, nrm, gp, sig, qv,
                      wout_own, wout_oth, lin_own, lin_oth, gate_own, gate_oth,
                      act, sl, d_out, dml, g_own, g_oth, skip_row, dst, comp, summ, packed, dl, dg):
    sums = sum_peers(got)
    bias_row, gain_row = row_of_tiles(sums[0:4]), row_of_tiles(sums[4:8])
    xhat, _ = normalized(x2[...], nrm2)
    gain = nrm2[2:3, :]
    d_in = d_out2[...].astype(f32) + nrm2[1:2, :] * (dn[...] * gain - gain * bias_row / count - xhat * (gain * gain_row / count))
    d_out[...] = d_in
    glu_backward(steps, 0, 1, True, place()[1], d_in, nrm, x, gp, sig, qv, own, oth, keep, wout_own, wout_oth,
                 lin_own, lin_oth, gate_own, gate_oth, skip_row, dst, comp, summ, packed, dl, dg, dml)
    mixer_grads(act, dl, dg, sl, dml, g_own, g_oth)


def adjoint_first_kernel(peers, steps, got, comp, dk, own, oth, keep, nl, x, nrm, cin, sl, dst, dml, win_own, win_oth, skip_row,
                         d_out, perm, small1_own, small1_oth,
                         g_own, g_oth, small_own, small_oth, a_own, a_oth, packed, held, proj, tmp, dp):
    _, core = place()
    d_normed = adjoint_part(peers, steps, 0, 0, 1, True, got, comp, dk, own, oth, keep, nl, x, nrm,
                            cin, sl, dst, dml, win_own, win_oth, skip_row, small_own, small_oth, 0, packed, held, proj, dp)
    small_own[16:32, :] = small1_own[...]
    small_oth[16:32, :] = small1_oth[...]
    partial = d_out[...] + nrm[1:2, :] * nrm[2:3, :] * d_normed
    tmp[...] = mm_tn(perm[...], partial.astype(bf16))
    a_own[...] = tmp[:, own_cols(core, 256)].astype(bf16)
    a_oth[...] = tmp[:, oth_cols(core, 256)].astype(bf16)
    in_grads(nl, dp, g_own, g_oth)


def finish_kernel(count, got, a_mine, a_other, tokens, nrm, rate_log, angle_log,
                  d_in, ngg, bias, skip, rate_grad, angle_grad, packed):
    _, core = place()
    packed[...] = sum_peers(got)
    for k in range(2):
        at = 16 * k
        for ref, j in ((skip, 0), (bias, 2), (ngg, 4)):
            ref[k : k + 1, :128] = packed[at + j : at + j + 1, :]
            ref[k : k + 1, 128:] = packed[at + j + 1 : at + j + 2, :]
        rate = jnp.exp(rate_log[...].astype(f32)[k : k + 1, :])
        angle = jnp.exp(angle_log[...].astype(f32)[k : k + 1, :])
        modulus = jnp.exp(-rate)
        scale = jnp.sqrt(1.0 - modulus * modulus)
        cos, sin = jnp.cos(angle), jnp.sin(angle)
        dr, di, ds = (packed[at + j : at + j + 1, :] for j in (6, 7, 8))
        g_mod = dr * cos + di * sin - ds * modulus / scale
        rate_grad[k : k + 1, :] = -g_mod * modulus * rate
        angle_grad[k : k + 1, :] = modulus * (di * cos - dr * sin) * angle
    mine = nrm[:, own_cols(core, 256)]
    mean, inv, gain = mine[0:1, :], mine[1:2, :], mine[2:3, :]
    bias_row, gain_row = bias[0:1, :], ngg[0:1, :]
    flat = inv * gain / count
    for r in range(4):
        held_rows = jnp.where(core == r // 2, a_mine[r % 2].astype(f32), a_other[r % 2].astype(f32))
        xhat = (tokens[r].astype(f32) - mean) * inv
        d_in[r] = held_rows - flat * (bias_row + xhat * gain_row)


def swap(value):
    return lax.ppermute(value, "state", [(0, 1), (1, 0)])


def to_all(value, axes):
    peers = 1
    for a in axes:
        peers *= lax.axis_size(a)
    return lax.all_to_all(jnp.broadcast_to(value[None], (peers,) + value.shape), axes, 0, 0)


def blocking(value, axes, others):
    value, others = lax.optimization_barrier((value, others))
    got, others = lax.optimization_barrier((lax.all_to_all(value, axes, 0, 0), others))
    return (got,), others


def gather_seq(value):
    if lax.axis_size("seq") != 16:
        return (to_all(value, ("seq",)),)
    near = jnp.stack([value] + [partner(value, m) for m in (1, 2, 3)])
    return (near,) + tuple(partner(near, m) for m in (4, 8, 12))


def sum_all(value):
    if lax.axis_size("seq") != 16:
        return (to_all(value, ("seq", "state")),)
    value = value + swap(value)
    near = value + partner(value, 1) + partner(value, 2) + partner(value, 3)
    return (near,) + tuple(partner(near, m) for m in (4, 8, 12))


def partner(value, mask):
    size = lax.axis_size("seq")
    return lax.ppermute(value, "seq", [(i, i ^ mask) for i in range(size)])


def partners(value, masks):
    size = lax.axis_size("seq")
    return lax.ppermute(value, ("seq", "state"), [(2 * i + c, 2 * (i ^ masks[c]) + c) for i in range(size) for c in range(2)])


def tie(value, others):
    return lax.optimization_barrier((value, others))


def bit_of(masks):
    me, core = place()
    return (me // jnp.where(core == 0, masks[0], masks[1])) & 1


def first_halves_kernel(masks, pairs, mine, other):
    bit, at = bit_of(masks), 0
    for own, got in pairs:
        half = own.shape[0] // 2
        for out, which in ((mine, bit), (other, 1 - bit)):
            rows = pl.ds(pl.multiple_of(which * half, half), half)
            out[at : at + half, :] = (own[rows, :] + got[rows, :].astype(f32)).astype(bf16)
        at += half


def next_halves_kernel(masks, held, got, mine, other):
    bit, half = bit_of(masks), mine.shape[0]
    for out, which in ((mine, bit), (other, 1 - bit)):
        rows = pl.ds(pl.multiple_of(which * half, half), half)
        out[...] = (held[rows, :].astype(f32) + got[rows, :].astype(f32)).astype(bf16)


class SeqSum:
    def __init__(self, pairs):
        masks, m = [], 1
        while m < lax.axis_size("seq"):
            masks.append(m)
            m *= 2
        self.masks = list(zip(masks, masks[2:3] + masks[:2] + masks[3:]))
        rows = sum(a.shape[0] for a, _ in pairs) // 2
        shape = ((rows, pairs[0][0].shape[1]), bf16)
        flat = tuple(v for p in pairs for v in p)

        def kernel(refs, mine, other):
            first_halves_kernel(self.masks[0], [(refs[i], refs[i + 1]) for i in range(0, len(refs), 2)], mine, other)

        self.mine, self.other = run(kernel, [shape, shape], (flat,))

    def down(self, beside):
        masks = self.masks
        for i, now in enumerate(masks):
            if i < len(beside):
                self.other = tie(self.other, beside[i]())[0]
            got = partners(self.other, now)
            if i + 1 < len(masks):
                shape = ((got.shape[0] // 2, got.shape[1]), bf16)
                self.mine, self.other = run(functools.partial(next_halves_kernel, masks[i + 1]), [shape, shape], (self.mine, got))
        self.value = (self.mine.astype(f32) + got.astype(f32)).astype(bf16)

    def up(self, beside):
        for i, now in enumerate(self.masks[::-1]):
            if i < len(beside):
                self.value = tie(self.value, beside[i]())[0]
            got = partners(self.value, now)
            if i + 1 < len(self.masks):
                bit = bit_of(now)
                self.value = jnp.concatenate([jnp.where(bit == 0, self.value, got), jnp.where(bit == 0, got, self.value)], axis=0)
        return self.value, got


def unpack_kernel(masks, mine, got, lin, gate, out, entry):
    bit = bit_of(masks)
    cut = 1024
    for ref, which in ((mine, bit), (got, 1 - bit)):
        def piece(at, rows):
            return ref[at : at + rows, :].astype(f32)

        @pl.when(which == 0)
        def _():
            lin[1], gate[1] = piece(0, 512), piece(512, 512)
            lin[0], gate[0, :256], entry[0, :256] = piece(cut, 512), piece(cut + 512, 256), piece(cut + 768, 256)

        @pl.when(which == 1)
        def _():
            out[1, :, :256], out[1, :, 256:], entry[1] = piece(0, 256), piece(256, 256), piece(512, 512)
            gate[0, 256:] = piece(cut, 256)
            out[0, :, :256], out[0, :, 256:], entry[0, 256:] = piece(cut + 256, 256), piece(cut + 512, 256), piece(cut + 768, 256)


class Far:
    def __init__(self, value, at=None, smem=False):
        self.value, self.at, self.smem = value, at, smem
        self.shape = value.shape if at is None else value.shape[1:] if at != "rows" else (2,) + value.shape[1:]

    def source(self, ref):
        if self.at is None:
            return ref
        return ref.at[pl.ds(lax.axis_index("state") * 2, 2)] if self.at == "rows" else ref.at[self.at]


class Held:
    def __init__(self, source, ref, sem):
        self.ref, self.copy, self.shape, self.dtype = ref, pltpu.make_async_copy(source, ref, sem), ref.shape, ref.dtype
        self.copy.start()

    def ready(self):
        if self.copy is not None:
            self.copy.wait()
            self.copy = None

    def __getitem__(self, index):
        self.ready()
        return self.ref[index]


class Drained:
    def __init__(self, ref, target, sem):
        self.ref, self.copy, self.sent = ref, pltpu.make_async_copy(ref, target, sem), False
        self.shape, self.dtype = ref.shape, ref.dtype

    def __getitem__(self, index):
        return self.ref[index]

    def __setitem__(self, index, value):
        self.ref[index] = value

    def send(self):
        if not self.sent:
            self.copy.start()
            self.sent = True


def run(kernel, outs, groups, scratch=(), limit=24, flops=0):
    args = [a for g in groups for a in (g if isinstance(g, tuple) else (g,))]
    far_in = [i for i, a in enumerate(args) if isinstance(a, Far)]
    far_out = [i for i, o in enumerate(outs) if len(o) == 3]
    moved = sum(a.value.size * a.value.dtype.itemsize if isinstance(a, Far) else a.size * a.dtype.itemsize for a in args)

    def whole(*refs):
        ins, results = list(refs[: len(args)]), list(refs[len(args) : len(args) + len(outs)])
        rest = refs[len(args) + len(outs) :]
        own = rest[: len(scratch)]
        if far_in or far_out:
            buffers, sem = rest[len(scratch) : -1], rest[-1]
        for j, i in enumerate(far_in):
            ins[i] = Held(args[i].source(ins[i]), buffers[j], sem.at[j])
        for j, i in enumerate(far_out, len(far_in)):
            results[i] = Drained(buffers[j], results[i], sem.at[j])
        grouped, at = [], 0
        for g in groups:
            if isinstance(g, tuple):
                grouped.append(tuple(ins[at : at + len(g)]))
                at += len(g)
            else:
                grouped.append(ins[at])
                at += 1
        kernel(*grouped, *results, *own)
        for i in far_in:
            ins[i].ready()
        for i in far_out:
            results[i].send()
        for i in far_out:
            results[i].copy.wait()

    def space(far):
        return pl.BlockSpec(memory_space=pltpu.HBM if far else pltpu.VMEM)

    held = [(pltpu.SMEM if args[i].smem else pltpu.VMEM)(args[i].shape, args[i].value.dtype) for i in far_in]
    held += [pltpu.VMEM(outs[i][0], outs[i][1]) for i in far_out]
    if held:
        held.append(pltpu.SemaphoreType.DMA((len(held),)))
    return pl.pallas_call(
        whole,
        out_shape=[jax.ShapeDtypeStruct(o[0], o[1]) for o in outs],
        in_specs=[space(isinstance(a, Far)) for a in args],
        out_specs=[space(len(o) == 3) for o in outs],
        scratch_shapes=[pltpu.VMEM(*s) for s in scratch] + held,
        compiler_params=pltpu.CompilerParams(vmem_limit_bytes=limit * 2**20),
        cost_estimate=pl.CostEstimate(flops=flops, bytes_accessed=moved, transcendentals=0),
    )(*[a.value if isinstance(a, Far) else a for a in args])


def body(tokens, gain, bias, in_proj, out_proj, rate_log, angle_log, skip, glu_lin, glu_gate, positions, cotangent):
    peers = lax.axis_size("seq")
    core = lax.axis_index("state")
    rows, span, width = tokens.shape
    steps = span // CHUNKS
    n = 2 * span
    count = float(rows * span * peers)
    packed = ((8, 128), f32)
    one = 2 * n * 512 * 512
    far = ((n, 512), bf16, "far")
    low = ((n, 512), bf16)
    full = ((n, 512), f32)

    w_in = in_proj.reshape(2, 512, 256)
    w_out = out_proj.reshape(2, 256, 512)
    x_oth, cot_oth, in_oth, out_oth, lin_oth, gate_oth = (swap(w) for w in (tokens, cotangent, w_in, w_out, glu_lin, glu_gate))
    enter = [(Far(w_in, k), Far(in_oth, k)) for k in range(2)]

    stats, own, keep, dk, perm = run(
        functools.partial(prep_kernel, peers, steps),
        [((2 * peers, 4, 128), f32), ((32, 128), f32), ((2, n, 128), f32), ((2, peers, 8, 128), f32), ((n, n), bf16)],
        (Far(positions, smem=True),) + tuple(Far(v) for v in (tokens, gain, bias, skip, rate_log, angle_log)))
    oth = swap(own)
    ordered = ((peers, 8, 128), f32)

    for_seq, for_all = ((peers, 8, 128), f32), ((2 * peers, 8, 128), f32)
    scan_outs = [full, ((16, 8, 128), f32), for_seq, ((8, 512), f32)]
    xp, nl0, proj, comp, summ, nrm0 = run(
        functools.partial(enter_first_kernel, peers, steps, count), [far, far] + scan_outs,
        (lax.all_to_all(stats, ("seq", "state"), 0, 0), Far(tokens, "rows"), Far(x_oth, "rows"), perm, own, oth, keep) + enter[0], [packed], flops=2 * one)
    got, (cot_oth, out_oth, lin_oth, gate_oth) = blocking(summ, "seq", (cot_oth, out_oth, lin_oth, gate_oth))
    glu = [tuple(Far(w, k) for w in (w_out, out_oth, glu_lin, lin_oth, glu_gate, gate_oth)) for k in range(2)]
    cin0, sl0, gp0, act0, sig0, qv0, y0, stats = run(
        functools.partial(leave_first_kernel, peers, steps),
        [((SLAB, 512), f32), far, far, far, far, far, full, for_all],
        (got, comp, dk, own, oth, keep, proj, Far(xp), nrm0) + glu[0], [packed, ordered], flops=3 * one)
    got, _ = blocking(stats, ("seq", "state"), ())
    nl1, proj, comp, summ, nrm1 = run(
        functools.partial(enter_second_kernel, peers, steps, count), [low] + scan_outs,
        (got, y0, own, oth, keep) + enter[1], [packed], flops=one)
    got, _ = blocking(summ, "seq", ())
    turn_outs = [((8, 512), f32), full, ((16, 8, 128), f32)]
    cin1, bo_own, bo_oth, d_out1, act1, dl1, dg1, sl1, dml1, skip1, dst, comp, summ = run(
        functools.partial(turn_kernel, peers, steps),
        [((SLAB, 512), f32), ((n, 256), bf16, "far"), ((n, 256), bf16, "far"), low, low, low, low, low, low] + turn_outs + [for_seq],
        (got, comp, dk, own, oth, keep, proj, y0, nrm1) + glu[1] + (perm, Far(cotangent, "rows"), Far(cot_oth, "rows")),
        [packed, ordered, full, full, full, full], flops=8 * one)
    got, (bo_oth,) = blocking(summ, "seq", (bo_oth,))
    g1_own, g1_oth, s1_own, s1_oth, dn, stats = run(
        functools.partial(adjoint_second_kernel, peers, steps),
        [((2048, 256), f32), ((2048, 256), bf16), ((16, 128), f32), ((16, 128), f32), full, for_all],
        (got, comp, dk, own, oth, keep, nl1, y0, nrm1, cin1, sl1, dst, dml1) + enter[1] + (skip1, act1, dl1, dg1),
        [packed, ordered, full, low], flops=6 * one)
    got, (bo_oth, g1_oth) = blocking(stats, ("seq", "state"), (bo_oth, g1_oth))
    bo_got, g1_got = swap(bo_oth), swap(g1_oth)
    d_out0, dml0, g0_own, g0_oth, skip0, dst, comp, summ = run(
        functools.partial(back_first_kernel, steps, count),
        [full, low, ((1536, 256), f32), ((1536, 256), bf16)] + turn_outs + [for_seq],
        (got, dn, y0, nrm1, d_out1, own, oth, keep, Far(xp), nrm0, Far(gp0), Far(sig0), Far(qv0)) + glu[0] + (Far(act0), Far(sl0)),
        [packed, low, low], flops=6 * one)
    got, (g0_oth, bo_got, g1_got) = blocking(summ, "seq", (g0_oth, bo_got, g1_got))
    g0_got = swap(g0_oth)
    i0_own, i0_oth, s_own, s_oth, a_own, a_oth = run(
        functools.partial(adjoint_first_kernel, peers, steps),
        [((512, 256), f32), ((512, 256), bf16), ((32, 128), f32), ((32, 128), f32), ((n, 256), bf16), ((n, 256), bf16)],
        (got, comp, dk, own, oth, keep, Far(nl0), Far(xp), nrm0, cin0, Far(sl0), dst, dml0) + enter[0]
        + (skip0, d_out0, perm, s1_own, s1_oth),
        [packed, ordered, full, full, low], flops=4 * one)
    i0_got = swap(i0_oth)
    bulk = SeqSum([(g1_own, g1_got), (g0_own, g0_got), (i0_own, i0_got)])
    s_got, a_got = swap(s_oth), swap(a_oth)
    s_all = jnp.broadcast_to((s_own + s_got)[None], (peers, 32, 128))
    got = lax.all_to_all(s_all, "seq", 0, 0)
    pair = (2, span, width)
    d_in, ngg, bias_grad, skip_grad, rate_grad, angle_grad = run(
        functools.partial(finish_kernel, count),
        [((rows, span, width), f32), ((2, 256), f32), ((2, 256), f32), ((2, 256), f32), ((2, 128), f32), ((2, 128), f32)],
        ((got,), a_own.reshape(pair), a_got.reshape(pair), Far(tokens), nrm0, Far(rate_log), Far(angle_log)),
        [((32, 128), f32)])
    bulk.down([lambda: (), lambda: s_all, lambda: got, lambda: d_in])
    mine, other = bulk.up([])
    lin_grad, gate_grad, out_grad, in_grad = run(
        functools.partial(unpack_kernel, bulk.masks[0]),
        [((2, 512, 256), f32), ((2, 512, 256), f32), ((2, 256, 512), f32), ((2, 512, 256), f32)],
        (mine, other))
    out_grad, in_grad = out_grad.reshape(2, 2, 128, 512), in_grad.reshape(2, 512, 2, 128)
    mine, other = bo_own.reshape(pair), bo_got.reshape(pair)
    block_out = jnp.concatenate([jnp.where(core == 0, mine, other), jnp.where(core == 0, other, mine)], axis=0)
    return (block_out, d_in, ngg, bias_grad, in_grad, out_grad, rate_grad, angle_grad, skip_grad, lin_grad, gate_grad)


def solution(mesh):
    placed = (
        P(None, "seq", "state"),
        P(None, "state"),
        P(None, "state"),
        P(None, None, None, "state"),
        P(None, None, "state", None),
        P(None, "state"),
        P(None, "state"),
        P(None, "state"),
        P(None, None, "state"),
        P(None, None, "state"),
        P(),
        P(None, "seq", "state"),
    )
    return jax.shard_map(
        body,
        mesh=mesh,
        in_specs=placed,
        out_specs=(
            P(None, "seq", "state"),
            P(None, "seq", "state"),
            P(None, "state"),
            P(None, "state"),
            P(None, None, None, "state"),
            P(None, None, "state", None),
            P(None, "state"),
            P(None, "state"),
            P(None, "state"),
            P(None, None, "state"),
            P(None, None, "state"),
        ),
        check_vma=False,
    )
```

```python
import functools

import jax
import jax.numpy as jnp
from jax import lax
from jax.experimental import pallas as pl
from jax.experimental.pallas import tpu as pltpu
from jax.sharding import PartitionSpec as P

f32, bf16 = jnp.float32, jnp.bfloat16
norm_eps = 1e-05
CHUNKS = 8
SLAB = 2 * CHUNKS
TILE = 256


def mm(a, b):
    return jnp.dot(a, b, preferred_element_type=f32)


def mm_nt(a, b):
    return lax.dot_general(a, b, (((1,), (1,)), ((), ())), preferred_element_type=f32)


def mm_tn(a, b):
    return lax.dot_general(a, b, (((0,), (0,)), ((), ())), preferred_element_type=f32)


def wide(row):
    return jnp.broadcast_to(row, (CHUNKS, 128))


def cmul(ar, ai, br, bi):
    return ar * br - ai * bi, ar * bi + ai * br


def row_of_tiles(tiles):
    return jnp.concatenate([tiles[i : i + 1, :] for i in range(tiles.shape[0])], axis=1)


def channel_row(core, own, oth, at):
    mine, other = own[at : at + 2, :], oth[at : at + 2, :]
    low = jnp.where(core == 0, mine, other)
    high = jnp.where(core == 0, other, mine)
    return jnp.concatenate([low[0:1], low[1:2], high[0:1], high[1:2]], axis=1)


def own_cols(core, width):
    return pl.ds(pl.multiple_of(core * width, width), width)


def oth_cols(core, width):
    return pl.ds(pl.multiple_of((1 - core) * width, width), width)


def scan(drive, lams, keep_ref, which, steps, reverse, start, visit):
    order = range(steps - 1, -1, -1) if reverse else range(steps)
    state = dict(start)
    for s in order:
        for row in range(2):
            at = s * SLAB + row * CHUNKS
            keep = keep_ref[which, at : at + CHUNKS, :]
            for half in range(2):
                lr, li = lams[half]
                hr, hi = state[half, row]
                hr, hi = keep * hr, keep * hi
                dr, di = drive(s, row, half)
                state[half, row] = (lr * hr - li * hi + dr, lr * hi + li * hr + di)
        visit(s, state, keep_ref)
    return state


def keep_products(keep_ref, which, steps):
    out = []
    for row in range(2):
        total = keep_ref[which, row * CHUNKS : (row + 1) * CHUNKS, :]
        for s in range(1, steps):
            at = s * SLAB + row * CHUNKS
            total = total * keep_ref[which, at : at + CHUNKS, :]
        out.append(total)
    return out


def chunk_scan(ends, keeps, powers, reverse, comp_ref, packed):
    index = lax.broadcasted_iota(jnp.int32, (CHUNKS, 128), 0)

    def shifted(value, by, fill):
        turned = pltpu.roll(value, CHUNKS - by if reverse else by, 0)
        valid = index < CHUNKS - by if reverse else index >= by
        return jnp.where(valid, turned, fill)

    for half in range(2):
        for row in range(2):
            er, ei = ends[half, row]
            pr, pi = powers[half][0] * keeps[row], powers[half][1] * keeps[row]
            for by in (1, 2, 4):
                tr, ti = cmul(pr, pi, shifted(er, by, 0.0), shifted(ei, by, 0.0))
                er, ei = er + tr, ei + ti
                pr, pi = cmul(pr, pi, shifted(pr, by, 1.0), shifted(pi, by, 0.0))
            edge = 0 if reverse else CHUNKS - 1
            q = row * 2 + half
            packed[q : q + 1, :] = er[edge : edge + 1, :]
            packed[4 + q : 5 + q, :] = ei[edge : edge + 1, :]
            base = (half * 2 + row) * 4
            comp_ref[base] = shifted(er, 1, 0.0)
            comp_ref[base + 1] = shifted(ei, 1, 0.0)
            comp_ref[base + 2] = shifted(pr, 1, 1.0)
            comp_ref[base + 3] = shifted(pi, 1, 0.0)


def device_carry(me, peers, got, held, dk_ref, which, own, oth, base, conj, reverse, packed):
    got_ref = arrange(got, held)
    index = lax.broadcasted_iota(jnp.int32, (CHUNKS, 128), 0)
    is_own = index % 2 == 0
    sign = jnp.where(index < 4, -1.0, 1.0) * (-1.0 if conj else 1.0)
    ar = jnp.where(is_own, wide(own[base + 11 : base + 12, :]), wide(oth[base + 11 : base + 12, :]))
    ai = jnp.where(is_own, wide(own[base + 12 : base + 13, :]), wide(oth[base + 12 : base + 13, :]))
    ai = ai * sign

    def step(k, held):
        at = peers - 1 - k if reverse else k
        reached = at > me if reverse else at < me
        new = dk_ref[which, at] * (ar * held + ai * pltpu.roll(held, 4, 0)) + got_ref[at]
        return jnp.where(reached, new, held)

    packed[...] = lax.fori_loop(0, peers, step, jnp.zeros((8, 128), f32), unroll=peers <= 16)


def entries(comp_ref, packed):
    start = {}
    for half in range(2):
        for row in range(2):
            base, q = (half * 2 + row) * 4, row * 2 + half
            hr, hi = wide(packed[q : q + 1, :]), wide(packed[4 + q : 5 + q, :])
            tr, ti = cmul(comp_ref[base + 2], comp_ref[base + 3], hr, hi)
            start[half, row] = (comp_ref[base] + tr, comp_ref[base + 1] + ti)
    return start


def decay(own, oth, base, at, conj=False):
    sign = -1.0 if conj else 1.0
    return [(wide(r[base + at : base + at + 1, :]), sign * wide(r[base + at + 1 : base + at + 2, :])) for r in (own, oth)]


def scales(own, oth, base):
    return [wide(r[base + 8 : base + 9, :]) for r in (own, oth)]


def nothing(*_):
    return None


def zeros_start():
    zero = jnp.zeros((CHUNKS, 128), f32)
    return {(half, row): (zero, zero) for half in range(2) for row in range(2)}


def part(s, row):
    at = s * SLAB + row * CHUNKS
    return slice(at, at + CHUNKS)


def cols(half, im):
    at = half * 256 + im * 128
    return slice(at, at + 128)


def flat_rows(ref):
    value = ref[...]
    return value.reshape(value.shape[0] * value.shape[1], value.shape[2])


def spread(out_ref, packed):
    value = packed[...]
    out_ref[...] = value if len(out_ref.shape) == 2 else jnp.broadcast_to(value[None], out_ref.shape)


def arrange(got, held):
    if len(got) == 1:
        return got[0]
    me = place()[0]
    for m, block in enumerate(got):
        for e in range(4):
            held[(((me >> 2) ^ m) << 2) + ((me & 3) ^ e)] = block[e]
    return held


def place():
    return lax.axis_index("seq"), lax.axis_index("state")


def stats_kernel(tokens, stats):
    s1 = s2 = 0.0
    for r in range(tokens.shape[0]):
        x = tokens[r].astype(f32)
        s1 = s1 + jnp.sum(x, axis=0, keepdims=True)
        s2 = s2 + jnp.sum(x * x, axis=0, keepdims=True)
    for i in range(2):
        stats[0, i : i + 1, :] = s1[:, 128 * i : 128 * (i + 1)]
        stats[0, 2 + i : 3 + i, :] = s2[:, 128 * i : 128 * (i + 1)]
    stats[...] = jnp.broadcast_to(stats[0][None], stats.shape)


def prep_kernel(peers, steps, span, pos, raw, small, keep, dk, perm):
    seq, core = place()
    docs = pos.shape[1]

    count = perm.shape[1]
    p = lax.broadcasted_iota(jnp.int32, (count, count), 0)
    q = lax.broadcasted_iota(jnp.int32, (count, count), 1)
    source = ((p >> 3) & 1) * span + (p & 7) * steps + (p >> 4)
    perm[0] = jnp.where(q == source, 1.0, 0.0).astype(bf16)
    source = ((q >> 3) & 1) * span + (q & 7) * steps + (q >> 4)
    perm[1] = jnp.where(p == source, 1.0, 0.0).astype(bf16)

    small[...] = jnp.zeros_like(small)
    for k in range(2):
        at = 16 * k
        values = raw[k : k + 1, :]
        for j in range(6):
            small[at + j : at + j + 1, :] = values[:, 128 * j : 128 * (j + 1)]
        rate = jnp.exp(values[:, 768:896])
        angle = jnp.exp(values[:, 896:])
        modulus = jnp.exp(-rate)
        lr, li = modulus * jnp.cos(angle), modulus * jnp.sin(angle)
        small[at + 6 : at + 7, :] = lr
        small[at + 7 : at + 8, :] = li
        small[at + 8 : at + 9, :] = jnp.sqrt(1.0 - modulus * modulus)
        power = 1
        while power < span:
            lr, li = cmul(lr, li, lr, li)
            power *= 2
            if power == steps:
                small[at + 9 : at + 10, :] = lr
                small[at + 10 : at + 11, :] = li
        small[at + 11 : at + 12, :] = lr
        small[at + 12 : at + 13, :] = li

    chunk = lax.broadcasted_iota(jnp.int32, (CHUNKS, 128), 0) * steps + seq * span
    for row in range(2):
        targets = [pos[core * 2 + row, d] - chunk for d in range(docs)]
        for s in range(steps + 1):
            hit = targets[0] == s
            for t in targets[1:]:
                hit = jnp.logical_or(hit, t == s)
            value = jnp.where(hit, 0.0, 1.0)
            at = s * SLAB + row * CHUNKS
            if s < steps:
                keep[0, at : at + CHUNKS, :] = value
            if s >= 1:
                keep[1, at - SLAB : at - SLAB + CHUNKS, :] = value

    first_row = (lax.broadcasted_iota(jnp.int32, (CHUNKS, 128), 0) // 2) % 2 == 0
    owners = ([], [])
    for d in range(docs):
        a, b = pos[core * 2, d], pos[core * 2 + 1, d]
        owners[0].append(jnp.where(first_row, a // span, b // span))
        owners[1].append(jnp.where(first_row, (a + span - 1) // span - 1, (b + span - 1) // span - 1))

    def mark(j, _):
        for m in range(2):
            hit = owners[m][0] == j
            for o in owners[m][1:]:
                hit = jnp.logical_or(hit, o == j)
            dk[m, j] = jnp.where(hit, 0.0, 1.0)
        return 0

    lax.fori_loop(0, peers, mark, 0)


def norm_rows(total, squares, count, core, own, oth, base, nrm):
    mean = total / count
    inv = lax.rsqrt(squares / count - mean * mean + norm_eps)
    nrm[0:1, :] = mean
    nrm[1:2, :] = inv
    nrm[2:3, :] = channel_row(core, own, oth, base)
    nrm[3:4, :] = channel_row(core, own, oth, base + 2)
    nrm[4:5, :] = channel_row(core, own, oth, base + 4)
    nrm[5:8, :] = jnp.zeros_like(nrm[5:8, :])


def normalized(x, nrm):
    xhat = (x - nrm[0:1, :]) * nrm[1:2, :]
    return xhat, xhat * nrm[2:3, :] + nrm[3:4, :]


def project_and_scan(steps, base, which, reverse, own, oth, keep, win_own, win_oth, nl, proj, comp, summ, packed):
    proj[:, :256] = mm(nl[...], win_own[...])
    proj[:, 256:] = mm(nl[...], win_oth[...])
    lams, sc = decay(own, oth, base, 6), scales(own, oth, base)

    def drive(s, row, half):
        return sc[half] * proj[part(s, row), cols(half, 0)], sc[half] * proj[part(s, row), cols(half, 1)]

    ends = scan(drive, lams, keep, which, steps, reverse, zeros_start(), nothing)
    chunk_scan(ends, keep_products(keep, which, steps), decay(own, oth, base, 9), reverse, comp, packed)
    spread(summ, packed)


def enter_first_kernel(peers, steps, count, got, x_own, x_oth, perm, own, oth, keep, win_own, win_oth,
                       xp, nl, proj, comp, summ, nrm, packed):
    _, core = place()
    sums = got[0:2]
    for j in range(1, peers):
        sums = sums + got[2 * j : 2 * j + 2]
    total = jnp.concatenate([sums[0, 0:1], sums[0, 1:2], sums[1, 0:1], sums[1, 1:2]], axis=1)
    squares = jnp.concatenate([sums[0, 2:3], sums[0, 3:4], sums[1, 2:3], sums[1, 3:4]], axis=1)
    norm_rows(total, squares, count, core, own, oth, 0, nrm)
    xp[:, own_cols(core, 256)] = mm(perm[0], flat_rows(x_own)).astype(bf16)
    xp[:, oth_cols(core, 256)] = mm(perm[0], flat_rows(x_oth)).astype(bf16)
    _, normed = normalized(xp[...].astype(f32), nrm)
    nl[...] = normed.astype(bf16)
    project_and_scan(steps, 0, 0, False, own, oth, keep, win_own, win_oth, nl, proj, comp, summ, packed)


def sum_peers(got):
    if len(got) == 1 and len(got[0].shape) == 3:
        got = [got[0].at[j] for j in range(got[0].shape[0])]
    total = got[0][...]
    for part in got[1:]:
        total = total + part[...]
    return total


def enter_second_kernel(peers, steps, count, got, x, own, oth, keep, win_own, win_oth,
                        nl, proj, comp, summ, nrm, packed):
    _, core = place()
    sums = sum_peers(got)
    norm_rows(row_of_tiles(sums[0:4]), row_of_tiles(sums[4:8]), count, core, own, oth, 16, nrm)
    _, normed = normalized(x[...], nrm)
    nl[...] = normed.astype(bf16)
    project_and_scan(steps, 16, 1, True, own, oth, keep, win_own, win_oth, nl, proj, comp, summ, packed)


def states_of(peers, steps, base, which, reverse, got, comp, dk, own, oth, keep, proj, cin, sl, packed, held):
    device_carry(place()[0], peers, got, held, dk, which, own, oth, base, False, reverse, packed)
    start = entries(comp, packed)
    lams, sc = decay(own, oth, base, 6), scales(own, oth, base)
    for (half, row), (hr, hi) in start.items():
        cin[part(0, row), cols(half, 0)] = hr
        cin[part(0, row), cols(half, 1)] = hi

    def drive(s, row, half):
        return sc[half] * proj[part(s, row), cols(half, 0)], sc[half] * proj[part(s, row), cols(half, 1)]

    def visit(s, state, _):
        for half in range(2):
            for im in range(2):
                both = jnp.concatenate([state[half, row][im] for row in range(2)], axis=0)
                sl[s * SLAB : (s + 1) * SLAB, cols(half, im)] = both.astype(bf16)

    scan(drive, lams, keep, which, steps, reverse, start, visit)


def mix_and_gate(core, x, nrm, sl, wout_own, wout_oth, lin_own, lin_oth, gate_own, gate_oth, gp, act, sig, qv, y):
    c = 0.7978845608028654
    for i in range(0, y.shape[0], TILE):
        rows = slice(i, i + TILE)
        _, normed = normalized(x[rows, :].astype(f32), nrm)
        mixed = mm(sl[rows, :256], wout_own[...]) + mm(sl[rows, 256:], wout_oth[...]) + nrm[4:5, :] * normed
        sq = mixed * mixed
        t = jnp.tanh(mixed * (c + (c * 0.044715) * sq))
        upper = 0.5 + 0.5 * t
        low = (mixed * upper).astype(bf16)
        act[rows, :] = low
        gp[rows, :] = (upper + mixed * (upper * (1.0 - t)) * (c + (3 * c * 0.044715) * sq)).astype(gp.dtype)
        for w_lin, w_gate, at in ((lin_own, gate_own, own_cols(core, 256)), (lin_oth, gate_oth, oth_cols(core, 256))):
            linear = mm(low, w_lin[...])
            gating = mm(low, w_gate[...])
            sg = 0.5 + 0.5 * jnp.tanh(0.5 * gating)
            out = linear * sg
            sig[rows, at] = sg.astype(sig.dtype)
            qv[rows, at] = (out * (1.0 - sg)).astype(qv.dtype)
            y[rows, at] = x[rows, at].astype(f32) + out
        yield rows


def leave_first_kernel(peers, steps, got, comp, dk, own, oth, keep, proj, x, nrm, wout_own, wout_oth,
                       lin_own, lin_oth, gate_own, gate_oth, cin, sl, gp, act, sig, qv, y, stats, packed, held):
    states_of(peers, steps, 0, 0, False, got, comp, dk, own, oth, keep, proj, cin, sl, packed, held)
    s1 = s2 = 0.0
    for rows in mix_and_gate(place()[1], x, nrm, sl, wout_own, wout_oth, lin_own, lin_oth, gate_own, gate_oth, gp, act, sig, qv, y):
        out = y[rows, :]
        s1, s2 = s1 + jnp.sum(out, axis=0, keepdims=True), s2 + jnp.sum(out * out, axis=0, keepdims=True)
    pack_two(s1, s2, packed)
    spread(stats, packed)


def pack_two(a, b, packed):
    for i in range(4):
        packed[i : i + 1, :] = a[:, 128 * i : 128 * (i + 1)]
        packed[4 + i : 5 + i, :] = b[:, 128 * i : 128 * (i + 1)]


def glu_backward(steps, base, adj_which, adj_reverse, core, d_out, nrm, x, gp, sig, qv, own, oth, keep, wout_own, wout_oth,
                 lin_own, lin_oth, gate_own, gate_oth, skip_row, dst, comp, summ, packed, dl, dg, dml):
    mine, other = own_cols(core, 256), oth_cols(core, 256)
    total = 0.0
    for i in range(0, dl.shape[0], TILE):
        rows = slice(i, i + TILE)
        grad = d_out(rows)
        dl[rows, :] = (grad * sig[rows, :].astype(f32)).astype(bf16)
        dg[rows, :] = (grad * qv[rows, :].astype(f32)).astype(bf16)
        d_active = (mm_nt(dl[rows, mine], lin_own[...]) + mm_nt(dg[rows, mine], gate_own[...])
                    + mm_nt(dl[rows, other], lin_oth[...]) + mm_nt(dg[rows, other], gate_oth[...]))
        d_mixed = d_active * gp[rows, :].astype(f32)
        _, normed = normalized(x[rows, :].astype(f32), nrm)
        total = total + jnp.sum(d_mixed * normed, axis=0, keepdims=True)
        low = d_mixed.astype(bf16)
        dml[rows, :] = low
        dst[rows, :256] = mm_nt(low, wout_own[...])
        dst[rows, 256:] = mm_nt(low, wout_oth[...])
    skip_row[0:1, :] = total
    lams = decay(own, oth, base, 6, conj=True)

    def drive(s, row, half):
        return dst[part(s, row), cols(half, 0)], dst[part(s, row), cols(half, 1)]

    ends = scan(drive, lams, keep, adj_which, steps, adj_reverse, zeros_start(), nothing)
    chunk_scan(ends, keep_products(keep, adj_which, steps), decay(own, oth, base, 9, conj=True), adj_reverse, comp, packed)
    spread(summ, packed)


def mixer_grads(act, dl, dg, sl, dml, g_own, g_oth):
    _, core = place()
    mine, other = own_cols(core, 256), oth_cols(core, 256)
    left = act[...].T
    for ref, at in ((dl, 0), (dg, 512)):
        g_own[at : at + 512, :] = mm(left, ref[:, mine])
        g_oth[at : at + 512, :] = mm(left, ref[:, other]).astype(bf16)
    for ref, cut in ((g_own, slice(0, 256)), (g_oth, slice(256, 512))):
        left = sl[:, cut].T
        for i in range(2):
            ref[1024 + 256 * i : 1280 + 256 * i, :] = mm(left, dml[:, 256 * i : 256 * (i + 1)]).astype(ref.dtype)


def in_grads(nl, dp, g_own, g_oth):
    left = nl[...].T
    g_own[...] = mm(left, dp[:, :256])
    g_oth[...] = mm(left, dp[:, 256:]).astype(bf16)


def turn_kernel(peers, steps, got, comp_in, dk, own, oth, keep, proj, x, nrm, wout_own, wout_oth,
                lin_own, lin_oth, gate_own, gate_oth, perm, cot_own, cot_oth,
                cin, bo_own, bo_oth, d_out, act, dl, dg, sl, dml, skip_row, dst, comp, summ,
                packed, held, gp, sig, qv, y):
    _, core = place()
    states_of(peers, steps, 16, 1, True, got, comp_in, dk, own, oth, keep, proj, cin, sl, packed, held)
    for _ in mix_and_gate(core, x, nrm, sl, wout_own, wout_oth, lin_own, lin_oth, gate_own, gate_oth, gp, act, sig, qv, y):
        pass
    bo_own[...] = mm(perm[1], y[:, own_cols(core, 256)].astype(bf16)).astype(bf16)
    bo_oth[...] = mm(perm[1], y[:, oth_cols(core, 256)].astype(bf16)).astype(bf16)
    d_out[:, own_cols(core, 256)] = mm(perm[0], flat_rows(cot_own)).astype(bf16)
    d_out[:, oth_cols(core, 256)] = mm(perm[0], flat_rows(cot_oth)).astype(bf16)
    glu_backward(steps, 16, 0, False, core, lambda rows: d_out[rows, :].astype(f32), nrm, x, gp, sig, qv, own, oth, keep, wout_own, wout_oth,
                 lin_own, lin_oth, gate_own, gate_oth, skip_row, dst, comp, summ, packed, dl, dg, dml)


def adjoint_part(peers, steps, base, keep_which, adj_which, adj_reverse, got, comp, dk, own, oth, keep, nl, x, nrm,
                 cin, sl, dst, dml, win_own, win_oth, skip_row, small_own, small_oth, at, packed, held, proj, dp, keep_tile):
    _, core = place()
    device_carry(place()[0], peers, got, held, dk, adj_which, own, oth, base, True, adj_reverse, packed)
    start = entries(comp, packed)
    lams, sc = decay(own, oth, base, 6, conj=True), scales(own, oth, base)
    zero = jnp.zeros((CHUNKS, 128), f32)
    acc = {half: [zero, zero, zero] for half in range(2)}
    proj[:, :256] = mm(nl[...], win_own[...])
    proj[:, 256:] = mm(nl[...], win_oth[...])

    def prior(s, half, im):
        before = s - 1 if adj_reverse else s + 1
        if 0 <= before < steps:
            return sl[before * SLAB : (before + 1) * SLAB, cols(half, im)].astype(f32)
        return cin[:, cols(half, im)]

    def drive(s, row, half):
        return dst[part(s, row), cols(half, 0)], dst[part(s, row), cols(half, 1)]

    def visit(s, state, _):
        for half in range(2):
            prior_re, prior_im = prior(s, half, 0), prior(s, half, 1)
            for row in range(2):
                ar, ai = state[half, row]
                pr, pi = prior_re[part(0, row)], prior_im[part(0, row)]
                keep_here = keep[keep_which, part(s, row), :]
                acc[half][0] = acc[half][0] + keep_here * (ar * pr + ai * pi)
                acc[half][1] = acc[half][1] + keep_here * (ai * pr - ar * pi)
                acc[half][2] = acc[half][2] + (ar * proj[part(s, row), cols(half, 0)] + ai * proj[part(s, row), cols(half, 1)])
            for im in range(2):
                both = jnp.concatenate([sc[half] * state[half, row][im] for row in range(2)], axis=0)
                dp[s * SLAB : (s + 1) * SLAB, cols(half, im)] = both.astype(bf16)

    scan(drive, lams, keep, adj_which, steps, adj_reverse, start, visit)

    bias_row = gain_row = 0.0
    for i in range(0, dp.shape[0], TILE):
        rows = slice(i, i + TILE)
        d_normed = dml[rows, :].astype(f32) * nrm[4:5, :] + mm_nt(dp[rows, :256], win_own[...]) + mm_nt(dp[rows, 256:], win_oth[...])
        xhat, _ = normalized(x[rows, :].astype(f32), nrm)
        bias_row = bias_row + jnp.sum(d_normed, axis=0, keepdims=True)
        gain_row = gain_row + jnp.sum(d_normed * xhat, axis=0, keepdims=True)
        keep_tile(rows, d_normed)
    pack_two(bias_row, gain_row, packed)

    for ref, half, flip in ((small_own, 0, 0), (small_oth, 1, 1)):
        ref[at : at + 16, :] = jnp.zeros((16, 128), f32)
        for j, row in enumerate((skip_row[0:1, :], bias_row, gain_row)):
            low = (core == 0) if flip == 0 else (core == 1)
            pick = jnp.where(low, row[:, :256], row[:, 256:])
            ref[at + 2 * j : at + 2 * j + 1, :] = pick[:, :128]
            ref[at + 2 * j + 1 : at + 2 * j + 2, :] = pick[:, 128:]
        for j in range(3):
            ref[at + 6 + j : at + 7 + j, :] = jnp.sum(acc[half][j], axis=0, keepdims=True)


def adjoint_second_kernel(peers, steps, got, comp, dk, own, oth, keep, nl, x, nrm, cin, sl, dst, dml, win_own, win_oth, skip_row, act, dl, dg,
                          g_own, g_oth, small_own, small_oth, dn, stats, packed, held, proj, dp):
    def keep_tile(rows, d_normed):
        dn[rows, :] = d_normed

    adjoint_part(peers, steps, 16, 1, 0, False, got, comp, dk, own, oth, keep, nl, x, nrm,
                 cin, sl, dst, dml, win_own, win_oth, skip_row, small_own, small_oth, 0, packed, held, proj, dp, keep_tile)
    spread(stats, packed)
    mixer_grads(act, dl, dg, sl, dml, g_own, g_oth)
    in_grads(nl, dp, g_own.at[1536:], g_oth.at[1536:])


def back_first_kernel(steps, count, got, dn, x2, nrm2, d_out2, own, oth, keep, x, nrm, gp, sig, qv,
                      wout_own, wout_oth, lin_own, lin_oth, gate_own, gate_oth,
                      act, sl, d_out, dml, g_own, g_oth, skip_row, dst, comp, summ, packed, dl, dg):
    sums = sum_peers(got)
    bias_row, gain_row = row_of_tiles(sums[0:4]), row_of_tiles(sums[4:8])
    mean, inv, gain = nrm2[0:1, :], nrm2[1:2, :], nrm2[2:3, :]
    scaled, shift, slope = inv * gain, inv * gain * bias_row / count, inv * inv * gain * gain_row / count

    def d_in(rows):
        value = d_out2[rows, :].astype(f32) + scaled * dn[rows, :] - shift - slope * (x2[rows, :] - mean)
        d_out[rows, :] = value
        return value

    glu_backward(steps, 0, 1, True, place()[1], d_in, nrm, x, gp, sig, qv, own, oth, keep, wout_own, wout_oth,
                 lin_own, lin_oth, gate_own, gate_oth, skip_row, dst, comp, summ, packed, dl, dg, dml)
    mixer_grads(act, dl, dg, sl, dml, g_own, g_oth)


def adjoint_first_kernel(peers, steps, got, comp, dk, own, oth, keep, nl, x, nrm, cin, sl, dst, dml, win_own, win_oth, skip_row,
                         d_out, perm, small1_own, small1_oth,
                         g_own, g_oth, small_own, small_oth, a_own, a_oth, packed, held, proj, tmp, dp):
    _, core = place()
    scaled = nrm[1:2, :] * nrm[2:3, :]

    def keep_tile(rows, d_normed):
        tmp[rows, :] = (d_out[rows, :] + scaled * d_normed).astype(bf16)

    adjoint_part(peers, steps, 0, 0, 1, True, got, comp, dk, own, oth, keep, nl, x, nrm,
                 cin, sl, dst, dml, win_own, win_oth, skip_row, small_own, small_oth, 0, packed, held, proj, dp, keep_tile)
    small_own[16:32, :] = small1_own[...]
    small_oth[16:32, :] = small1_oth[...]
    a_own[...] = mm(perm[1], tmp[:, own_cols(core, 256)]).astype(bf16)
    a_oth[...] = mm(perm[1], tmp[:, oth_cols(core, 256)]).astype(bf16)
    in_grads(nl, dp, g_own, g_oth)


def finish_kernel(count, got, a_mine, a_other, tokens, nrm, raw,
                  d_in, ngg, bias, skip, rate_grad, angle_grad, packed):
    _, core = place()
    packed[...] = sum_peers(got)
    for k in range(2):
        at = 16 * k
        for ref, j in ((skip, 0), (bias, 2), (ngg, 4)):
            ref[k : k + 1, :128] = packed[at + j : at + j + 1, :]
            ref[k : k + 1, 128:] = packed[at + j + 1 : at + j + 2, :]
        values = raw[k : k + 1, :]
        rate = jnp.exp(values[:, 768:896])
        angle = jnp.exp(values[:, 896:])
        modulus = jnp.exp(-rate)
        scale = jnp.sqrt(1.0 - modulus * modulus)
        cos, sin = jnp.cos(angle), jnp.sin(angle)
        dr, di, ds = (packed[at + j : at + j + 1, :] for j in (6, 7, 8))
        g_mod = dr * cos + di * sin - ds * modulus / scale
        rate_grad[k : k + 1, :] = -g_mod * modulus * rate
        angle_grad[k : k + 1, :] = modulus * (di * cos - dr * sin) * angle
    mine = nrm[:, own_cols(core, 256)]
    mean, inv, gain = mine[0:1, :], mine[1:2, :], mine[2:3, :]
    bias_row, gain_row = bias[0:1, :], ngg[0:1, :]
    flat = inv * gain / count
    for r in range(4):
        held_rows = jnp.where(core == r // 2, a_mine[r % 2].astype(f32), a_other[r % 2].astype(f32))
        xhat = (tokens[r].astype(f32) - mean) * inv
        d_in[r] = held_rows - flat * (bias_row + xhat * gain_row)


def swap(value):
    return lax.ppermute(value, "state", [(0, 1), (1, 0)])


def to_all(value, axes):
    peers = 1
    for a in axes:
        peers *= lax.axis_size(a)
    return lax.all_to_all(jnp.broadcast_to(value[None], (peers,) + value.shape), axes, 0, 0)


def blocking(value, axes, others):
    value, others = lax.optimization_barrier((value, others))
    got, others = lax.optimization_barrier((lax.all_to_all(value, axes, 0, 0), others))
    return (got,), others


def gather_seq(value):
    if lax.axis_size("seq") != 16:
        return (to_all(value, ("seq",)),)
    near = jnp.stack([value] + [partner(value, m) for m in (1, 2, 3)])
    return (near,) + tuple(partner(near, m) for m in (4, 8, 12))


def sum_all(value):
    if lax.axis_size("seq") != 16:
        return (to_all(value, ("seq", "state")),)
    value = value + swap(value)
    near = value + partner(value, 1) + partner(value, 2) + partner(value, 3)
    return (near,) + tuple(partner(near, m) for m in (4, 8, 12))


def partner(value, mask):
    size = lax.axis_size("seq")
    return lax.ppermute(value, "seq", [(i, i ^ mask) for i in range(size)])


def partners(value, masks):
    size = lax.axis_size("seq")
    return lax.ppermute(value, ("seq", "state"), [(2 * i + c, 2 * (i ^ masks[c]) + c) for i in range(size) for c in range(2)])


def tie(value, others):
    return lax.optimization_barrier((value, others))


def bit_of(masks):
    me, core = place()
    return (me // jnp.where(core == 0, masks[0], masks[1])) & 1


def first_halves_kernel(masks, pairs, mine, other):
    bit, at = bit_of(masks), 0
    for own, got in pairs:
        half = own.shape[0] // 2
        for out, which in ((mine, bit), (other, 1 - bit)):
            rows = pl.ds(pl.multiple_of(which * half, half), half)
            out[at : at + half, :] = (own[rows, :] + got[rows, :].astype(f32)).astype(bf16)
        at += half


def next_halves_kernel(masks, held, got, mine, other):
    bit, half = bit_of(masks), mine.shape[0]
    for out, which in ((mine, bit), (other, 1 - bit)):
        rows = pl.ds(pl.multiple_of(which * half, half), half)
        out[...] = (held[rows, :].astype(f32) + got[rows, :].astype(f32)).astype(bf16)


def axes_orders(*orders):
    masks, m = [], 1
    while m < lax.axis_size("seq"):
        masks.append(m)
        m *= 2
    return list(zip(*[[masks[i] for i in o] + masks[4:] for o in orders]))


class SeqSum:
    def __init__(self, pairs, masks):
        self.masks, self.at = masks, 0
        rows = sum(a.shape[0] for a, _ in pairs) // 2
        shape = ((rows, pairs[0][0].shape[1]), bf16)
        flat = tuple(v for p in pairs for v in p)

        def kernel(refs, mine, other):
            first_halves_kernel(masks[0], [(refs[i], refs[i + 1]) for i in range(0, len(refs), 2)], mine, other)

        self.mine, self.send = run(kernel, [shape, shape], (flat,))

    def step(self):
        count, i = len(self.masks), self.at
        self.at += 1
        if i + 1 < count:
            got = partners(self.send, self.masks[i])
            if i + 2 < count:
                shape = ((got.shape[0] // 2, got.shape[1]), bf16)
                self.mine, self.send = run(functools.partial(next_halves_kernel, self.masks[i + 1]), [shape, shape], (self.mine, got))
            else:
                self.send = (self.mine.astype(f32) + got.astype(f32)).astype(bf16)
            return False
        if i + 1 == count:
            self.send = (self.send.astype(f32) + partners(self.send, self.masks[i]).astype(f32)).astype(bf16)
            return False
        mask = self.masks[2 * count - 2 - i]
        got = partners(self.send, mask)
        if i + 2 == 2 * count:
            self.result = (self.send, got)
            return True
        bit = bit_of(mask)
        self.send = jnp.concatenate([jnp.where(bit == 0, self.send, got), jnp.where(bit == 0, got, self.send)], axis=0)
        return False

    def after(self, values):
        self.send = tie(self.send, values)[0]

    def before(self, value):
        value, self.send = tie(value, self.send)
        return value


def unpack_kernel(masks0, masks1, mine0, got0, mine1, got1, lin, gate, out, entry):
    for k, mine, got, masks in ((0, mine0, got0, masks0), (1, mine1, got1, masks1)):
        bit = bit_of(masks)
        for ref, which in ((mine, bit), (got, 1 - bit)):

            def piece(at, rows):
                return ref[at : at + rows, :].astype(f32)

            def put_entry(at, start, rows):
                value = piece(at, rows)
                entry[k, pl.ds(2 * start, rows, stride=2), :] = value[:, :128]
                entry[k, pl.ds(2 * start + 1, rows, stride=2), :] = value[:, 128:]

            @pl.when(which == 0)
            def _():
                lin[k] = piece(0, 512)
                if k == 1:
                    gate[1] = piece(512, 512)
                else:
                    gate[0, :256] = piece(512, 256)
                    put_entry(768, 0, 256)

            @pl.when(which == 1)
            def _():
                if k == 1:
                    out[1, :, :256], out[1, :, 256:] = piece(0, 256), piece(256, 256)
                    put_entry(512, 0, 512)
                else:
                    gate[0, 256:] = piece(0, 256)
                    put_entry(768, 256, 256)
                    out[0, :, :256], out[0, :, 256:] = piece(256, 256), piece(512, 256)


class Far:
    def __init__(self, value, at=None, smem=False):
        self.value, self.at, self.smem = value, at, smem
        self.shape = value.shape if at is None else value.shape[1:] if at != "rows" else (2,) + value.shape[1:]

    def source(self, ref):
        if self.at is None:
            return ref
        return ref.at[pl.ds(lax.axis_index("state") * 2, 2)] if self.at == "rows" else ref.at[self.at]


class Held:
    def __init__(self, source, ref, sem):
        self.ref, self.copy, self.shape, self.dtype = ref, pltpu.make_async_copy(source, ref, sem), ref.shape, ref.dtype
        self.copy.start()

    def ready(self):
        if self.copy is not None:
            self.copy.wait()
            self.copy = None

    def __getitem__(self, index):
        self.ready()
        return self.ref[index]


def run(kernel, outs, groups, scratch=(), limit=24, flops=0):
    args = [a for g in groups for a in (g if isinstance(g, tuple) else (g,))]
    far_in = [i for i, a in enumerate(args) if isinstance(a, Far)]
    moved = sum(a.value.size * a.value.dtype.itemsize if isinstance(a, Far) else a.size * a.dtype.itemsize for a in args)

    def whole(*refs):
        ins, results = list(refs[: len(args)]), list(refs[len(args) : len(args) + len(outs)])
        rest = refs[len(args) + len(outs) :]
        own = rest[: len(scratch)]
        if far_in:
            buffers, sem = rest[len(scratch) : -1], rest[-1]
        for j, i in enumerate(far_in):
            ins[i] = Held(args[i].source(ins[i]), buffers[j], sem.at[j])
        grouped, at = [], 0
        for g in groups:
            if isinstance(g, tuple):
                grouped.append(tuple(ins[at : at + len(g)]))
                at += len(g)
            else:
                grouped.append(ins[at])
                at += 1
        kernel(*grouped, *results, *own)
        for i in far_in:
            ins[i].ready()

    def space(far):
        return pl.BlockSpec(memory_space=pltpu.HBM if far else pltpu.VMEM)

    held = [(pltpu.SMEM if args[i].smem else pltpu.VMEM)(args[i].shape, args[i].value.dtype) for i in far_in]
    if held:
        held.append(pltpu.SemaphoreType.DMA((len(held),)))
    return pl.pallas_call(
        whole,
        out_shape=[jax.ShapeDtypeStruct(o[0], o[1]) for o in outs],
        in_specs=[space(isinstance(a, Far)) for a in args],
        out_specs=[space(False)] * len(outs),
        scratch_shapes=[pltpu.VMEM(*s) for s in scratch] + held,
        compiler_params=pltpu.CompilerParams(vmem_limit_bytes=limit * 2**20),
        cost_estimate=pl.CostEstimate(flops=flops, bytes_accessed=moved, transcendentals=0),
    )(*[a.value if isinstance(a, Far) else a for a in args])


def body(tokens, gain, bias, in_proj, out_proj, rate_log, angle_log, skip, glu_lin, glu_gate, positions, cotangent):
    peers = lax.axis_size("seq")
    core = lax.axis_index("state")
    rows, span, width = tokens.shape
    steps = span // CHUNKS
    n = 2 * span
    count = float(rows * span * peers)
    packed = ((8, 128), f32)
    one = 2 * n * 512 * 512
    low = ((n, 512), bf16)
    full = ((n, 512), f32)

    (stats,) = run(stats_kernel, [((2 * peers, 4, 128), f32)], (Far(tokens),))
    raw, at = 0.0, 0
    for v in (gain, bias, skip, rate_log, angle_log):
        raw, at = raw + jnp.pad(v.astype(f32), ((0, 0), (at, 1024 - at - v.shape[1]))), at + v.shape[1]
    w_in = in_proj.reshape(2, 512, 256)
    w_out = out_proj.reshape(2, 256, 512)
    x_oth, cot_oth, in_oth, out_oth, lin_oth, gate_oth = (swap(w) for w in (tokens, cotangent, w_in, w_out, glu_lin, glu_gate))
    enter = [(Far(w_in, k), Far(in_oth, k)) for k in range(2)]
    own, keep, dk, perm = run(
        functools.partial(prep_kernel, peers, steps, span),
        [((32, 128), f32), ((2, n, 128), f32), ((2, peers, 8, 128), f32), ((2, n, n), bf16)],
        (Far(positions, smem=True), raw))
    oth = swap(own)
    ordered = ((peers, 8, 128), f32)

    for_seq, for_all = ((peers, 8, 128), f32), ((2 * peers, 8, 128), f32)
    scan_outs = [full, ((16, 8, 128), f32), for_seq, ((8, 512), f32)]
    xp, nl0, proj, comp, summ, nrm0 = run(
        functools.partial(enter_first_kernel, peers, steps, count), [low, low] + scan_outs,
        (lax.all_to_all(stats, ("seq", "state"), 0, 0), Far(tokens, "rows"), Far(x_oth, "rows"), perm, own, oth, keep) + enter[0], [packed], flops=2 * one)
    got, (cot_oth, out_oth, lin_oth, gate_oth) = blocking(summ, "seq", (cot_oth, out_oth, lin_oth, gate_oth))
    glu = [tuple(Far(w, k) for w in (w_out, out_oth, glu_lin, lin_oth, glu_gate, gate_oth)) for k in range(2)]
    cin0, sl0, gp0, act0, sig0, qv0, y0, stats = run(
        functools.partial(leave_first_kernel, peers, steps),
        [((SLAB, 512), f32), low, low, low, low, low, full, for_all],
        (got, comp, dk, own, oth, keep, proj, xp, nrm0) + glu[0], [packed, ordered], flops=3 * one)
    got, _ = blocking(stats, ("seq", "state"), ())
    nl1, proj, comp, summ, nrm1 = run(
        functools.partial(enter_second_kernel, peers, steps, count), [low] + scan_outs,
        (got, y0, own, oth, keep) + enter[1], [packed], flops=one)
    got, _ = blocking(summ, "seq", ())
    turn_outs = [((8, 512), f32), full, ((16, 8, 128), f32)]
    cin1, bo_own, bo_oth, d_out1, act1, dl1, dg1, sl1, dml1, skip1, dst, comp, summ = run(
        functools.partial(turn_kernel, peers, steps),
        [((SLAB, 512), f32), ((n, 256), bf16), ((n, 256), bf16), low, low, low, low, low, low] + turn_outs + [for_seq],
        (got, comp, dk, own, oth, keep, proj, y0, nrm1) + glu[1] + (perm, Far(cotangent, "rows"), Far(cot_oth, "rows")),
        [packed, ordered, full, full, full, full], flops=8 * one)
    got, (bo_oth,) = blocking(summ, "seq", (bo_oth,))
    g1_own, g1_oth, s1_own, s1_oth, dn, stats = run(
        functools.partial(adjoint_second_kernel, peers, steps),
        [((2048, 256), f32), ((2048, 256), bf16), ((16, 128), f32), ((16, 128), f32), full, for_all],
        (got, comp, dk, own, oth, keep, nl1, y0, nrm1, cin1, sl1, dst, dml1) + enter[1] + (skip1, act1, dl1, dg1),
        [packed, ordered, full, low], flops=6 * one)
    got, (bo_oth, g1_oth) = blocking(stats, ("seq", "state"), (bo_oth, g1_oth))
    bo_got, g1_got = swap(bo_oth), swap(g1_oth)
    d_out0, dml0, g0_own, g0_oth, skip0, dst, comp, summ = run(
        functools.partial(back_first_kernel, steps, count),
        [full, low, ((1536, 256), f32), ((1536, 256), bf16)] + turn_outs + [for_seq],
        (got, dn, y0, nrm1, d_out1, own, oth, keep, xp, nrm0, gp0, sig0, qv0) + glu[0] + (act0, sl0),
        [packed, low, low], flops=6 * one)
    got, (g0_oth, bo_got, g1_got) = blocking(summ, "seq", (g0_oth, bo_got, g1_got))
    bulk1 = SeqSum([(g1_own, g1_got)], axes_orders((0, 1, 2, 3), (1, 0, 2, 3)))
    got = (bulk1.before(got[0]),)
    g0_got = swap(g0_oth)
    i0_own, i0_oth, s_own, s_oth, a_own, a_oth = run(
        functools.partial(adjoint_first_kernel, peers, steps),
        [((512, 256), f32), ((512, 256), bf16), ((32, 128), f32), ((32, 128), f32), ((n, 256), bf16), ((n, 256), bf16)],
        (got, comp, dk, own, oth, keep, nl0, xp, nrm0, cin0, sl0, dst, dml0) + enter[0]
        + (skip0, d_out0, perm, s1_own, s1_oth),
        [packed, ordered, full, low, low], flops=4 * one)
    i0_got = swap(i0_oth)
    bulk0 = SeqSum([(g0_own, g0_got), (i0_own, i0_got)], axes_orders((2, 0, 1, 3), (2, 1, 0, 3)))
    s_got, a_got = swap(s_oth), swap(a_oth)
    s_all = jnp.broadcast_to((s_own + s_got)[None], (peers, 32, 128))
    got = lax.all_to_all(s_all, "seq", 0, 0)
    pair = (2, span, width)
    d_in, ngg, bias_grad, skip_grad, rate_grad, angle_grad = run(
        functools.partial(finish_kernel, count),
        [((rows, span, width), f32), ((2, 256), f32), ((2, 256), f32), ((2, 256), f32), ((2, 128), f32), ((2, 128), f32)],
        ((got,), a_own.reshape(pair), a_got.reshape(pair), Far(tokens), nrm0, raw),
        [((32, 128), f32)])
    while not bulk1.step():
        pass
    bulk0.step()
    bulk0.after(s_all)
    bulk0.step()
    bulk0.after(got)
    bulk0.step()
    bulk0.after(d_in)
    while not bulk0.step():
        pass
    lin_grad, gate_grad, out_grad, in_grad = run(
        functools.partial(unpack_kernel, bulk0.masks[0], bulk1.masks[0]),
        [((2, 512, 256), f32), ((2, 512, 256), f32), ((2, 256, 512), f32), ((2, 1024, 128), f32)],
        bulk0.result + bulk1.result)
    out_grad, in_grad = out_grad.reshape(2, 2, 128, 512), in_grad.reshape(2, 512, 2, 128)
    mine, other = bo_own.reshape(pair), bo_got.reshape(pair)
    block_out = jnp.concatenate([jnp.where(core == 0, mine, other), jnp.where(core == 0, other, mine)], axis=0)
    return (block_out, d_in, ngg, bias_grad, in_grad, out_grad, rate_grad, angle_grad, skip_grad, lin_grad, gate_grad)


def solution(mesh):
    placed = (
        P(None, "seq", "state"),
        P(None, "state"),
        P(None, "state"),
        P(None, None, None, "state"),
        P(None, None, "state", None),
        P(None, "state"),
        P(None, "state"),
        P(None, "state"),
        P(None, None, "state"),
        P(None, None, "state"),
        P(),
        P(None, "seq", "state"),
    )
    return jax.shard_map(
        body,
        mesh=mesh,
        in_specs=placed,
        out_specs=(
            P(None, "seq", "state"),
            P(None, "seq", "state"),
            P(None, "state"),
            P(None, "state"),
            P(None, None, None, "state"),
            P(None, None, "state", None),
            P(None, "state"),
            P(None, "state"),
            P(None, "state"),
            P(None, None, "state"),
            P(None, None, "state"),
        ),
        check_vma=False,
    )
```

```python
import functools

import jax
import jax.numpy as jnp
from jax import lax
from jax.experimental import pallas as pl
from jax.experimental.pallas import tpu as pltpu
from jax.sharding import PartitionSpec as P

f32, bf16 = jnp.float32, jnp.bfloat16
norm_eps = 1e-05
CHUNKS = 8
SLAB = 2 * CHUNKS
TILE = 256


def mm(a, b):
    return jnp.dot(a, b, preferred_element_type=f32)


def mm_nt(a, b):
    return lax.dot_general(a, b, (((1,), (1,)), ((), ())), preferred_element_type=f32)


def mm_tn(a, b):
    return lax.dot_general(a, b, (((0,), (0,)), ((), ())), preferred_element_type=f32)


def wide(row):
    return jnp.broadcast_to(row, (CHUNKS, 128))


def cmul(ar, ai, br, bi):
    return ar * br - ai * bi, ar * bi + ai * br


def row_of_tiles(tiles):
    return jnp.concatenate([tiles[i : i + 1, :] for i in range(tiles.shape[0])], axis=1)


def channel_row(core, own, oth, at):
    mine, other = own[at : at + 2, :], oth[at : at + 2, :]
    low = jnp.where(core == 0, mine, other)
    high = jnp.where(core == 0, other, mine)
    return jnp.concatenate([low[0:1], low[1:2], high[0:1], high[1:2]], axis=1)


def own_cols(core, width):
    return pl.ds(pl.multiple_of(core * width, width), width)


def oth_cols(core, width):
    return pl.ds(pl.multiple_of((1 - core) * width, width), width)


def scan(drive, lams, keep_ref, which, steps, reverse, start, visit):
    order = range(steps - 1, -1, -1) if reverse else range(steps)
    state = dict(start)
    for s in order:
        for row in range(2):
            at = s * SLAB + row * CHUNKS
            keep = keep_ref[which, at : at + CHUNKS, :]
            for half in range(2):
                lr, li = lams[half]
                hr, hi = state[half, row]
                hr, hi = keep * hr, keep * hi
                dr, di = drive(s, row, half)
                state[half, row] = (lr * hr - li * hi + dr, lr * hi + li * hr + di)
        visit(s, state, keep_ref)
    return state


def keep_products(keep_ref, which, steps):
    out = []
    for row in range(2):
        total = keep_ref[which, row * CHUNKS : (row + 1) * CHUNKS, :]
        for s in range(1, steps):
            at = s * SLAB + row * CHUNKS
            total = total * keep_ref[which, at : at + CHUNKS, :]
        out.append(total)
    return out


def chunk_scan(ends, keeps, powers, reverse, comp_ref, packed):
    index = lax.broadcasted_iota(jnp.int32, (CHUNKS, 128), 0)

    def shifted(value, by, fill):
        turned = pltpu.roll(value, CHUNKS - by if reverse else by, 0)
        valid = index < CHUNKS - by if reverse else index >= by
        return jnp.where(valid, turned, fill)

    for half in range(2):
        for row in range(2):
            er, ei = ends[half, row]
            pr, pi = powers[half][0] * keeps[row], powers[half][1] * keeps[row]
            for by in (1, 2, 4):
                tr, ti = cmul(pr, pi, shifted(er, by, 0.0), shifted(ei, by, 0.0))
                er, ei = er + tr, ei + ti
                pr, pi = cmul(pr, pi, shifted(pr, by, 1.0), shifted(pi, by, 0.0))
            edge = 0 if reverse else CHUNKS - 1
            q = row * 2 + half
            packed[q : q + 1, :] = er[edge : edge + 1, :]
            packed[4 + q : 5 + q, :] = ei[edge : edge + 1, :]
            base = (half * 2 + row) * 4
            comp_ref[base] = shifted(er, 1, 0.0)
            comp_ref[base + 1] = shifted(ei, 1, 0.0)
            comp_ref[base + 2] = shifted(pr, 1, 1.0)
            comp_ref[base + 3] = shifted(pi, 1, 0.0)


def device_carry(me, peers, got, held, dk_ref, which, own, oth, base, conj, reverse, packed):
    got_ref = arrange(got, held)
    index = lax.broadcasted_iota(jnp.int32, (CHUNKS, 128), 0)
    is_own = index % 2 == 0
    sign = jnp.where(index < 4, -1.0, 1.0) * (-1.0 if conj else 1.0)
    ar = jnp.where(is_own, wide(own[base + 11 : base + 12, :]), wide(oth[base + 11 : base + 12, :]))
    ai = jnp.where(is_own, wide(own[base + 12 : base + 13, :]), wide(oth[base + 12 : base + 13, :]))
    ai = ai * sign

    def step(k, held):
        at = peers - 1 - k if reverse else k
        reached = at > me if reverse else at < me
        new = dk_ref[which, at] * (ar * held + ai * pltpu.roll(held, 4, 0)) + got_ref[at]
        return jnp.where(reached, new, held)

    packed[...] = lax.fori_loop(0, peers, step, jnp.zeros((8, 128), f32), unroll=peers <= 16)


def entries(comp_ref, packed):
    start = {}
    for half in range(2):
        for row in range(2):
            base, q = (half * 2 + row) * 4, row * 2 + half
            hr, hi = wide(packed[q : q + 1, :]), wide(packed[4 + q : 5 + q, :])
            tr, ti = cmul(comp_ref[base + 2], comp_ref[base + 3], hr, hi)
            start[half, row] = (comp_ref[base] + tr, comp_ref[base + 1] + ti)
    return start


def decay(own, oth, base, at, conj=False):
    sign = -1.0 if conj else 1.0
    return [(wide(r[base + at : base + at + 1, :]), sign * wide(r[base + at + 1 : base + at + 2, :])) for r in (own, oth)]


def scales(own, oth, base):
    return [wide(r[base + 8 : base + 9, :]) for r in (own, oth)]


def nothing(*_):
    return None


def zeros_start():
    zero = jnp.zeros((CHUNKS, 128), f32)
    return {(half, row): (zero, zero) for half in range(2) for row in range(2)}


def part(s, row):
    at = s * SLAB + row * CHUNKS
    return slice(at, at + CHUNKS)


def cols(half, im):
    at = half * 256 + im * 128
    return slice(at, at + 128)


def flat_rows(ref):
    value = ref[...]
    return value.reshape(value.shape[0] * value.shape[1], value.shape[2])


def spread(out_ref, packed):
    value = packed[...]
    out_ref[...] = value if len(out_ref.shape) == 2 else jnp.broadcast_to(value[None], out_ref.shape)


def arrange(got, held):
    if len(got) == 1:
        return got[0]
    me = place()[0]
    for m, block in enumerate(got):
        for e in range(4):
            held[(((me >> 2) ^ m) << 2) + ((me & 3) ^ e)] = block[e]
    return held


def place():
    return lax.axis_index("seq"), lax.axis_index("state")


def stats_kernel(tokens, stats):
    s1 = s2 = 0.0
    for r in range(tokens.shape[0]):
        x = tokens[r].astype(f32)
        s1 = s1 + jnp.sum(x, axis=0, keepdims=True)
        s2 = s2 + jnp.sum(x * x, axis=0, keepdims=True)
    for i in range(2):
        stats[0, i : i + 1, :] = s1[:, 128 * i : 128 * (i + 1)]
        stats[0, 2 + i : 3 + i, :] = s2[:, 128 * i : 128 * (i + 1)]
    stats[...] = jnp.broadcast_to(stats[0][None], stats.shape)


def prep_kernel(peers, steps, span, pos, raw, small, keep, dk, perm):
    seq, core = place()
    docs = pos.shape[1]

    count = perm.shape[1]
    p = lax.broadcasted_iota(jnp.int32, (count, count), 0)
    q = lax.broadcasted_iota(jnp.int32, (count, count), 1)
    source = ((p >> 3) & 1) * span + (p & 7) * steps + (p >> 4)
    perm[0] = jnp.where(q == source, 1.0, 0.0).astype(bf16)
    source = ((q >> 3) & 1) * span + (q & 7) * steps + (q >> 4)
    perm[1] = jnp.where(p == source, 1.0, 0.0).astype(bf16)

    small[...] = jnp.zeros_like(small)
    for k in range(2):
        at = 16 * k
        values = raw[k : k + 1, :]
        for j in range(6):
            small[at + j : at + j + 1, :] = values[:, 128 * j : 128 * (j + 1)]
        rate = jnp.exp(values[:, 768:896])
        angle = jnp.exp(values[:, 896:])
        modulus = jnp.exp(-rate)
        lr, li = modulus * jnp.cos(angle), modulus * jnp.sin(angle)
        small[at + 6 : at + 7, :] = lr
        small[at + 7 : at + 8, :] = li
        small[at + 8 : at + 9, :] = jnp.sqrt(1.0 - modulus * modulus)
        power = 1
        while power < span:
            lr, li = cmul(lr, li, lr, li)
            power *= 2
            if power == steps:
                small[at + 9 : at + 10, :] = lr
                small[at + 10 : at + 11, :] = li
        small[at + 11 : at + 12, :] = lr
        small[at + 12 : at + 13, :] = li

    chunk = lax.broadcasted_iota(jnp.int32, (CHUNKS, 128), 0) * steps + seq * span
    for row in range(2):
        targets = [pos[core * 2 + row, d] - chunk for d in range(docs)]
        for s in range(steps + 1):
            hit = targets[0] == s
            for t in targets[1:]:
                hit = jnp.logical_or(hit, t == s)
            value = jnp.where(hit, 0.0, 1.0)
            at = s * SLAB + row * CHUNKS
            if s < steps:
                keep[0, at : at + CHUNKS, :] = value
            if s >= 1:
                keep[1, at - SLAB : at - SLAB + CHUNKS, :] = value

    first_row = (lax.broadcasted_iota(jnp.int32, (CHUNKS, 128), 0) // 2) % 2 == 0
    owners = ([], [])
    for d in range(docs):
        a, b = pos[core * 2, d], pos[core * 2 + 1, d]
        owners[0].append(jnp.where(first_row, a // span, b // span))
        owners[1].append(jnp.where(first_row, (a + span - 1) // span - 1, (b + span - 1) // span - 1))

    def mark(j, _):
        for m in range(2):
            hit = owners[m][0] == j
            for o in owners[m][1:]:
                hit = jnp.logical_or(hit, o == j)
            dk[m, j] = jnp.where(hit, 0.0, 1.0)
        return 0

    lax.fori_loop(0, peers, mark, 0)


def norm_rows(total, squares, count, core, own, oth, base, nrm):
    mean = total / count
    inv = lax.rsqrt(squares / count - mean * mean + norm_eps)
    nrm[0:1, :] = mean
    nrm[1:2, :] = inv
    nrm[2:3, :] = channel_row(core, own, oth, base)
    nrm[3:4, :] = channel_row(core, own, oth, base + 2)
    nrm[4:5, :] = channel_row(core, own, oth, base + 4)
    nrm[5:8, :] = jnp.zeros_like(nrm[5:8, :])


def normalized(x, nrm):
    xhat = (x - nrm[0:1, :]) * nrm[1:2, :]
    return xhat, xhat * nrm[2:3, :] + nrm[3:4, :]


def project_and_scan(steps, base, which, reverse, own, oth, keep, win_own, win_oth, nl, proj, comp, summ, packed):
    proj[:, :256] = mm(nl[...], win_own[...])
    proj[:, 256:] = mm(nl[...], win_oth[...])
    lams, sc = decay(own, oth, base, 6), scales(own, oth, base)

    def drive(s, row, half):
        return sc[half] * proj[part(s, row), cols(half, 0)], sc[half] * proj[part(s, row), cols(half, 1)]

    ends = scan(drive, lams, keep, which, steps, reverse, zeros_start(), nothing)
    chunk_scan(ends, keep_products(keep, which, steps), decay(own, oth, base, 9), reverse, comp, packed)
    spread(summ, packed)


def enter_first_kernel(peers, steps, count, got, x_own, x_oth, perm, own, oth, keep, win_own, win_oth,
                       xp, nl, proj, comp, summ, nrm, packed):
    _, core = place()
    sums = got[0:2]
    for j in range(1, peers):
        sums = sums + got[2 * j : 2 * j + 2]
    total = jnp.concatenate([sums[0, 0:1], sums[0, 1:2], sums[1, 0:1], sums[1, 1:2]], axis=1)
    squares = jnp.concatenate([sums[0, 2:3], sums[0, 3:4], sums[1, 2:3], sums[1, 3:4]], axis=1)
    norm_rows(total, squares, count, core, own, oth, 0, nrm)
    xp[:, own_cols(core, 256)] = mm(perm[0], flat_rows(x_own)).astype(bf16)
    xp[:, oth_cols(core, 256)] = mm(perm[0], flat_rows(x_oth)).astype(bf16)
    _, normed = normalized(xp[...].astype(f32), nrm)
    nl[...] = normed.astype(bf16)
    project_and_scan(steps, 0, 0, False, own, oth, keep, win_own, win_oth, nl, proj, comp, summ, packed)


def sum_peers(got):
    if len(got) == 1 and len(got[0].shape) == 3:
        got = [got[0].at[j] for j in range(got[0].shape[0])]
    total = got[0][...]
    for part in got[1:]:
        total = total + part[...]
    return total


def enter_second_kernel(peers, steps, count, got, x, own, oth, keep, win_own, win_oth,
                        nl, proj, comp, summ, nrm, packed):
    _, core = place()
    sums = sum_peers(got)
    norm_rows(row_of_tiles(sums[0:4]), row_of_tiles(sums[4:8]), count, core, own, oth, 16, nrm)
    _, normed = normalized(x[...], nrm)
    nl[...] = normed.astype(bf16)
    project_and_scan(steps, 16, 1, True, own, oth, keep, win_own, win_oth, nl, proj, comp, summ, packed)


def states_of(peers, steps, base, which, reverse, got, comp, dk, own, oth, keep, proj, cin, sl, packed, held):
    device_carry(place()[0], peers, got, held, dk, which, own, oth, base, False, reverse, packed)
    start = entries(comp, packed)
    lams, sc = decay(own, oth, base, 6), scales(own, oth, base)
    for (half, row), (hr, hi) in start.items():
        cin[part(0, row), cols(half, 0)] = hr
        cin[part(0, row), cols(half, 1)] = hi

    def drive(s, row, half):
        return sc[half] * proj[part(s, row), cols(half, 0)], sc[half] * proj[part(s, row), cols(half, 1)]

    def visit(s, state, _):
        for half in range(2):
            for im in range(2):
                both = jnp.concatenate([state[half, row][im] for row in range(2)], axis=0)
                sl[s * SLAB : (s + 1) * SLAB, cols(half, im)] = both.astype(bf16)

    scan(drive, lams, keep, which, steps, reverse, start, visit)


def mix_and_gate(core, x, nrm, sl, wout_own, wout_oth, lin_own, lin_oth, gate_own, gate_oth, gp, act, sig, qv, y):
    c = 0.7978845608028654
    for i in range(0, y.shape[0], TILE):
        rows = slice(i, i + TILE)
        _, normed = normalized(x[rows, :].astype(f32), nrm)
        mixed = mm(sl[rows, :256], wout_own[...]) + mm(sl[rows, 256:], wout_oth[...]) + nrm[4:5, :] * normed
        sq = mixed * mixed
        t = jnp.tanh(mixed * (c + (c * 0.044715) * sq))
        upper = 0.5 + 0.5 * t
        low = (mixed * upper).astype(bf16)
        act[rows, :] = low
        gp[rows, :] = (upper + mixed * (upper * (1.0 - t)) * (c + (3 * c * 0.044715) * sq)).astype(gp.dtype)
        for w_lin, w_gate, at in ((lin_own, gate_own, own_cols(core, 256)), (lin_oth, gate_oth, oth_cols(core, 256))):
            linear = mm(low, w_lin[...])
            gating = mm(low, w_gate[...])
            sg = 0.5 + 0.5 * jnp.tanh(0.5 * gating)
            out = linear * sg
            sig[rows, at] = sg.astype(sig.dtype)
            qv[rows, at] = (out * (1.0 - sg)).astype(qv.dtype)
            y[rows, at] = x[rows, at].astype(f32) + out
        yield rows


def leave_first_kernel(peers, steps, got, comp, dk, own, oth, keep, proj, x, nrm, wout_own, wout_oth,
                       lin_own, lin_oth, gate_own, gate_oth, cin, sl, gp, act, sig, qv, y, stats, packed, held):
    states_of(peers, steps, 0, 0, False, got, comp, dk, own, oth, keep, proj, cin, sl, packed, held)
    s1 = s2 = 0.0
    for rows in mix_and_gate(place()[1], x, nrm, sl, wout_own, wout_oth, lin_own, lin_oth, gate_own, gate_oth, gp, act, sig, qv, y):
        out = y[rows, :]
        s1, s2 = s1 + jnp.sum(out, axis=0, keepdims=True), s2 + jnp.sum(out * out, axis=0, keepdims=True)
    pack_two(s1, s2, packed)
    spread(stats, packed)


def pack_two(a, b, packed):
    for i in range(4):
        packed[i : i + 1, :] = a[:, 128 * i : 128 * (i + 1)]
        packed[4 + i : 5 + i, :] = b[:, 128 * i : 128 * (i + 1)]


def glu_backward(steps, base, adj_which, adj_reverse, core, d_out, nrm, x, gp, sig, qv, own, oth, keep, wout_own, wout_oth,
                 lin_own, lin_oth, gate_own, gate_oth, skip_row, dst, comp, summ, packed, dl, dg, dml):
    mine, other = own_cols(core, 256), oth_cols(core, 256)
    total = 0.0
    for i in range(0, dl.shape[0], TILE):
        rows = slice(i, i + TILE)
        grad = d_out(rows)
        dl[rows, :] = (grad * sig[rows, :].astype(f32)).astype(bf16)
        dg[rows, :] = (grad * qv[rows, :].astype(f32)).astype(bf16)
        d_active = (mm_nt(dl[rows, mine], lin_own[...]) + mm_nt(dg[rows, mine], gate_own[...])
                    + mm_nt(dl[rows, other], lin_oth[...]) + mm_nt(dg[rows, other], gate_oth[...]))
        d_mixed = d_active * gp[rows, :].astype(f32)
        _, normed = normalized(x[rows, :].astype(f32), nrm)
        total = total + jnp.sum(d_mixed * normed, axis=0, keepdims=True)
        low = d_mixed.astype(bf16)
        dml[rows, :] = low
        dst[rows, :256] = mm_nt(low, wout_own[...])
        dst[rows, 256:] = mm_nt(low, wout_oth[...])
    skip_row[0:1, :] = total
    lams = decay(own, oth, base, 6, conj=True)

    def drive(s, row, half):
        return dst[part(s, row), cols(half, 0)], dst[part(s, row), cols(half, 1)]

    ends = scan(drive, lams, keep, adj_which, steps, adj_reverse, zeros_start(), nothing)
    chunk_scan(ends, keep_products(keep, adj_which, steps), decay(own, oth, base, 9, conj=True), adj_reverse, comp, packed)
    spread(summ, packed)


def mixer_grads(act, dl, dg, sl, dml, l_own, l_oth, g_own, g_oth):
    _, core = place()
    mine, other = own_cols(core, 256), oth_cols(core, 256)
    left = act[...].T
    l_own[...] = mm(left, dl[:, mine])
    l_oth[...] = mm(left, dl[:, other]).astype(bf16)
    g_own[0:512, :] = mm(left, dg[:, mine])
    g_oth[0:512, :] = mm(left, dg[:, other]).astype(bf16)
    for ref, cut in ((g_own, slice(0, 256)), (g_oth, slice(256, 512))):
        left = sl[:, cut].T
        for i in range(2):
            ref[512 + 256 * i : 768 + 256 * i, :] = mm(left, dml[:, 256 * i : 256 * (i + 1)]).astype(ref.dtype)


def in_grads(nl, dp, g_own, g_oth):
    left = nl[...].T
    g_own[...] = mm(left, dp[:, :256])
    g_oth[...] = mm(left, dp[:, 256:]).astype(bf16)


def turn_kernel(peers, steps, got, comp_in, dk, own, oth, keep, proj, x, nrm, wout_own, wout_oth,
                lin_own, lin_oth, gate_own, gate_oth, perm, cot_own, cot_oth,
                cin, result, d_out, act, dl, dg, sl, dml, skip_row, dst, comp, summ,
                packed, held, gp, sig, qv, y):
    _, core = place()
    states_of(peers, steps, 16, 1, True, got, comp_in, dk, own, oth, keep, proj, cin, sl, packed, held)
    for _ in mix_and_gate(core, x, nrm, sl, wout_own, wout_oth, lin_own, lin_oth, gate_own, gate_oth, gp, act, sig, qv, y):
        pass
    result[...] = y[...].astype(bf16)
    d_out[:, own_cols(core, 256)] = mm(perm[0], flat_rows(cot_own)).astype(bf16)
    d_out[:, oth_cols(core, 256)] = mm(perm[0], flat_rows(cot_oth)).astype(bf16)
    glu_backward(steps, 16, 0, False, core, lambda rows: d_out[rows, :].astype(f32), nrm, x, gp, sig, qv, own, oth, keep, wout_own, wout_oth,
                 lin_own, lin_oth, gate_own, gate_oth, skip_row, dst, comp, summ, packed, dl, dg, dml)


def adjoint_part(peers, steps, base, keep_which, adj_which, adj_reverse, got, comp, dk, own, oth, keep, nl, x, nrm,
                 cin, sl, dst, dml, win_own, win_oth, skip_row, small_own, small_oth, all_rows, packed, held, proj, dp, keep_tile):
    _, core = place()
    device_carry(place()[0], peers, got, held, dk, adj_which, own, oth, base, True, adj_reverse, packed)
    start = entries(comp, packed)
    lams, sc = decay(own, oth, base, 6, conj=True), scales(own, oth, base)
    zero = jnp.zeros((CHUNKS, 128), f32)
    acc = {half: [zero, zero, zero] for half in range(2)}
    proj[:, :256] = mm(nl[...], win_own[...])
    proj[:, 256:] = mm(nl[...], win_oth[...])

    def prior(s, half, im):
        before = s - 1 if adj_reverse else s + 1
        if 0 <= before < steps:
            return sl[before * SLAB : (before + 1) * SLAB, cols(half, im)].astype(f32)
        return cin[:, cols(half, im)]

    def drive(s, row, half):
        return dst[part(s, row), cols(half, 0)], dst[part(s, row), cols(half, 1)]

    def visit(s, state, _):
        for half in range(2):
            prior_re, prior_im = prior(s, half, 0), prior(s, half, 1)
            for row in range(2):
                ar, ai = state[half, row]
                pr, pi = prior_re[part(0, row)], prior_im[part(0, row)]
                keep_here = keep[keep_which, part(s, row), :]
                acc[half][0] = acc[half][0] + keep_here * (ar * pr + ai * pi)
                acc[half][1] = acc[half][1] + keep_here * (ai * pr - ar * pi)
                acc[half][2] = acc[half][2] + (ar * proj[part(s, row), cols(half, 0)] + ai * proj[part(s, row), cols(half, 1)])
            for im in range(2):
                both = jnp.concatenate([sc[half] * state[half, row][im] for row in range(2)], axis=0)
                dp[s * SLAB : (s + 1) * SLAB, cols(half, im)] = both.astype(bf16)

    scan(drive, lams, keep, adj_which, steps, adj_reverse, start, visit)

    bias_row = gain_row = 0.0
    for i in range(0, dp.shape[0], TILE):
        rows = slice(i, i + TILE)
        d_normed = dml[rows, :].astype(f32) * nrm[4:5, :] + mm_nt(dp[rows, :256], win_own[...]) + mm_nt(dp[rows, 256:], win_oth[...])
        xhat, _ = normalized(x[rows, :].astype(f32), nrm)
        bias_row = bias_row + jnp.sum(d_normed, axis=0, keepdims=True)
        gain_row = gain_row + jnp.sum(d_normed * xhat, axis=0, keepdims=True)
        keep_tile(rows, d_normed)
    pack_two(bias_row, gain_row, packed)

    wanted = (skip_row[0:1, :], bias_row, gain_row) if all_rows else (skip_row[0:1, :],)
    for ref, half in ((small_own, 0), (small_oth, 1)):
        ref[...] = jnp.zeros_like(ref)
        at = 0
        for row in wanted:
            pick = jnp.where(core == half, row[:, :256], row[:, 256:])
            ref[at : at + 1, :] = pick[:, :128]
            ref[at + 1 : at + 2, :] = pick[:, 128:]
            at += 2
        for j in range(3):
            ref[at + j : at + j + 1, :] = jnp.sum(acc[half][j], axis=0, keepdims=True)


def adjoint_second_kernel(peers, steps, got, comp, dk, own, oth, keep, nl, x, nrm, cin, sl, dst, dml, win_own, win_oth, skip_row, act, dl, dg,
                          g_own, g_oth, small_own, small_oth, dn, stats, packed, held, proj, dp):
    def keep_tile(rows, d_normed):
        dn[rows, :] = d_normed

    adjoint_part(peers, steps, 16, 1, 0, False, got, comp, dk, own, oth, keep, nl, x, nrm,
                 cin, sl, dst, dml, win_own, win_oth, skip_row, small_own, small_oth, False, packed, held, proj, dp, keep_tile)
    spread(stats, packed)
    mixer_grads(act, dl, dg, sl, dml, g_own.at[:512], g_oth.at[:512], g_own.at[512:1536], g_oth.at[512:1536])
    in_grads(nl, dp, g_own.at[1536:], g_oth.at[1536:])


def back_first_kernel(steps, count, got, dn, x2, nrm2, d_out2, own, oth, keep, x, nrm, gp, sig, qv,
                      wout_own, wout_oth, lin_own, lin_oth, gate_own, gate_oth,
                      act, sl, d_out, dml, totals, l_own, l_oth, g_own, g_oth, skip_row, dst, comp, summ, packed, dl, dg):
    sums = sum_peers(got)
    bias_row, gain_row = row_of_tiles(sums[0:4]), row_of_tiles(sums[4:8])
    totals[...] = jnp.zeros_like(totals)
    totals[0:1, :], totals[1:2, :] = bias_row, gain_row
    mean, inv, gain = nrm2[0:1, :], nrm2[1:2, :], nrm2[2:3, :]
    scaled, shift, slope = inv * gain, inv * gain * bias_row / count, inv * inv * gain * gain_row / count

    def d_in(rows):
        value = d_out2[rows, :].astype(f32) + scaled * dn[rows, :] - shift - slope * (x2[rows, :] - mean)
        d_out[rows, :] = value
        return value

    glu_backward(steps, 0, 1, True, place()[1], d_in, nrm, x, gp, sig, qv, own, oth, keep, wout_own, wout_oth,
                 lin_own, lin_oth, gate_own, gate_oth, skip_row, dst, comp, summ, packed, dl, dg, dml)
    mixer_grads(act, dl, dg, sl, dml, l_own, l_oth, g_own, g_oth)


def adjoint_first_kernel(peers, steps, got, comp, dk, own, oth, keep, nl, x, nrm, cin, sl, dst, dml, win_own, win_oth, skip_row,
                         d_out, small1_own, small1_oth,
                         g_own, g_oth, small_own, partial, packed, held, proj, dp, small_oth):
    _, core = place()
    scaled = nrm[1:2, :] * nrm[2:3, :]

    def keep_tile(rows, d_normed):
        partial[rows, :] = (d_out[rows, :] + scaled * d_normed).astype(bf16)

    adjoint_part(peers, steps, 0, 0, 1, True, got, comp, dk, own, oth, keep, nl, x, nrm,
                 cin, sl, dst, dml, win_own, win_oth, skip_row, small_own, small_oth, True, packed, held, proj, dp, keep_tile)
    small_own[9:14, :] = small1_own[0:5, :]
    small_oth[9:14, :] = small1_oth[0:5, :]
    in_grads(nl, dp, g_own, g_oth.at[:512])
    put_small(g_oth, 512, small_oth[...])


def order_kernel(perm, result, partial, own, oth):
    _, core = place()
    for i, ref in enumerate((result, partial)):
        own[i] = mm(perm[1], ref[:, own_cols(core, 256)]).astype(bf16)
        oth[i] = mm(perm[1], ref[:, oth_cols(core, 256)]).astype(bf16)


def finish_kernel(count, packed, totals1, mine_parts, other_parts, tokens, nrm, raw,
                  block_out, d_in, ngg, bias, skip, rate_grad, angle_grad):
    _, core = place()
    for ref, j in ((skip, 0), (bias, 2), (ngg, 4)):
        ref[0:1, :128], ref[0:1, 128:] = packed[j : j + 1, :], packed[j + 1 : j + 2, :]
    skip[1:2, :128], skip[1:2, 128:] = packed[9:10, :], packed[10:11, :]
    bias[1:2, :] = totals1[0:1, own_cols(core, 256)]
    ngg[1:2, :] = totals1[1:2, own_cols(core, 256)]
    for k, at in ((0, 6), (1, 11)):
        values = raw[k : k + 1, :]
        rate = jnp.exp(values[:, 768:896])
        angle = jnp.exp(values[:, 896:])
        modulus = jnp.exp(-rate)
        scale = jnp.sqrt(1.0 - modulus * modulus)
        cos, sin = jnp.cos(angle), jnp.sin(angle)
        dr, di, ds = (packed[at + j : at + j + 1, :] for j in range(3))
        g_mod = dr * cos + di * sin - ds * modulus / scale
        rate_grad[k : k + 1, :] = -g_mod * modulus * rate
        angle_grad[k : k + 1, :] = modulus * (di * cos - dr * sin) * angle
    mine = nrm[:, own_cols(core, 256)]
    mean, inv, gain = mine[0:1, :], mine[1:2, :], mine[2:3, :]
    bias_row, gain_row = bias[0:1, :], ngg[0:1, :]
    flat = inv * gain / count
    for r in range(4):
        block_out[r] = jnp.where(core == r // 2, mine_parts[0, r % 2], other_parts[0, r % 2])
        held_rows = jnp.where(core == r // 2, mine_parts[1, r % 2].astype(f32), other_parts[1, r % 2].astype(f32))
        xhat = (tokens[r].astype(f32) - mean) * inv
        d_in[r] = held_rows - flat * (bias_row + xhat * gain_row)


def swap(value):
    return lax.ppermute(value, "state", [(0, 1), (1, 0)])


def to_all(value, axes):
    peers = 1
    for a in axes:
        peers *= lax.axis_size(a)
    return lax.all_to_all(jnp.broadcast_to(value[None], (peers,) + value.shape), axes, 0, 0)


def blocking(value, axes, others):
    value, others = lax.optimization_barrier((value, others))
    got, others = lax.optimization_barrier((lax.all_to_all(value, axes, 0, 0), others))
    return (got,), others


def gather_seq(value):
    if lax.axis_size("seq") != 16:
        return (to_all(value, ("seq",)),)
    near = jnp.stack([value] + [partner(value, m) for m in (1, 2, 3)])
    return (near,) + tuple(partner(near, m) for m in (4, 8, 12))


def sum_all(value):
    if lax.axis_size("seq") != 16:
        return (to_all(value, ("seq", "state")),)
    value = value + swap(value)
    near = value + partner(value, 1) + partner(value, 2) + partner(value, 3)
    return (near,) + tuple(partner(near, m) for m in (4, 8, 12))


def partner(value, mask):
    size = lax.axis_size("seq")
    return lax.ppermute(value, "seq", [(i, i ^ mask) for i in range(size)])


def partners(value, masks):
    size = lax.axis_size("seq")
    return lax.ppermute(value, ("seq", "state"), [(2 * i + c, 2 * (i ^ masks[c]) + c) for i in range(size) for c in range(2)])


def tie(value, others):
    return lax.optimization_barrier((value, others))


def bit_of(masks):
    me, core = place()
    return (me // jnp.where(core == 0, masks[0], masks[1])) & 1


def put_small(out, at, value):
    high = value.astype(bf16)
    rest = value - high.astype(f32)
    middle = rest.astype(bf16)
    low = (rest - middle.astype(f32)).astype(bf16)
    out[at : at + 16, :128], out[at : at + 16, 128:] = high, middle
    out[at + 16 : at + 32, :128], out[at + 16 : at + 32, 128:] = low, jnp.zeros_like(low)


def get_small(ref, at):
    return (ref[at : at + 16, :128].astype(f32) + ref[at : at + 16, 128:].astype(f32)) + ref[at + 16 : at + 32, :128].astype(f32)


def first_halves_kernel(masks, pairs, small, mine, other):
    bit, at = bit_of(masks), 0
    for own, got in pairs:
        half = own.shape[0] // 2
        for out, which in ((mine, bit), (other, 1 - bit)):
            rows = pl.ds(pl.multiple_of(which * half, half), half)
            out[at : at + half, :] = (own[rows, :] + got[rows, :].astype(f32)).astype(bf16)
        at += half
    if small is not None:
        total = small[...] + get_small(pairs[-1][1], pairs[-1][0].shape[0])
        put_small(mine, at, total)
        put_small(other, at, total)


def next_halves_kernel(masks, extra, held, got, mine, other):
    bit, half = bit_of(masks), mine.shape[0] - extra
    for out, which in ((mine, bit), (other, 1 - bit)):
        rows = pl.ds(pl.multiple_of(which * half, half), half)
        out[:half, :] = (held[rows, :].astype(f32) + got[rows, :].astype(f32)).astype(bf16)
    if extra:
        total = get_small(held, 2 * half) + get_small(got, 2 * half)
        put_small(mine, half, total)
        put_small(other, half, total)


def add_kernel(extra, held, got, total, *small):
    rows = held.shape[0] - extra
    total[:rows, :] = (held[:rows, :].astype(f32) + got[:rows, :].astype(f32)).astype(bf16)
    if extra:
        value = get_small(held, rows) + get_small(got, rows)
        if small:
            small[0][...] = value
        else:
            put_small(total, rows, value)


def axes_orders(*orders):
    masks, m = [], 1
    while m < lax.axis_size("seq"):
        masks.append(m)
        m *= 2
    return list(zip(*[[masks[i] for i in o] + masks[4:] for o in orders]))


class SeqSum:
    def __init__(self, pairs, masks, small=None):
        self.masks, self.at, self.small, self.extra = masks, 0, (), 0 if small is None else 32
        rows = sum(a.shape[0] for a, _ in pairs) // 2 + self.extra
        shape = ((rows, pairs[0][0].shape[1]), bf16)
        flat = tuple(v for p in pairs for v in p) + (() if small is None else (small,))

        def kernel(refs, mine, other):
            count = 2 * len(pairs)
            first_halves_kernel(masks[0], [(refs[i], refs[i + 1]) for i in range(0, count, 2)],
                                None if small is None else refs[count], mine, other)

        self.mine, self.send = run(kernel, [shape, shape], (flat,))

    def step(self):
        count, i = len(self.masks), self.at
        self.at += 1
        if i < count:
            got = partners(self.send, self.masks[i])
            rows, width = got.shape
            rows -= self.extra
            if i + 2 < count:
                shape = ((rows // 2 + self.extra, width), bf16)
                self.mine, self.send = run(functools.partial(next_halves_kernel, self.masks[i + 1], self.extra), [shape, shape], (self.mine, got))
            elif i + 2 == count:
                (self.send,) = run(functools.partial(add_kernel, self.extra), [((rows + self.extra, width), bf16)], (self.mine, got))
            else:
                outs = [((rows, width), bf16)] + ([((16, 128), f32)] if self.extra else [])
                self.send, *self.small = run(functools.partial(add_kernel, self.extra), outs, (self.send, got))
            return False
        mask = self.masks[2 * count - 2 - i]
        got = partners(self.send, mask)
        if i + 2 == 2 * count:
            self.result = (self.send, got)
            return True
        bit = bit_of(mask)
        self.send = jnp.concatenate([jnp.where(bit == 0, self.send, got), jnp.where(bit == 0, got, self.send)], axis=0)
        return False

    def after(self, values):
        self.send = tie(self.send, values)[0]

    def before(self, value):
        value, self.send = tie(value, self.send)
        return value


def unpack_kernel(masks0, masks1, mine0, got0, mine1, got1, lin, gate, out, entry):
    def put_entry(ref, at, k, start, rows):
        value = ref[at : at + rows, :].astype(f32)
        entry[k, pl.ds(2 * start, rows, stride=2), :] = value[:, :128]
        entry[k, pl.ds(2 * start + 1, rows, stride=2), :] = value[:, 128:]

    for mine, got, masks, second in ((mine0, got0, masks0, False), (mine1, got1, masks1, True)):
        bit = bit_of(masks)
        for ref, which in ((mine, bit), (got, 1 - bit)):

            def piece(at, rows):
                return ref[at : at + rows, :].astype(f32)

            @pl.when(which == 0)
            def _():
                if second:
                    lin[1], gate[1], lin[0, :256] = piece(0, 512), piece(512, 512), piece(1024, 256)
                else:
                    gate[0] = piece(0, 512)
                    put_entry(ref, 512, 0, 0, 256)

            @pl.when(which == 1)
            def _():
                if second:
                    out[1, :, :256], out[1, :, 256:], lin[0, 256:] = piece(0, 256), piece(256, 256), piece(1024, 256)
                    put_entry(ref, 512, 1, 0, 512)
                else:
                    out[0, :, :256], out[0, :, 256:] = piece(0, 256), piece(256, 256)
                    put_entry(ref, 512, 0, 256, 256)


class Far:
    def __init__(self, value, at=None, smem=False):
        self.value, self.at, self.smem = value, at, smem
        self.shape = value.shape if at is None else value.shape[1:] if at != "rows" else (2,) + value.shape[1:]

    def source(self, ref):
        if self.at is None:
            return ref
        return ref.at[pl.ds(lax.axis_index("state") * 2, 2)] if self.at == "rows" else ref.at[self.at]


class Held:
    def __init__(self, source, ref, sem):
        self.ref, self.copy, self.shape, self.dtype = ref, pltpu.make_async_copy(source, ref, sem), ref.shape, ref.dtype
        self.copy.start()

    def ready(self):
        if self.copy is not None:
            self.copy.wait()
            self.copy = None

    def __getitem__(self, index):
        self.ready()
        return self.ref[index]


def run(kernel, outs, groups, scratch=(), limit=24, flops=0):
    args = [a for g in groups for a in (g if isinstance(g, tuple) else (g,))]
    far_in = [i for i, a in enumerate(args) if isinstance(a, Far)]
    moved = sum(a.value.size * a.value.dtype.itemsize if isinstance(a, Far) else a.size * a.dtype.itemsize for a in args)

    def whole(*refs):
        ins, results = list(refs[: len(args)]), list(refs[len(args) : len(args) + len(outs)])
        rest = refs[len(args) + len(outs) :]
        own = rest[: len(scratch)]
        if far_in:
            buffers, sem = rest[len(scratch) : -1], rest[-1]
        for j, i in enumerate(far_in):
            ins[i] = Held(args[i].source(ins[i]), buffers[j], sem.at[j])
        grouped, at = [], 0
        for g in groups:
            if isinstance(g, tuple):
                grouped.append(tuple(ins[at : at + len(g)]))
                at += len(g)
            else:
                grouped.append(ins[at])
                at += 1
        kernel(*grouped, *results, *own)
        for i in far_in:
            ins[i].ready()

    def space(far):
        return pl.BlockSpec(memory_space=pltpu.HBM if far else pltpu.VMEM)

    held = [(pltpu.SMEM if args[i].smem else pltpu.VMEM)(args[i].shape, args[i].value.dtype) for i in far_in]
    if held:
        held.append(pltpu.SemaphoreType.DMA((len(held),)))
    return pl.pallas_call(
        whole,
        out_shape=[jax.ShapeDtypeStruct(o[0], o[1]) for o in outs],
        in_specs=[space(isinstance(a, Far)) for a in args],
        out_specs=[space(False)] * len(outs),
        scratch_shapes=[pltpu.VMEM(*s) for s in scratch] + held,
        compiler_params=pltpu.CompilerParams(vmem_limit_bytes=limit * 2**20),
        cost_estimate=pl.CostEstimate(flops=flops, bytes_accessed=moved, transcendentals=0),
    )(*[a.value if isinstance(a, Far) else a for a in args])


def body(tokens, gain, bias, in_proj, out_proj, rate_log, angle_log, skip, glu_lin, glu_gate, positions, cotangent):
    peers = lax.axis_size("seq")
    core = lax.axis_index("state")
    rows, span, width = tokens.shape
    steps = span // CHUNKS
    n = 2 * span
    count = float(rows * span * peers)
    packed = ((8, 128), f32)
    one = 2 * n * 512 * 512
    low = ((n, 512), bf16)
    full = ((n, 512), f32)

    (stats,) = run(stats_kernel, [((2 * peers, 4, 128), f32)], (Far(tokens),))
    raw, at = 0.0, 0
    for v in (gain, bias, skip, rate_log, angle_log):
        raw, at = raw + jnp.pad(v.astype(f32), ((0, 0), (at, 1024 - at - v.shape[1]))), at + v.shape[1]
    w_in = in_proj.reshape(2, 512, 256)
    w_out = out_proj.reshape(2, 256, 512)
    x_oth, cot_oth, in_oth, out_oth, lin_oth, gate_oth = (swap(w) for w in (tokens, cotangent, w_in, w_out, glu_lin, glu_gate))
    enter = [(Far(w_in, k), Far(in_oth, k)) for k in range(2)]
    own, keep, dk, perm = run(
        functools.partial(prep_kernel, peers, steps, span),
        [((32, 128), f32), ((2, n, 128), f32), ((2, peers, 8, 128), f32), ((2, n, n), bf16)],
        (Far(positions, smem=True), raw))
    oth = swap(own)
    ordered = ((peers, 8, 128), f32)

    for_seq, for_all = ((peers, 8, 128), f32), ((2 * peers, 8, 128), f32)
    scan_outs = [full, ((16, 8, 128), f32), for_seq, ((8, 512), f32)]
    xp, nl0, proj, comp, summ, nrm0 = run(
        functools.partial(enter_first_kernel, peers, steps, count), [low, low] + scan_outs,
        (lax.all_to_all(stats, ("seq", "state"), 0, 0), Far(tokens, "rows"), Far(x_oth, "rows"), perm, own, oth, keep) + enter[0], [packed], flops=2 * one)
    got, (cot_oth, out_oth, lin_oth, gate_oth) = blocking(summ, "seq", (cot_oth, out_oth, lin_oth, gate_oth))
    glu = [tuple(Far(w, k) for w in (w_out, out_oth, glu_lin, lin_oth, glu_gate, gate_oth)) for k in range(2)]
    cin0, sl0, gp0, act0, sig0, qv0, y0, stats = run(
        functools.partial(leave_first_kernel, peers, steps),
        [((SLAB, 512), f32), low, low, low, low, low, full, for_all],
        (got, comp, dk, own, oth, keep, proj, xp, nrm0) + glu[0], [packed, ordered], flops=3 * one)
    got, _ = blocking(stats, ("seq", "state"), ())
    nl1, proj, comp, summ, nrm1 = run(
        functools.partial(enter_second_kernel, peers, steps, count), [low] + scan_outs,
        (got, y0, own, oth, keep) + enter[1], [packed], flops=one)
    got, _ = blocking(summ, "seq", ())
    turn_outs = [((8, 512), f32), full, ((16, 8, 128), f32)]
    cin1, result, d_out1, act1, dl1, dg1, sl1, dml1, skip1, dst, comp, summ = run(
        functools.partial(turn_kernel, peers, steps),
        [((SLAB, 512), f32), low, low, low, low, low, low, low] + turn_outs + [for_seq],
        (got, comp, dk, own, oth, keep, proj, y0, nrm1) + glu[1] + (perm, Far(cotangent, "rows"), Far(cot_oth, "rows")),
        [packed, ordered, full, full, full, full], flops=8 * one)
    got, _ = blocking(summ, "seq", ())
    g1_own, g1_oth, s1_own, s1_oth, dn, stats = run(
        functools.partial(adjoint_second_kernel, peers, steps),
        [((2048, 256), f32), ((2048, 256), bf16), ((8, 128), f32), ((8, 128), f32), full, for_all],
        (got, comp, dk, own, oth, keep, nl1, y0, nrm1, cin1, sl1, dst, dml1) + enter[1] + (skip1, act1, dl1, dg1),
        [packed, ordered, full, low], flops=6 * one)
    got, (g1_oth,) = blocking(stats, ("seq", "state"), (g1_oth,))
    g1_got = swap(g1_oth)
    d_out0, dml0, totals1, l0_own, l0_oth, g0_own, g0_oth, skip0, dst, comp, summ = run(
        functools.partial(back_first_kernel, steps, count),
        [full, low, ((8, 512), f32), ((512, 256), f32), ((512, 256), bf16), ((1024, 256), f32), ((1024, 256), bf16)] + turn_outs + [for_seq],
        (got, dn, y0, nrm1, d_out1, own, oth, keep, xp, nrm0, gp0, sig0, qv0) + glu[0] + (act0, sl0),
        [packed, low, low], flops=6 * one)
    got, (l0_oth, g0_oth, g1_got, result) = blocking(summ, "seq", (l0_oth, g0_oth, g1_got, result))
    l0_got, g0_got = swap(l0_oth), swap(g0_oth)
    i0_own, i0_oth, s_own, partial = run(
        functools.partial(adjoint_first_kernel, peers, steps),
        [((512, 256), f32), ((544, 256), bf16), ((16, 128), f32), low],
        (got, comp, dk, own, oth, keep, nl0, xp, nrm0, cin0, sl0, dst, dml0) + enter[0]
        + (skip0, d_out0, s1_own, s1_oth),
        [packed, ordered, full, low, ((16, 128), f32)], flops=3 * one)
    i0_got = swap(i0_oth)
    bulk1 = SeqSum([(g1_own, g1_got), (l0_own, l0_got)], axes_orders((0, 1, 2, 3), (1, 0, 2, 3)))
    bulk0 = SeqSum([(g0_own, g0_got), (i0_own, i0_got)], axes_orders((2, 1, 0, 3), (2, 0, 1, 3)), s_own)
    own_parts, oth_parts = run(order_kernel, [((2, n, 256), bf16)] * 2, (perm, result, partial), flops=2 * one)
    got_parts = swap(oth_parts)
    while not bulk1.step():
        pass
    while not bulk0.small:
        bulk0.step()
    quad = (2, 2, span, width)
    block_out, d_in, ngg, bias_grad, skip_grad, rate_grad, angle_grad = run(
        functools.partial(finish_kernel, count),
        [((rows, span, width), bf16), ((rows, span, width), f32), ((2, 256), f32), ((2, 256), f32), ((2, 256), f32), ((2, 128), f32), ((2, 128), f32)],
        (bulk0.small[0], totals1, own_parts.reshape(quad), got_parts.reshape(quad), Far(tokens), nrm0, raw))
    while not bulk0.step():
        pass
    lin_grad, gate_grad, out_grad, in_grad = run(
        functools.partial(unpack_kernel, bulk0.masks[0], bulk1.masks[0]),
        [((2, 512, 256), f32), ((2, 512, 256), f32), ((2, 256, 512), f32), ((2, 1024, 128), f32)],
        bulk0.result + bulk1.result)
    out_grad, in_grad = out_grad.reshape(2, 2, 128, 512), in_grad.reshape(2, 512, 2, 128)
    return (block_out, d_in, ngg, bias_grad, in_grad, out_grad, rate_grad, angle_grad, skip_grad, lin_grad, gate_grad)


def solution(mesh):
    placed = (
        P(None, "seq", "state"),
        P(None, "state"),
        P(None, "state"),
        P(None, None, None, "state"),
        P(None, None, "state", None),
        P(None, "state"),
        P(None, "state"),
        P(None, "state"),
        P(None, None, "state"),
        P(None, None, "state"),
        P(),
        P(None, "seq", "state"),
    )
    return jax.shard_map(
        body,
        mesh=mesh,
        in_specs=placed,
        out_specs=(
            P(None, "seq", "state"),
            P(None, "seq", "state"),
            P(None, "state"),
            P(None, "state"),
            P(None, None, None, "state"),
            P(None, None, "state", None),
            P(None, "state"),
            P(None, "state"),
            P(None, "state"),
            P(None, None, "state"),
            P(None, None, "state"),
        ),
        check_vma=False,
    )
```

```python
import functools

import jax
import jax.numpy as jnp
from jax import lax
from jax.experimental import pallas as pl
from jax.experimental.pallas import tpu as pltpu
from jax.sharding import PartitionSpec as P

f32, bf16 = jnp.float32, jnp.bfloat16
norm_eps = 1e-05
CHUNKS = 8
SLAB = 2 * CHUNKS
TILE = 256


def mm(a, b):
    return jnp.dot(a, b, preferred_element_type=f32)


def mm_nt(a, b):
    return lax.dot_general(a, b, (((1,), (1,)), ((), ())), preferred_element_type=f32)


def mm_tn(a, b):
    return lax.dot_general(a, b, (((0,), (0,)), ((), ())), preferred_element_type=f32)


def wide(row):
    return jnp.broadcast_to(row, (CHUNKS, 128))


def cmul(ar, ai, br, bi):
    return ar * br - ai * bi, ar * bi + ai * br


def row_of_tiles(tiles):
    return jnp.concatenate([tiles[i : i + 1, :] for i in range(tiles.shape[0])], axis=1)


def channel_row(core, own, oth, at):
    mine, other = own[at : at + 2, :], oth[at : at + 2, :]
    low = jnp.where(core == 0, mine, other)
    high = jnp.where(core == 0, other, mine)
    return jnp.concatenate([low[0:1], low[1:2], high[0:1], high[1:2]], axis=1)


def own_cols(core, width):
    return pl.ds(pl.multiple_of(core * width, width), width)


def oth_cols(core, width):
    return pl.ds(pl.multiple_of((1 - core) * width, width), width)


def scan(drive, lams, keep_ref, which, steps, reverse, start, visit):
    order = range(steps - 1, -1, -1) if reverse else range(steps)
    state = dict(start)
    for s in order:
        for row in range(2):
            at = s * SLAB + row * CHUNKS
            keep = keep_ref[which, at : at + CHUNKS, :]
            for half in range(2):
                lr, li = lams[half]
                hr, hi = state[half, row]
                hr, hi = keep * hr, keep * hi
                dr, di = drive(s, row, half)
                state[half, row] = (lr * hr - li * hi + dr, lr * hi + li * hr + di)
        visit(s, state, keep_ref)
    return state


def keep_products(keep_ref, which, steps):
    out = []
    for row in range(2):
        total = keep_ref[which, row * CHUNKS : (row + 1) * CHUNKS, :]
        for s in range(1, steps):
            at = s * SLAB + row * CHUNKS
            total = total * keep_ref[which, at : at + CHUNKS, :]
        out.append(total)
    return out


def chunk_scan(ends, keeps, powers, reverse, comp_ref, packed):
    index = lax.broadcasted_iota(jnp.int32, (CHUNKS, 128), 0)

    def shifted(value, by, fill):
        turned = pltpu.roll(value, CHUNKS - by if reverse else by, 0)
        valid = index < CHUNKS - by if reverse else index >= by
        return jnp.where(valid, turned, fill)

    for half in range(2):
        for row in range(2):
            er, ei = ends[half, row]
            pr, pi = powers[half][0] * keeps[row], powers[half][1] * keeps[row]
            for by in (1, 2, 4):
                tr, ti = cmul(pr, pi, shifted(er, by, 0.0), shifted(ei, by, 0.0))
                er, ei = er + tr, ei + ti
                pr, pi = cmul(pr, pi, shifted(pr, by, 1.0), shifted(pi, by, 0.0))
            edge = 0 if reverse else CHUNKS - 1
            q = row * 2 + half
            packed[q : q + 1, :] = er[edge : edge + 1, :]
            packed[4 + q : 5 + q, :] = ei[edge : edge + 1, :]
            base = (half * 2 + row) * 4
            comp_ref[base] = shifted(er, 1, 0.0)
            comp_ref[base + 1] = shifted(ei, 1, 0.0)
            comp_ref[base + 2] = shifted(pr, 1, 1.0)
            comp_ref[base + 3] = shifted(pi, 1, 0.0)


def device_carry(me, peers, got, held, dk_ref, which, own, oth, base, conj, reverse, packed):
    got_ref = arrange(got, held)
    index = lax.broadcasted_iota(jnp.int32, (CHUNKS, 128), 0)
    is_own = index % 2 == 0
    sign = jnp.where(index < 4, -1.0, 1.0) * (-1.0 if conj else 1.0)
    ar = jnp.where(is_own, wide(own[base + 11 : base + 12, :]), wide(oth[base + 11 : base + 12, :]))
    ai = jnp.where(is_own, wide(own[base + 12 : base + 13, :]), wide(oth[base + 12 : base + 13, :]))
    ai = ai * sign

    def step(k, held):
        at = peers - 1 - k if reverse else k
        reached = at > me if reverse else at < me
        new = dk_ref[which, at] * (ar * held + ai * pltpu.roll(held, 4, 0)) + got_ref[at]
        return jnp.where(reached, new, held)

    packed[...] = lax.fori_loop(0, peers, step, jnp.zeros((8, 128), f32), unroll=peers <= 16)


def entries(comp_ref, packed):
    start = {}
    for half in range(2):
        for row in range(2):
            base, q = (half * 2 + row) * 4, row * 2 + half
            hr, hi = wide(packed[q : q + 1, :]), wide(packed[4 + q : 5 + q, :])
            tr, ti = cmul(comp_ref[base + 2], comp_ref[base + 3], hr, hi)
            start[half, row] = (comp_ref[base] + tr, comp_ref[base + 1] + ti)
    return start


def decay(own, oth, base, at, conj=False):
    sign = -1.0 if conj else 1.0
    return [(wide(r[base + at : base + at + 1, :]), sign * wide(r[base + at + 1 : base + at + 2, :])) for r in (own, oth)]


def scales(own, oth, base):
    return [wide(r[base + 8 : base + 9, :]) for r in (own, oth)]


def nothing(*_):
    return None


def zeros_start():
    zero = jnp.zeros((CHUNKS, 128), f32)
    return {(half, row): (zero, zero) for half in range(2) for row in range(2)}


def part(s, row):
    at = s * SLAB + row * CHUNKS
    return slice(at, at + CHUNKS)


def cols(half, im):
    at = half * 256 + im * 128
    return slice(at, at + 128)


def flat_rows(ref):
    value = ref[...]
    return value.reshape(value.shape[0] * value.shape[1], value.shape[2])


def spread(out_ref, packed):
    value = packed[...]
    out_ref[...] = value if len(out_ref.shape) == 2 else jnp.broadcast_to(value[None], out_ref.shape)


def arrange(got, held):
    if len(got) == 1:
        return got[0]
    me = place()[0]
    for m, block in enumerate(got):
        for e in range(4):
            held[(((me >> 2) ^ m) << 2) + ((me & 3) ^ e)] = block[e]
    return held


def place():
    return lax.axis_index("seq"), lax.axis_index("state")


def stats_kernel(tokens, stats):
    s1 = s2 = 0.0
    for r in range(tokens.shape[0]):
        x = tokens[r].astype(f32)
        s1 = s1 + jnp.sum(x, axis=0, keepdims=True)
        s2 = s2 + jnp.sum(x * x, axis=0, keepdims=True)
    for i in range(2):
        stats[0, i : i + 1, :] = s1[:, 128 * i : 128 * (i + 1)]
        stats[0, 2 + i : 3 + i, :] = s2[:, 128 * i : 128 * (i + 1)]
    stats[...] = jnp.broadcast_to(stats[0][None], stats.shape)


def prep_kernel(peers, steps, span, pos, raw, small, keep, dk, perm):
    seq, core = place()
    docs = pos.shape[1]

    count = perm.shape[1]
    p = lax.broadcasted_iota(jnp.int32, (count, count), 0)
    q = lax.broadcasted_iota(jnp.int32, (count, count), 1)
    source = ((p >> 3) & 1) * span + (p & 7) * steps + (p >> 4)
    perm[0] = jnp.where(q == source, 1.0, 0.0).astype(bf16)
    source = ((q >> 3) & 1) * span + (q & 7) * steps + (q >> 4)
    perm[1] = jnp.where(p == source, 1.0, 0.0).astype(bf16)

    small[...] = jnp.zeros_like(small)
    for k in range(2):
        at = 16 * k
        values = raw[k : k + 1, :]
        for j in range(6):
            small[at + j : at + j + 1, :] = values[:, 128 * j : 128 * (j + 1)]
        rate = jnp.exp(values[:, 768:896])
        angle = jnp.exp(values[:, 896:])
        modulus = jnp.exp(-rate)
        lr, li = modulus * jnp.cos(angle), modulus * jnp.sin(angle)
        small[at + 6 : at + 7, :] = lr
        small[at + 7 : at + 8, :] = li
        small[at + 8 : at + 9, :] = jnp.sqrt(1.0 - modulus * modulus)
        power = 1
        while power < span:
            lr, li = cmul(lr, li, lr, li)
            power *= 2
            if power == steps:
                small[at + 9 : at + 10, :] = lr
                small[at + 10 : at + 11, :] = li
        small[at + 11 : at + 12, :] = lr
        small[at + 12 : at + 13, :] = li

    chunk = lax.broadcasted_iota(jnp.int32, (CHUNKS, 128), 0) * steps + seq * span
    for row in range(2):
        targets = [pos[core * 2 + row, d] - chunk for d in range(docs)]
        for s in range(steps + 1):
            hit = targets[0] == s
            for t in targets[1:]:
                hit = jnp.logical_or(hit, t == s)
            value = jnp.where(hit, 0.0, 1.0)
            at = s * SLAB + row * CHUNKS
            if s < steps:
                keep[0, at : at + CHUNKS, :] = value
            if s >= 1:
                keep[1, at - SLAB : at - SLAB + CHUNKS, :] = value

    first_row = (lax.broadcasted_iota(jnp.int32, (CHUNKS, 128), 0) // 2) % 2 == 0
    owners = ([], [])
    for d in range(docs):
        a, b = pos[core * 2, d], pos[core * 2 + 1, d]
        owners[0].append(jnp.where(first_row, a // span, b // span))
        owners[1].append(jnp.where(first_row, (a + span - 1) // span - 1, (b + span - 1) // span - 1))

    def mark(j, _):
        for m in range(2):
            hit = owners[m][0] == j
            for o in owners[m][1:]:
                hit = jnp.logical_or(hit, o == j)
            dk[m, j] = jnp.where(hit, 0.0, 1.0)
        return 0

    lax.fori_loop(0, peers, mark, 0)


def norm_rows(total, squares, count, core, own, oth, base, nrm):
    mean = total / count
    inv = lax.rsqrt(squares / count - mean * mean + norm_eps)
    nrm[0:1, :] = mean
    nrm[1:2, :] = inv
    nrm[2:3, :] = channel_row(core, own, oth, base)
    nrm[3:4, :] = channel_row(core, own, oth, base + 2)
    nrm[4:5, :] = channel_row(core, own, oth, base + 4)
    nrm[5:8, :] = jnp.zeros_like(nrm[5:8, :])


def normalized(x, nrm):
    xhat = (x - nrm[0:1, :]) * nrm[1:2, :]
    return xhat, xhat * nrm[2:3, :] + nrm[3:4, :]


def project_and_scan(steps, base, which, reverse, own, oth, keep, win_own, win_oth, nl, proj, comp, summ, packed):
    proj[:, :256] = mm(nl[...], win_own[...])
    proj[:, 256:] = mm(nl[...], win_oth[...])
    lams, sc = decay(own, oth, base, 6), scales(own, oth, base)

    def drive(s, row, half):
        return sc[half] * proj[part(s, row), cols(half, 0)], sc[half] * proj[part(s, row), cols(half, 1)]

    ends = scan(drive, lams, keep, which, steps, reverse, zeros_start(), nothing)
    chunk_scan(ends, keep_products(keep, which, steps), decay(own, oth, base, 9), reverse, comp, packed)
    spread(summ, packed)


def enter_first_kernel(peers, steps, count, got, x_own, x_oth, perm, own, oth, keep, win_own, win_oth,
                       xp, nl, proj, comp, summ, nrm, packed):
    _, core = place()
    sums = got[0:2]
    for j in range(1, peers):
        sums = sums + got[2 * j : 2 * j + 2]
    total = jnp.concatenate([sums[0, 0:1], sums[0, 1:2], sums[1, 0:1], sums[1, 1:2]], axis=1)
    squares = jnp.concatenate([sums[0, 2:3], sums[0, 3:4], sums[1, 2:3], sums[1, 3:4]], axis=1)
    norm_rows(total, squares, count, core, own, oth, 0, nrm)
    xp[:, own_cols(core, 256)] = mm(perm[0], flat_rows(x_own)).astype(bf16)
    xp[:, oth_cols(core, 256)] = mm(perm[0], flat_rows(x_oth)).astype(bf16)
    _, normed = normalized(xp[...].astype(f32), nrm)
    nl[...] = normed.astype(bf16)
    project_and_scan(steps, 0, 0, False, own, oth, keep, win_own, win_oth, nl, proj, comp, summ, packed)


def sum_peers(got):
    if len(got) == 1 and len(got[0].shape) == 3:
        got = [got[0].at[j] for j in range(got[0].shape[0])]
    total = got[0][...]
    for part in got[1:]:
        total = total + part[...]
    return total


def enter_second_kernel(peers, steps, count, got, x, own, oth, keep, win_own, win_oth,
                        nl, proj, comp, summ, nrm, packed):
    _, core = place()
    sums = sum_peers(got)
    norm_rows(row_of_tiles(sums[0:4]), row_of_tiles(sums[4:8]), count, core, own, oth, 16, nrm)
    _, normed = normalized(x[...], nrm)
    nl[...] = normed.astype(bf16)
    project_and_scan(steps, 16, 1, True, own, oth, keep, win_own, win_oth, nl, proj, comp, summ, packed)


def states_of(peers, steps, base, which, reverse, got, comp, dk, own, oth, keep, proj, cin, sl, packed, held):
    device_carry(place()[0], peers, got, held, dk, which, own, oth, base, False, reverse, packed)
    start = entries(comp, packed)
    lams, sc = decay(own, oth, base, 6), scales(own, oth, base)
    for (half, row), (hr, hi) in start.items():
        cin[part(0, row), cols(half, 0)] = hr
        cin[part(0, row), cols(half, 1)] = hi

    def drive(s, row, half):
        return sc[half] * proj[part(s, row), cols(half, 0)], sc[half] * proj[part(s, row), cols(half, 1)]

    def visit(s, state, _):
        for half in range(2):
            for im in range(2):
                both = jnp.concatenate([state[half, row][im] for row in range(2)], axis=0)
                sl[s * SLAB : (s + 1) * SLAB, cols(half, im)] = both.astype(bf16)

    scan(drive, lams, keep, which, steps, reverse, start, visit)


def mix_and_gate(core, x, nrm, sl, wout_own, wout_oth, lin_own, lin_oth, gate_own, gate_oth, gp, act, sig, qv, y):
    c = 0.7978845608028654
    for i in range(0, y.shape[0], TILE):
        rows = slice(i, i + TILE)
        _, normed = normalized(x[rows, :].astype(f32), nrm)
        mixed = mm(sl[rows, :256], wout_own[...]) + mm(sl[rows, 256:], wout_oth[...]) + nrm[4:5, :] * normed
        sq = mixed * mixed
        t = jnp.tanh(mixed * (c + (c * 0.044715) * sq))
        upper = 0.5 + 0.5 * t
        low = (mixed * upper).astype(bf16)
        act[rows, :] = low
        gp[rows, :] = (upper + mixed * (upper * (1.0 - t)) * (c + (3 * c * 0.044715) * sq)).astype(gp.dtype)
        for w_lin, w_gate, at in ((lin_own, gate_own, own_cols(core, 256)), (lin_oth, gate_oth, oth_cols(core, 256))):
            linear = mm(low, w_lin[...])
            gating = mm(low, w_gate[...])
            sg = 0.5 + 0.5 * jnp.tanh(0.5 * gating)
            out = linear * sg
            sig[rows, at] = sg.astype(sig.dtype)
            qv[rows, at] = (out * (1.0 - sg)).astype(qv.dtype)
            y[rows, at] = x[rows, at].astype(f32) + out
        yield rows


def leave_first_kernel(peers, steps, got, comp, dk, own, oth, keep, proj, x, nrm, wout_own, wout_oth,
                       lin_own, lin_oth, gate_own, gate_oth, cin, sl, gp, act, sig, qv, y, stats, packed, held):
    states_of(peers, steps, 0, 0, False, got, comp, dk, own, oth, keep, proj, cin, sl, packed, held)
    s1 = s2 = 0.0
    for rows in mix_and_gate(place()[1], x, nrm, sl, wout_own, wout_oth, lin_own, lin_oth, gate_own, gate_oth, gp, act, sig, qv, y):
        out = y[rows, :]
        s1, s2 = s1 + jnp.sum(out, axis=0, keepdims=True), s2 + jnp.sum(out * out, axis=0, keepdims=True)
    pack_two(s1, s2, packed)
    spread(stats, packed)


def pack_two(a, b, packed):
    for i in range(4):
        packed[i : i + 1, :] = a[:, 128 * i : 128 * (i + 1)]
        packed[4 + i : 5 + i, :] = b[:, 128 * i : 128 * (i + 1)]


def glu_backward(steps, base, adj_which, adj_reverse, core, d_out, nrm, x, gp, sig, qv, own, oth, keep, wout_own, wout_oth,
                 lin_own, lin_oth, gate_own, gate_oth, skip_row, dst, comp, summ, packed, dl, dg, dml):
    mine, other = own_cols(core, 256), oth_cols(core, 256)
    total = 0.0
    for i in range(0, dl.shape[0], TILE):
        rows = slice(i, i + TILE)
        grad = d_out(rows)
        dl[rows, :] = (grad * sig[rows, :].astype(f32)).astype(bf16)
        dg[rows, :] = (grad * qv[rows, :].astype(f32)).astype(bf16)
        d_active = (mm_nt(dl[rows, mine], lin_own[...]) + mm_nt(dg[rows, mine], gate_own[...])
                    + mm_nt(dl[rows, other], lin_oth[...]) + mm_nt(dg[rows, other], gate_oth[...]))
        d_mixed = d_active * gp[rows, :].astype(f32)
        _, normed = normalized(x[rows, :].astype(f32), nrm)
        total = total + jnp.sum(d_mixed * normed, axis=0, keepdims=True)
        low = d_mixed.astype(bf16)
        dml[rows, :] = low
        dst[rows, :256] = mm_nt(low, wout_own[...])
        dst[rows, 256:] = mm_nt(low, wout_oth[...])
    skip_row[0:1, :] = total
    lams = decay(own, oth, base, 6, conj=True)

    def drive(s, row, half):
        return dst[part(s, row), cols(half, 0)], dst[part(s, row), cols(half, 1)]

    ends = scan(drive, lams, keep, adj_which, steps, adj_reverse, zeros_start(), nothing)
    chunk_scan(ends, keep_products(keep, adj_which, steps), decay(own, oth, base, 9, conj=True), adj_reverse, comp, packed)
    spread(summ, packed)


def mixer_grads(act, dl, dg, sl, dml, l_own, l_oth, g_own, g_oth):
    _, core = place()
    mine, other = own_cols(core, 256), oth_cols(core, 256)
    left = act[...].T
    l_own[...] = mm(left, dl[:, mine]).astype(bf16)
    l_oth[...] = mm(left, dl[:, other]).astype(bf16)
    g_own[0:512, :] = mm(left, dg[:, mine]).astype(bf16)
    g_oth[0:512, :] = mm(left, dg[:, other]).astype(bf16)
    for ref, cut in ((g_own, slice(0, 256)), (g_oth, slice(256, 512))):
        left = sl[:, cut].T
        for i in range(2):
            ref[512 + 256 * i : 768 + 256 * i, :] = mm(left, dml[:, 256 * i : 256 * (i + 1)]).astype(ref.dtype)


def in_grads(nl, dp, g_own, g_oth):
    left = nl[...].T
    g_own[...] = mm(left, dp[:, :256]).astype(bf16)
    g_oth[...] = mm(left, dp[:, 256:]).astype(bf16)


def turn_kernel(peers, steps, got, comp_in, dk, own, oth, keep, proj, x, nrm, wout_own, wout_oth,
                lin_own, lin_oth, gate_own, gate_oth, perm, cot_own, cot_oth,
                cin, result, d_out, act, dl, dg, sl, dml, skip_row, dst, comp, summ,
                packed, held, gp, sig, qv, y):
    _, core = place()
    states_of(peers, steps, 16, 1, True, got, comp_in, dk, own, oth, keep, proj, cin, sl, packed, held)
    for _ in mix_and_gate(core, x, nrm, sl, wout_own, wout_oth, lin_own, lin_oth, gate_own, gate_oth, gp, act, sig, qv, y):
        pass
    result[...] = y[...].astype(bf16)
    d_out[:, own_cols(core, 256)] = mm(perm[0], flat_rows(cot_own)).astype(bf16)
    d_out[:, oth_cols(core, 256)] = mm(perm[0], flat_rows(cot_oth)).astype(bf16)
    glu_backward(steps, 16, 0, False, core, lambda rows: d_out[rows, :].astype(f32), nrm, x, gp, sig, qv, own, oth, keep, wout_own, wout_oth,
                 lin_own, lin_oth, gate_own, gate_oth, skip_row, dst, comp, summ, packed, dl, dg, dml)


def adjoint_part(peers, steps, base, keep_which, adj_which, adj_reverse, got, comp, dk, own, oth, keep, nl, x, nrm,
                 cin, sl, dst, dml, win_own, win_oth, skip_row, small_own, small_oth, all_rows, packed, held, proj, dp, keep_tile):
    _, core = place()
    device_carry(place()[0], peers, got, held, dk, adj_which, own, oth, base, True, adj_reverse, packed)
    start = entries(comp, packed)
    lams, sc = decay(own, oth, base, 6, conj=True), scales(own, oth, base)
    zero = jnp.zeros((CHUNKS, 128), f32)
    acc = {half: [zero, zero, zero] for half in range(2)}
    proj[:, :256] = mm(nl[...], win_own[...])
    proj[:, 256:] = mm(nl[...], win_oth[...])

    def prior(s, half, im):
        before = s - 1 if adj_reverse else s + 1
        if 0 <= before < steps:
            return sl[before * SLAB : (before + 1) * SLAB, cols(half, im)].astype(f32)
        return cin[:, cols(half, im)]

    def drive(s, row, half):
        return dst[part(s, row), cols(half, 0)], dst[part(s, row), cols(half, 1)]

    def visit(s, state, _):
        for half in range(2):
            prior_re, prior_im = prior(s, half, 0), prior(s, half, 1)
            for row in range(2):
                ar, ai = state[half, row]
                pr, pi = prior_re[part(0, row)], prior_im[part(0, row)]
                keep_here = keep[keep_which, part(s, row), :]
                acc[half][0] = acc[half][0] + keep_here * (ar * pr + ai * pi)
                acc[half][1] = acc[half][1] + keep_here * (ai * pr - ar * pi)
                acc[half][2] = acc[half][2] + (ar * proj[part(s, row), cols(half, 0)] + ai * proj[part(s, row), cols(half, 1)])
            for im in range(2):
                both = jnp.concatenate([sc[half] * state[half, row][im] for row in range(2)], axis=0)
                dp[s * SLAB : (s + 1) * SLAB, cols(half, im)] = both.astype(bf16)

    scan(drive, lams, keep, adj_which, steps, adj_reverse, start, visit)

    bias_row = gain_row = 0.0
    for i in range(0, dp.shape[0], TILE):
        rows = slice(i, i + TILE)
        d_normed = dml[rows, :].astype(f32) * nrm[4:5, :] + mm_nt(dp[rows, :256], win_own[...]) + mm_nt(dp[rows, 256:], win_oth[...])
        xhat, _ = normalized(x[rows, :].astype(f32), nrm)
        bias_row = bias_row + jnp.sum(d_normed, axis=0, keepdims=True)
        gain_row = gain_row + jnp.sum(d_normed * xhat, axis=0, keepdims=True)
        keep_tile(rows, d_normed)
    pack_two(bias_row, gain_row, packed)

    wanted = (skip_row[0:1, :], bias_row, gain_row) if all_rows else (skip_row[0:1, :],)
    for ref, half in ((small_own, 0), (small_oth, 1)):
        ref[...] = jnp.zeros_like(ref)
        at = 0
        for row in wanted:
            pick = jnp.where(core == half, row[:, :256], row[:, 256:])
            ref[at : at + 1, :] = pick[:, :128]
            ref[at + 1 : at + 2, :] = pick[:, 128:]
            at += 2
        for j in range(3):
            ref[at + j : at + j + 1, :] = jnp.sum(acc[half][j], axis=0, keepdims=True)


def adjoint_second_kernel(peers, steps, got, comp, dk, own, oth, keep, nl, x, nrm, cin, sl, dst, dml, win_own, win_oth, skip_row, act, dl, dg,
                          g_own, g_oth, small_own, small_oth, dn, stats, packed, held, proj, dp):
    def keep_tile(rows, d_normed):
        dn[rows, :] = d_normed

    adjoint_part(peers, steps, 16, 1, 0, False, got, comp, dk, own, oth, keep, nl, x, nrm,
                 cin, sl, dst, dml, win_own, win_oth, skip_row, small_own, small_oth, False, packed, held, proj, dp, keep_tile)
    spread(stats, packed)
    mixer_grads(act, dl, dg, sl, dml, g_own.at[:512], g_oth.at[:512], g_own.at[512:1536], g_oth.at[512:1536])
    in_grads(nl, dp, g_own.at[1536:], g_oth.at[1536:])


def back_first_kernel(steps, count, got, dn, x2, nrm2, d_out2, own, oth, keep, x, nrm, gp, sig, qv,
                      wout_own, wout_oth, lin_own, lin_oth, gate_own, gate_oth,
                      act, sl, d_out, dml, totals, l_own, l_oth, g_own, g_oth, skip_row, dst, comp, summ, packed, dl, dg):
    sums = sum_peers(got)
    bias_row, gain_row = row_of_tiles(sums[0:4]), row_of_tiles(sums[4:8])
    totals[...] = jnp.zeros_like(totals)
    totals[0:1, :], totals[1:2, :] = bias_row, gain_row
    mean, inv, gain = nrm2[0:1, :], nrm2[1:2, :], nrm2[2:3, :]
    scaled, shift, slope = inv * gain, inv * gain * bias_row / count, inv * inv * gain * gain_row / count

    def d_in(rows):
        value = d_out2[rows, :].astype(f32) + scaled * dn[rows, :] - shift - slope * (x2[rows, :] - mean)
        d_out[rows, :] = value
        return value

    glu_backward(steps, 0, 1, True, place()[1], d_in, nrm, x, gp, sig, qv, own, oth, keep, wout_own, wout_oth,
                 lin_own, lin_oth, gate_own, gate_oth, skip_row, dst, comp, summ, packed, dl, dg, dml)
    mixer_grads(act, dl, dg, sl, dml, l_own, l_oth, g_own, g_oth)


def adjoint_first_kernel(peers, steps, got, comp, dk, own, oth, keep, nl, x, nrm, cin, sl, dst, dml, win_own, win_oth, skip_row,
                         d_out, small1_own, small1_oth,
                         g_own, g_oth, small_own, partial, packed, held, proj, dp, small_oth):
    _, core = place()
    scaled = nrm[1:2, :] * nrm[2:3, :]

    def keep_tile(rows, d_normed):
        partial[rows, :] = (d_out[rows, :] + scaled * d_normed).astype(bf16)

    adjoint_part(peers, steps, 0, 0, 1, True, got, comp, dk, own, oth, keep, nl, x, nrm,
                 cin, sl, dst, dml, win_own, win_oth, skip_row, small_own, small_oth, True, packed, held, proj, dp, keep_tile)
    small_own[9:14, :] = small1_own[0:5, :]
    small_oth[9:14, :] = small1_oth[0:5, :]
    in_grads(nl, dp, g_own, g_oth.at[:512])
    put_small(g_oth, 512, small_oth[...])


def order_kernel(perm, result, partial, own, oth):
    _, core = place()
    for i, ref in enumerate((result, partial)):
        own[i] = mm(perm[1], ref[:, own_cols(core, 256)]).astype(bf16)
        oth[i] = mm(perm[1], ref[:, oth_cols(core, 256)]).astype(bf16)


def finish_kernel(count, packed, totals1, mine_parts, other_parts, tokens, nrm, raw,
                  block_out, d_in, ngg, bias, skip, rate_grad, angle_grad):
    _, core = place()
    for ref, j in ((skip, 0), (bias, 2), (ngg, 4)):
        ref[0:1, :128], ref[0:1, 128:] = packed[j : j + 1, :], packed[j + 1 : j + 2, :]
    skip[1:2, :128], skip[1:2, 128:] = packed[9:10, :], packed[10:11, :]
    bias[1:2, :] = totals1[0:1, own_cols(core, 256)]
    ngg[1:2, :] = totals1[1:2, own_cols(core, 256)]
    for k, at in ((0, 6), (1, 11)):
        values = raw[k : k + 1, :]
        rate = jnp.exp(values[:, 768:896])
        angle = jnp.exp(values[:, 896:])
        modulus = jnp.exp(-rate)
        scale = jnp.sqrt(1.0 - modulus * modulus)
        cos, sin = jnp.cos(angle), jnp.sin(angle)
        dr, di, ds = (packed[at + j : at + j + 1, :] for j in range(3))
        g_mod = dr * cos + di * sin - ds * modulus / scale
        rate_grad[k : k + 1, :] = -g_mod * modulus * rate
        angle_grad[k : k + 1, :] = modulus * (di * cos - dr * sin) * angle
    mine = nrm[:, own_cols(core, 256)]
    mean, inv, gain = mine[0:1, :], mine[1:2, :], mine[2:3, :]
    bias_row, gain_row = bias[0:1, :], ngg[0:1, :]
    flat = inv * gain / count
    for r in range(4):
        block_out[r] = jnp.where(core == r // 2, mine_parts[0, r % 2], other_parts[0, r % 2])
        held_rows = jnp.where(core == r // 2, mine_parts[1, r % 2].astype(f32), other_parts[1, r % 2].astype(f32))
        xhat = (tokens[r].astype(f32) - mean) * inv
        d_in[r] = held_rows - flat * (bias_row + xhat * gain_row)


def swap(value):
    return lax.ppermute(value, "state", [(0, 1), (1, 0)])


def to_all(value, axes):
    peers = 1
    for a in axes:
        peers *= lax.axis_size(a)
    return lax.all_to_all(jnp.broadcast_to(value[None], (peers,) + value.shape), axes, 0, 0)


def blocking(value, axes, others):
    value, others = lax.optimization_barrier((value, others))
    got, others = lax.optimization_barrier((lax.all_to_all(value, axes, 0, 0), others))
    return (got,), others


def gather_seq(value):
    if lax.axis_size("seq") != 16:
        return (to_all(value, ("seq",)),)
    near = jnp.stack([value] + [partner(value, m) for m in (1, 2, 3)])
    return (near,) + tuple(partner(near, m) for m in (4, 8, 12))


def sum_all(value):
    if lax.axis_size("seq") != 16:
        return (to_all(value, ("seq", "state")),)
    value = value + swap(value)
    near = value + partner(value, 1) + partner(value, 2) + partner(value, 3)
    return (near,) + tuple(partner(near, m) for m in (4, 8, 12))


def partner(value, mask):
    size = lax.axis_size("seq")
    return lax.ppermute(value, "seq", [(i, i ^ mask) for i in range(size)])


def partners(value, masks):
    size = lax.axis_size("seq")
    return lax.ppermute(value, ("seq", "state"), [(2 * i + c, 2 * (i ^ masks[c]) + c) for i in range(size) for c in range(2)])


def tie(value, others):
    return lax.optimization_barrier((value, others))


def bit_of(masks):
    me, core = place()
    return (me // jnp.where(core == 0, masks[0], masks[1])) & 1


def put_small(out, at, value):
    high = value.astype(bf16)
    rest = value - high.astype(f32)
    middle = rest.astype(bf16)
    low = (rest - middle.astype(f32)).astype(bf16)
    out[at : at + 16, :128], out[at : at + 16, 128:] = high, middle
    out[at + 16 : at + 32, :128], out[at + 16 : at + 32, 128:] = low, jnp.zeros_like(low)


def get_small(ref, at):
    return (ref[at : at + 16, :128].astype(f32) + ref[at : at + 16, 128:].astype(f32)) + ref[at + 16 : at + 32, :128].astype(f32)


def first_halves_kernel(masks, pairs, small, mine, other):
    bit, at = bit_of(masks), 0
    for own, got in pairs:
        half = own.shape[0] // 2
        for out, which in ((mine, bit), (other, 1 - bit)):
            rows = pl.ds(pl.multiple_of(which * half, half), half)
            out[at : at + half, :] = (own[rows, :].astype(f32) + got[rows, :].astype(f32)).astype(bf16)
        at += half
    if small is not None:
        total = small[...] + get_small(pairs[-1][1], pairs[-1][0].shape[0])
        put_small(mine, at, total)
        put_small(other, at, total)


def next_halves_kernel(masks, extra, held, got, mine, other):
    bit, half = bit_of(masks), mine.shape[0] - extra
    for out, which in ((mine, bit), (other, 1 - bit)):
        rows = pl.ds(pl.multiple_of(which * half, half), half)
        out[:half, :] = (held[rows, :].astype(f32) + got[rows, :].astype(f32)).astype(bf16)
    if extra:
        total = get_small(held, 2 * half) + get_small(got, 2 * half)
        put_small(mine, half, total)
        put_small(other, half, total)


def add_kernel(extra, held, got, total, *small):
    rows = held.shape[0] - extra
    total[:rows, :] = (held[:rows, :].astype(f32) + got[:rows, :].astype(f32)).astype(bf16)
    if extra:
        value = get_small(held, rows) + get_small(got, rows)
        if small:
            small[0][...] = value
        else:
            put_small(total, rows, value)


def axes_orders(*orders):
    masks, m = [], 1
    while m < lax.axis_size("seq"):
        masks.append(m)
        m *= 2
    return list(zip(*[[masks[i] for i in o] + masks[4:] for o in orders]))


class SeqSum:
    def __init__(self, pairs, masks, small=None):
        self.masks, self.at, self.small, self.extra = masks, 0, (), 0 if small is None else 32
        rows = sum(a.shape[0] for a, _ in pairs) // 2 + self.extra
        shape = ((rows, pairs[0][0].shape[1]), bf16)
        flat = tuple(v for p in pairs for v in p) + (() if small is None else (small,))

        def kernel(refs, mine, other):
            count = 2 * len(pairs)
            first_halves_kernel(masks[0], [(refs[i], refs[i + 1]) for i in range(0, count, 2)],
                                None if small is None else refs[count], mine, other)

        self.mine, self.send = run(kernel, [shape, shape], (flat,))

    def step(self):
        count, i = len(self.masks), self.at
        self.at += 1
        if i < count:
            got = partners(self.send, self.masks[i])
            rows, width = got.shape
            rows -= self.extra
            if i + 2 < count:
                shape = ((rows // 2 + self.extra, width), bf16)
                self.mine, self.send = run(functools.partial(next_halves_kernel, self.masks[i + 1], self.extra), [shape, shape], (self.mine, got))
            elif i + 2 == count:
                (self.send,) = run(functools.partial(add_kernel, self.extra), [((rows + self.extra, width), bf16)], (self.mine, got))
            else:
                outs = [((rows, width), bf16)] + ([((16, 128), f32)] if self.extra else [])
                self.send, *self.small = run(functools.partial(add_kernel, self.extra), outs, (self.send, got))
            return False
        mask = self.masks[2 * count - 2 - i]
        got = partners(self.send, mask)
        if i + 2 == 2 * count:
            self.result = (self.send, got)
            return True
        bit = bit_of(mask)
        self.send = jnp.concatenate([jnp.where(bit == 0, self.send, got), jnp.where(bit == 0, got, self.send)], axis=0)
        return False

    def after(self, values):
        self.send = tie(self.send, values)[0]

    def before(self, value):
        value, self.send = tie(value, self.send)
        return value


def unpack_kernel(masks0, masks1, mine0, got0, mine1, got1, lin, gate, out, entry):
    def put_entry(ref, at, k, start, rows):
        value = ref[at : at + rows, :].astype(f32)
        entry[k, pl.ds(2 * start, rows, stride=2), :] = value[:, :128]
        entry[k, pl.ds(2 * start + 1, rows, stride=2), :] = value[:, 128:]

    for mine, got, masks, second in ((mine0, got0, masks0, False), (mine1, got1, masks1, True)):
        bit = bit_of(masks)
        for ref, which in ((mine, bit), (got, 1 - bit)):

            def piece(at, rows):
                return ref[at : at + rows, :].astype(f32)

            @pl.when(which == 0)
            def _():
                if second:
                    lin[1], gate[1], lin[0, :256] = piece(0, 512), piece(512, 512), piece(1024, 256)
                else:
                    gate[0] = piece(0, 512)
                    put_entry(ref, 512, 0, 0, 256)

            @pl.when(which == 1)
            def _():
                if second:
                    out[1, :, :256], out[1, :, 256:], lin[0, 256:] = piece(0, 256), piece(256, 256), piece(1024, 256)
                    put_entry(ref, 512, 1, 0, 512)
                else:
                    out[0, :, :256], out[0, :, 256:] = piece(0, 256), piece(256, 256)
                    put_entry(ref, 512, 0, 256, 256)


class Far:
    def __init__(self, value, at=None, smem=False):
        self.value, self.at, self.smem = value, at, smem
        self.shape = value.shape if at is None else value.shape[1:] if at != "rows" else (2,) + value.shape[1:]

    def source(self, ref):
        if self.at is None:
            return ref
        return ref.at[pl.ds(lax.axis_index("state") * 2, 2)] if self.at == "rows" else ref.at[self.at]


class Part:
    def __init__(self, value, at):
        self.value, self.at = value, at

    def view(self, ref):
        return ref.at[pl.ds(lax.axis_index("state") * 2, 2)] if self.at == "rows" else ref.at[self.at]


class Held:
    def __init__(self, source, ref, sem):
        self.ref, self.copy, self.shape, self.dtype = ref, pltpu.make_async_copy(source, ref, sem), ref.shape, ref.dtype
        self.copy.start()

    def ready(self):
        if self.copy is not None:
            self.copy.wait()
            self.copy = None

    def __getitem__(self, index):
        self.ready()
        return self.ref[index]


def run(kernel, outs, groups, scratch=(), limit=24, flops=0):
    args = [a for g in groups for a in (g if isinstance(g, tuple) else (g,))]
    far_in = [i for i, a in enumerate(args) if isinstance(a, Far)]
    arrays = [a.value if isinstance(a, (Far, Part)) else a for a in args]
    moved = sum(a.size * a.dtype.itemsize for a in arrays)

    def whole(*refs):
        ins, results = list(refs[: len(args)]), list(refs[len(args) : len(args) + len(outs)])
        rest = refs[len(args) + len(outs) :]
        own = rest[: len(scratch)]
        if far_in:
            buffers, sem = rest[len(scratch) : -1], rest[-1]
        for j, i in enumerate(far_in):
            ins[i] = Held(args[i].source(ins[i]), buffers[j], sem.at[j])
        ins = [a.view(r) if isinstance(a, Part) else r for r, a in zip(ins, args)]
        grouped, at = [], 0
        for g in groups:
            if isinstance(g, tuple):
                grouped.append(tuple(ins[at : at + len(g)]))
                at += len(g)
            else:
                grouped.append(ins[at])
                at += 1
        kernel(*grouped, *results, *own)
        for i in far_in:
            ins[i].ready()

    def space(far):
        return pl.BlockSpec(memory_space=pltpu.HBM if far else pltpu.VMEM)

    held = [(pltpu.SMEM if args[i].smem else pltpu.VMEM)(args[i].shape, args[i].value.dtype) for i in far_in]
    if held:
        held.append(pltpu.SemaphoreType.DMA((len(held),)))
    return pl.pallas_call(
        whole,
        out_shape=[jax.ShapeDtypeStruct(o[0], o[1]) for o in outs],
        in_specs=[space(isinstance(a, Far)) for a in args],
        out_specs=[space(False)] * len(outs),
        scratch_shapes=[pltpu.VMEM(*s) for s in scratch] + held,
        compiler_params=pltpu.CompilerParams(vmem_limit_bytes=limit * 2**20),
        cost_estimate=pl.CostEstimate(flops=flops, bytes_accessed=moved, transcendentals=0),
    )(*arrays)


def body(tokens, gain, bias, in_proj, out_proj, rate_log, angle_log, skip, glu_lin, glu_gate, positions, cotangent):
    peers = lax.axis_size("seq")
    core = lax.axis_index("state")
    rows, span, width = tokens.shape
    steps = span // CHUNKS
    n = 2 * span
    count = float(rows * span * peers)
    packed = ((8, 128), f32)
    one = 2 * n * 512 * 512
    low = ((n, 512), bf16)
    full = ((n, 512), f32)

    (stats,) = run(stats_kernel, [((2 * peers, 4, 128), f32)], (tokens,))
    raw, at = 0.0, 0
    for v in (gain, bias, skip, rate_log, angle_log):
        raw, at = raw + jnp.pad(v.astype(f32), ((0, 0), (at, 1024 - at - v.shape[1]))), at + v.shape[1]
    w_in = in_proj.reshape(2, 512, 256)
    w_out = out_proj.reshape(2, 256, 512)
    x_oth, cot_oth, in_oth, out_oth, lin_oth, gate_oth = (swap(w) for w in (tokens, cotangent, w_in, w_out, glu_lin, glu_gate))
    enter = [(Part(w_in, k), Part(in_oth, k)) for k in range(2)]
    own, keep, dk, perm = run(
        functools.partial(prep_kernel, peers, steps, span),
        [((32, 128), f32), ((2, n, 128), f32), ((2, peers, 8, 128), f32), ((2, n, n), bf16)],
        (Far(positions, smem=True), raw))
    oth = swap(own)
    ordered = ((peers, 8, 128), f32)

    for_seq, for_all = ((peers, 8, 128), f32), ((2 * peers, 8, 128), f32)
    scan_outs = [full, ((16, 8, 128), f32), for_seq, ((8, 512), f32)]
    xp, nl0, proj, comp, summ, nrm0 = run(
        functools.partial(enter_first_kernel, peers, steps, count), [low, low] + scan_outs,
        (lax.all_to_all(stats, ("seq", "state"), 0, 0), Part(tokens, "rows"), Part(x_oth, "rows"), perm, own, oth, keep) + enter[0], [packed], flops=2 * one)
    got, (cot_oth, out_oth, lin_oth, gate_oth) = blocking(summ, "seq", (cot_oth, out_oth, lin_oth, gate_oth))
    glu = [tuple((Part if i % 2 else Part)(w, k) for i, w in enumerate((w_out, out_oth, glu_lin, lin_oth, glu_gate, gate_oth))) for k in range(2)]
    cin0, sl0, gp0, act0, sig0, qv0, y0, stats = run(
        functools.partial(leave_first_kernel, peers, steps),
        [((SLAB, 512), f32), low, low, low, low, low, full, for_all],
        (got, comp, dk, own, oth, keep, proj, xp, nrm0) + glu[0], [packed, ordered], flops=3 * one)
    got, _ = blocking(stats, ("seq", "state"), ())
    nl1, proj, comp, summ, nrm1 = run(
        functools.partial(enter_second_kernel, peers, steps, count), [low] + scan_outs,
        (got, y0, own, oth, keep) + enter[1], [packed], flops=one)
    got, _ = blocking(summ, "seq", ())
    turn_outs = [((8, 512), f32), full, ((16, 8, 128), f32)]
    cin1, result, d_out1, act1, dl1, dg1, sl1, dml1, skip1, dst, comp, summ = run(
        functools.partial(turn_kernel, peers, steps),
        [((SLAB, 512), f32), low, low, low, low, low, low, low] + turn_outs + [for_seq],
        (got, comp, dk, own, oth, keep, proj, y0, nrm1) + glu[1] + (perm, Part(cotangent, "rows"), Part(cot_oth, "rows")),
        [packed, ordered, full, full, full, full], flops=8 * one)
    got, _ = blocking(summ, "seq", ())
    g1_own, g1_oth, s1_own, s1_oth, dn, stats = run(
        functools.partial(adjoint_second_kernel, peers, steps),
        [((2048, 256), bf16), ((2048, 256), bf16), ((8, 128), f32), ((8, 128), f32), full, for_all],
        (got, comp, dk, own, oth, keep, nl1, y0, nrm1, cin1, sl1, dst, dml1) + enter[1] + (skip1, act1, dl1, dg1),
        [packed, ordered, full, low], flops=6 * one)
    got, (g1_oth,) = blocking(stats, ("seq", "state"), (g1_oth,))
    g1_got = swap(g1_oth)
    d_out0, dml0, totals1, l0_own, l0_oth, g0_own, g0_oth, skip0, dst, comp, summ = run(
        functools.partial(back_first_kernel, steps, count),
        [full, low, ((8, 512), f32), ((512, 256), bf16), ((512, 256), bf16), ((1024, 256), bf16), ((1024, 256), bf16)] + turn_outs + [for_seq],
        (got, dn, y0, nrm1, d_out1, own, oth, keep, xp, nrm0, gp0, sig0, qv0) + glu[0] + (act0, sl0),
        [packed, low, low], flops=6 * one)
    got, (l0_oth, g0_oth, g1_got, result) = blocking(summ, "seq", (l0_oth, g0_oth, g1_got, result))
    l0_got, g0_got = swap(l0_oth), swap(g0_oth)
    i0_own, i0_oth, s_own, partial = run(
        functools.partial(adjoint_first_kernel, peers, steps),
        [((512, 256), bf16), ((544, 256), bf16), ((16, 128), f32), low],
        (got, comp, dk, own, oth, keep, nl0, xp, nrm0, cin0, sl0, dst, dml0) + enter[0]
        + (skip0, d_out0, s1_own, s1_oth),
        [packed, ordered, full, low, ((16, 128), f32)], flops=3 * one)
    i0_got = swap(i0_oth)
    bulk1 = SeqSum([(g1_own, g1_got), (l0_own, l0_got)], axes_orders((0, 1, 2, 3), (1, 0, 2, 3)))
    bulk0 = SeqSum([(g0_own, g0_got), (i0_own, i0_got)], axes_orders((2, 1, 0, 3), (2, 0, 1, 3)), s_own)
    own_parts, oth_parts = run(order_kernel, [((2, n, 256), bf16)] * 2, (perm, result, partial), flops=2 * one)
    got_parts = swap(oth_parts)
    for _ in range(3):
        bulk1.step()
    ended = False
    while not bulk0.step():
        if not ended:
            bulk1.after(bulk0.send)
            ended = bulk1.step()
    while not ended:
        ended = bulk1.step()
    quad = (2, 2, span, width)
    block_out, d_in, ngg, bias_grad, skip_grad, rate_grad, angle_grad = run(
        functools.partial(finish_kernel, count),
        [((rows, span, width), bf16), ((rows, span, width), f32), ((2, 256), f32), ((2, 256), f32), ((2, 256), f32), ((2, 128), f32), ((2, 128), f32)],
        (bulk0.small[0], totals1, own_parts.reshape(quad), got_parts.reshape(quad), tokens, nrm0, raw))
    lin_grad, gate_grad, out_grad, in_grad = run(
        functools.partial(unpack_kernel, bulk0.masks[0], bulk1.masks[0]),
        [((2, 512, 256), f32), ((2, 512, 256), f32), ((2, 256, 512), f32), ((2, 1024, 128), f32)],
        bulk0.result + bulk1.result)
    out_grad, in_grad = out_grad.reshape(2, 2, 128, 512), in_grad.reshape(2, 512, 2, 128)
    return (block_out, d_in, ngg, bias_grad, in_grad, out_grad, rate_grad, angle_grad, skip_grad, lin_grad, gate_grad)


def solution(mesh):
    placed = (
        P(None, "seq", "state"),
        P(None, "state"),
        P(None, "state"),
        P(None, None, None, "state"),
        P(None, None, "state", None),
        P(None, "state"),
        P(None, "state"),
        P(None, "state"),
        P(None, None, "state"),
        P(None, None, "state"),
        P(),
        P(None, "seq", "state"),
    )
    return jax.shard_map(
        body,
        mesh=mesh,
        in_specs=placed,
        out_specs=(
            P(None, "seq", "state"),
            P(None, "seq", "state"),
            P(None, "state"),
            P(None, "state"),
            P(None, None, None, "state"),
            P(None, None, "state", None),
            P(None, "state"),
            P(None, "state"),
            P(None, "state"),
            P(None, None, "state"),
            P(None, None, "state"),
        ),
        check_vma=False,
    )
```

```python
import functools

import jax
import jax.numpy as jnp
from jax import lax
from jax.experimental import pallas as pl
from jax.experimental.pallas import tpu as pltpu
from jax.sharding import PartitionSpec as P

f32, bf16 = jnp.float32, jnp.bfloat16
norm_eps = 1e-05
CHUNKS = 8
SLAB = 2 * CHUNKS
TILE = 256


def mm(a, b):
    return jnp.dot(a, b, preferred_element_type=f32)


def mm_nt(a, b):
    return lax.dot_general(a, b, (((1,), (1,)), ((), ())), preferred_element_type=f32)


def mm_tn(a, b):
    return lax.dot_general(a, b, (((0,), (0,)), ((), ())), preferred_element_type=f32)


def wide(row):
    return jnp.broadcast_to(row, (CHUNKS, 128))


def cmul(ar, ai, br, bi):
    return ar * br - ai * bi, ar * bi + ai * br


def row_of_tiles(tiles):
    return jnp.concatenate([tiles[i : i + 1, :] for i in range(tiles.shape[0])], axis=1)


def channel_row(core, own, oth, at):
    mine, other = own[at : at + 2, :], oth[at : at + 2, :]
    low = jnp.where(core == 0, mine, other)
    high = jnp.where(core == 0, other, mine)
    return jnp.concatenate([low[0:1], low[1:2], high[0:1], high[1:2]], axis=1)


def own_cols(core, width):
    return pl.ds(pl.multiple_of(core * width, width), width)


def oth_cols(core, width):
    return pl.ds(pl.multiple_of((1 - core) * width, width), width)


def scan(drive, lams, keep_ref, which, steps, reverse, start, visit):
    order = range(steps - 1, -1, -1) if reverse else range(steps)
    state = dict(start)
    for s in order:
        for row in range(2):
            at = s * SLAB + row * CHUNKS
            keep = keep_ref[which, at : at + CHUNKS, :]
            for half in range(2):
                lr, li = lams[half]
                hr, hi = state[half, row]
                hr, hi = keep * hr, keep * hi
                dr, di = drive(s, row, half)
                state[half, row] = (lr * hr - li * hi + dr, lr * hi + li * hr + di)
        visit(s, state, keep_ref)
    return state


def keep_products(keep_ref, which, steps):
    out = []
    for row in range(2):
        total = keep_ref[which, row * CHUNKS : (row + 1) * CHUNKS, :]
        for s in range(1, steps):
            at = s * SLAB + row * CHUNKS
            total = total * keep_ref[which, at : at + CHUNKS, :]
        out.append(total)
    return out


def chunk_scan(ends, keeps, powers, reverse, comp_ref, packed):
    index = lax.broadcasted_iota(jnp.int32, (CHUNKS, 128), 0)

    def shifted(value, by, fill):
        turned = pltpu.roll(value, CHUNKS - by if reverse else by, 0)
        valid = index < CHUNKS - by if reverse else index >= by
        return jnp.where(valid, turned, fill)

    for half in range(2):
        for row in range(2):
            er, ei = ends[half, row]
            pr, pi = powers[half][0] * keeps[row], powers[half][1] * keeps[row]
            for by in (1, 2, 4):
                tr, ti = cmul(pr, pi, shifted(er, by, 0.0), shifted(ei, by, 0.0))
                er, ei = er + tr, ei + ti
                pr, pi = cmul(pr, pi, shifted(pr, by, 1.0), shifted(pi, by, 0.0))
            edge = 0 if reverse else CHUNKS - 1
            q = row * 2 + half
            packed[q : q + 1, :] = er[edge : edge + 1, :]
            packed[4 + q : 5 + q, :] = ei[edge : edge + 1, :]
            base = (half * 2 + row) * 4
            comp_ref[base] = shifted(er, 1, 0.0)
            comp_ref[base + 1] = shifted(ei, 1, 0.0)
            comp_ref[base + 2] = shifted(pr, 1, 1.0)
            comp_ref[base + 3] = shifted(pi, 1, 0.0)


def device_carry(me, peers, got, held, dk_ref, which, own, oth, base, conj, reverse, packed):
    got_ref = arrange(got, held)
    index = lax.broadcasted_iota(jnp.int32, (CHUNKS, 128), 0)
    is_own = index % 2 == 0
    sign = jnp.where(index < 4, -1.0, 1.0) * (-1.0 if conj else 1.0)
    ar = jnp.where(is_own, wide(own[base + 11 : base + 12, :]), wide(oth[base + 11 : base + 12, :]))
    ai = jnp.where(is_own, wide(own[base + 12 : base + 13, :]), wide(oth[base + 12 : base + 13, :]))
    ai = ai * sign

    def step(k, held):
        at = peers - 1 - k if reverse else k
        reached = at > me if reverse else at < me
        new = dk_ref[which, at] * (ar * held + ai * pltpu.roll(held, 4, 0)) + got_ref[at]
        return jnp.where(reached, new, held)

    packed[...] = lax.fori_loop(0, peers, step, jnp.zeros((8, 128), f32), unroll=peers <= 16)


def entries(comp_ref, packed):
    start = {}
    for half in range(2):
        for row in range(2):
            base, q = (half * 2 + row) * 4, row * 2 + half
            hr, hi = wide(packed[q : q + 1, :]), wide(packed[4 + q : 5 + q, :])
            tr, ti = cmul(comp_ref[base + 2], comp_ref[base + 3], hr, hi)
            start[half, row] = (comp_ref[base] + tr, comp_ref[base + 1] + ti)
    return start


def decay(own, oth, base, at, conj=False):
    sign = -1.0 if conj else 1.0
    return [(wide(r[base + at : base + at + 1, :]), sign * wide(r[base + at + 1 : base + at + 2, :])) for r in (own, oth)]


def scales(own, oth, base):
    return [wide(r[base + 8 : base + 9, :]) for r in (own, oth)]


def nothing(*_):
    return None


def zeros_start():
    zero = jnp.zeros((CHUNKS, 128), f32)
    return {(half, row): (zero, zero) for half in range(2) for row in range(2)}


def part(s, row):
    at = s * SLAB + row * CHUNKS
    return slice(at, at + CHUNKS)


def cols(half, im):
    at = half * 256 + im * 128
    return slice(at, at + 128)


def flat_rows(ref):
    value = ref[...]
    return value.reshape(value.shape[0] * value.shape[1], value.shape[2])


def spread(out_ref, packed):
    value = packed[...]
    out_ref[...] = value if len(out_ref.shape) == 2 else jnp.broadcast_to(value[None], out_ref.shape)


def arrange(got, held):
    if len(got) == 1:
        return got[0]
    me = place()[0]
    for m, block in enumerate(got):
        for e in range(4):
            held[(((me >> 2) ^ m) << 2) + ((me & 3) ^ e)] = block[e]
    return held


def place():
    return lax.axis_index("seq"), lax.axis_index("state")


def stats_kernel(tokens, stats):
    s1 = s2 = 0.0
    for r in range(tokens.shape[0]):
        x = tokens[r].astype(f32)
        s1 = s1 + jnp.sum(x, axis=0, keepdims=True)
        s2 = s2 + jnp.sum(x * x, axis=0, keepdims=True)
    for i in range(2):
        stats[0, i : i + 1, :] = s1[:, 128 * i : 128 * (i + 1)]
        stats[0, 2 + i : 3 + i, :] = s2[:, 128 * i : 128 * (i + 1)]
    stats[...] = jnp.broadcast_to(stats[0][None], stats.shape)


def prep_kernel(peers, steps, span, pos, raw, small, keep, dk, perm):
    seq, core = place()
    docs = pos.shape[1]

    count = perm.shape[1]
    p = lax.broadcasted_iota(jnp.int32, (count, count), 0)
    q = lax.broadcasted_iota(jnp.int32, (count, count), 1)
    source = ((p >> 3) & 1) * span + (p & 7) * steps + (p >> 4)
    perm[0] = jnp.where(q == source, 1.0, 0.0).astype(bf16)
    source = ((q >> 3) & 1) * span + (q & 7) * steps + (q >> 4)
    perm[1] = jnp.where(p == source, 1.0, 0.0).astype(bf16)

    small[...] = jnp.zeros_like(small)
    for k in range(2):
        at = 16 * k
        values = raw[k : k + 1, :]
        for j in range(6):
            small[at + j : at + j + 1, :] = values[:, 128 * j : 128 * (j + 1)]
        rate = jnp.exp(values[:, 768:896])
        angle = jnp.exp(values[:, 896:])
        modulus = jnp.exp(-rate)
        lr, li = modulus * jnp.cos(angle), modulus * jnp.sin(angle)
        small[at + 6 : at + 7, :] = lr
        small[at + 7 : at + 8, :] = li
        small[at + 8 : at + 9, :] = jnp.sqrt(1.0 - modulus * modulus)
        power = 1
        while power < span:
            lr, li = cmul(lr, li, lr, li)
            power *= 2
            if power == steps:
                small[at + 9 : at + 10, :] = lr
                small[at + 10 : at + 11, :] = li
        small[at + 11 : at + 12, :] = lr
        small[at + 12 : at + 13, :] = li

    chunk = lax.broadcasted_iota(jnp.int32, (CHUNKS, 128), 0) * steps + seq * span
    for row in range(2):
        targets = [pos[core * 2 + row, d] - chunk for d in range(docs)]
        for s in range(steps + 1):
            hit = targets[0] == s
            for t in targets[1:]:
                hit = jnp.logical_or(hit, t == s)
            value = jnp.where(hit, 0.0, 1.0)
            at = s * SLAB + row * CHUNKS
            if s < steps:
                keep[0, at : at + CHUNKS, :] = value
            if s >= 1:
                keep[1, at - SLAB : at - SLAB + CHUNKS, :] = value

    first_row = (lax.broadcasted_iota(jnp.int32, (CHUNKS, 128), 0) // 2) % 2 == 0
    owners = ([], [])
    for d in range(docs):
        a, b = pos[core * 2, d], pos[core * 2 + 1, d]
        owners[0].append(jnp.where(first_row, a // span, b // span))
        owners[1].append(jnp.where(first_row, (a + span - 1) // span - 1, (b + span - 1) // span - 1))

    def mark(j, _):
        for m in range(2):
            hit = owners[m][0] == j
            for o in owners[m][1:]:
                hit = jnp.logical_or(hit, o == j)
            dk[m, j] = jnp.where(hit, 0.0, 1.0)
        return 0

    lax.fori_loop(0, peers, mark, 0)


def norm_rows(total, squares, count, core, own, oth, base, nrm):
    mean = total / count
    inv = lax.rsqrt(squares / count - mean * mean + norm_eps)
    nrm[0:1, :] = mean
    nrm[1:2, :] = inv
    nrm[2:3, :] = channel_row(core, own, oth, base)
    nrm[3:4, :] = channel_row(core, own, oth, base + 2)
    nrm[4:5, :] = channel_row(core, own, oth, base + 4)
    nrm[5:8, :] = jnp.zeros_like(nrm[5:8, :])


def normalized(x, nrm):
    xhat = (x - nrm[0:1, :]) * nrm[1:2, :]
    return xhat, xhat * nrm[2:3, :] + nrm[3:4, :]


def project_and_scan(steps, base, which, reverse, own, oth, keep, win_own, win_oth, nl, proj, comp, summ, packed):
    proj[:, :256] = mm(nl[...], win_own[...])
    proj[:, 256:] = mm(nl[...], win_oth[...])
    lams, sc = decay(own, oth, base, 6), scales(own, oth, base)

    def drive(s, row, half):
        return sc[half] * proj[part(s, row), cols(half, 0)], sc[half] * proj[part(s, row), cols(half, 1)]

    ends = scan(drive, lams, keep, which, steps, reverse, zeros_start(), nothing)
    chunk_scan(ends, keep_products(keep, which, steps), decay(own, oth, base, 9), reverse, comp, packed)
    spread(summ, packed)


def enter_first_kernel(peers, steps, count, got, x_own, x_oth, perm, own, oth, keep, win_own, win_oth,
                       xp, nl, proj, comp, summ, nrm, packed):
    _, core = place()
    sums = got[0:2]
    for j in range(1, peers):
        sums = sums + got[2 * j : 2 * j + 2]
    total = jnp.concatenate([sums[0, 0:1], sums[0, 1:2], sums[1, 0:1], sums[1, 1:2]], axis=1)
    squares = jnp.concatenate([sums[0, 2:3], sums[0, 3:4], sums[1, 2:3], sums[1, 3:4]], axis=1)
    norm_rows(total, squares, count, core, own, oth, 0, nrm)
    xp[:, own_cols(core, 256)] = mm(perm[0], flat_rows(x_own)).astype(bf16)
    xp[:, oth_cols(core, 256)] = mm(perm[0], flat_rows(x_oth)).astype(bf16)
    _, normed = normalized(xp[...].astype(f32), nrm)
    nl[...] = normed.astype(bf16)
    project_and_scan(steps, 0, 0, False, own, oth, keep, win_own, win_oth, nl, proj, comp, summ, packed)


def sum_peers(got):
    if len(got) == 1 and len(got[0].shape) == 3:
        got = [got[0].at[j] for j in range(got[0].shape[0])]
    total = got[0][...]
    for part in got[1:]:
        total = total + part[...]
    return total


def enter_second_kernel(peers, steps, count, got, x, own, oth, keep, win_own, win_oth,
                        nl, proj, comp, summ, nrm, packed):
    _, core = place()
    sums = sum_peers(got)
    norm_rows(row_of_tiles(sums[0:4]), row_of_tiles(sums[4:8]), count, core, own, oth, 16, nrm)
    _, normed = normalized(x[...], nrm)
    nl[...] = normed.astype(bf16)
    project_and_scan(steps, 16, 1, True, own, oth, keep, win_own, win_oth, nl, proj, comp, summ, packed)


def states_of(peers, steps, base, which, reverse, got, comp, dk, own, oth, keep, proj, cin, sl, packed, held):
    device_carry(place()[0], peers, got, held, dk, which, own, oth, base, False, reverse, packed)
    start = entries(comp, packed)
    lams, sc = decay(own, oth, base, 6), scales(own, oth, base)
    for (half, row), (hr, hi) in start.items():
        cin[part(0, row), cols(half, 0)] = hr
        cin[part(0, row), cols(half, 1)] = hi

    def drive(s, row, half):
        return sc[half] * proj[part(s, row), cols(half, 0)], sc[half] * proj[part(s, row), cols(half, 1)]

    def visit(s, state, _):
        for half in range(2):
            for im in range(2):
                both = jnp.concatenate([state[half, row][im] for row in range(2)], axis=0)
                sl[s * SLAB : (s + 1) * SLAB, cols(half, im)] = both.astype(bf16)

    scan(drive, lams, keep, which, steps, reverse, start, visit)


def mix_and_gate(core, x, nrm, sl, wout_own, wout_oth, lin_own, lin_oth, gate_own, gate_oth, gp, act, sig, qv, y):
    c = 0.7978845608028654
    for i in range(0, y.shape[0], TILE):
        rows = slice(i, i + TILE)
        _, normed = normalized(x[rows, :].astype(f32), nrm)
        mixed = mm(sl[rows, :256], wout_own[...]) + mm(sl[rows, 256:], wout_oth[...]) + nrm[4:5, :] * normed
        sq = mixed * mixed
        t = jnp.tanh(mixed * (c + (c * 0.044715) * sq))
        upper = 0.5 + 0.5 * t
        low = (mixed * upper).astype(bf16)
        act[rows, :] = low
        gp[rows, :] = (upper + mixed * (upper * (1.0 - t)) * (c + (3 * c * 0.044715) * sq)).astype(gp.dtype)
        for w_lin, w_gate, at in ((lin_own, gate_own, own_cols(core, 256)), (lin_oth, gate_oth, oth_cols(core, 256))):
            linear = mm(low, w_lin[...])
            gating = mm(low, w_gate[...])
            sg = 0.5 + 0.5 * jnp.tanh(0.5 * gating)
            out = linear * sg
            sig[rows, at] = sg.astype(sig.dtype)
            qv[rows, at] = (out * (1.0 - sg)).astype(qv.dtype)
            y[rows, at] = x[rows, at].astype(f32) + out
        yield rows


def leave_first_kernel(peers, steps, got, comp, dk, own, oth, keep, proj, x, nrm, wout_own, wout_oth,
                       lin_own, lin_oth, gate_own, gate_oth, cin, sl, gp, act, sig, qv, y, stats, packed, held):
    states_of(peers, steps, 0, 0, False, got, comp, dk, own, oth, keep, proj, cin, sl, packed, held)
    s1 = s2 = 0.0
    for rows in mix_and_gate(place()[1], x, nrm, sl, wout_own, wout_oth, lin_own, lin_oth, gate_own, gate_oth, gp, act, sig, qv, y):
        out = y[rows, :]
        s1, s2 = s1 + jnp.sum(out, axis=0, keepdims=True), s2 + jnp.sum(out * out, axis=0, keepdims=True)
    pack_two(s1, s2, packed)
    spread(stats, packed)


def pack_two(a, b, packed):
    for i in range(4):
        packed[i : i + 1, :] = a[:, 128 * i : 128 * (i + 1)]
        packed[4 + i : 5 + i, :] = b[:, 128 * i : 128 * (i + 1)]


def glu_backward(steps, base, adj_which, adj_reverse, core, d_out, nrm, x, gp, sig, qv, own, oth, keep, wout_own, wout_oth,
                 lin_own, lin_oth, gate_own, gate_oth, skip_row, dst, comp, summ, packed, dl, dg, dml):
    mine, other = own_cols(core, 256), oth_cols(core, 256)
    total = 0.0
    for i in range(0, dl.shape[0], TILE):
        rows = slice(i, i + TILE)
        grad = d_out(rows)
        dl[rows, :] = (grad * sig[rows, :].astype(f32)).astype(bf16)
        dg[rows, :] = (grad * qv[rows, :].astype(f32)).astype(bf16)
        d_active = (mm_nt(dl[rows, mine], lin_own[...]) + mm_nt(dg[rows, mine], gate_own[...])
                    + mm_nt(dl[rows, other], lin_oth[...]) + mm_nt(dg[rows, other], gate_oth[...]))
        d_mixed = d_active * gp[rows, :].astype(f32)
        _, normed = normalized(x[rows, :].astype(f32), nrm)
        total = total + jnp.sum(d_mixed * normed, axis=0, keepdims=True)
        low = d_mixed.astype(bf16)
        dml[rows, :] = low
        dst[rows, :256] = mm_nt(low, wout_own[...])
        dst[rows, 256:] = mm_nt(low, wout_oth[...])
    skip_row[0:1, :] = total
    lams = decay(own, oth, base, 6, conj=True)

    def drive(s, row, half):
        return dst[part(s, row), cols(half, 0)], dst[part(s, row), cols(half, 1)]

    ends = scan(drive, lams, keep, adj_which, steps, adj_reverse, zeros_start(), nothing)
    chunk_scan(ends, keep_products(keep, adj_which, steps), decay(own, oth, base, 9, conj=True), adj_reverse, comp, packed)
    spread(summ, packed)


def mixer_grads(act, dl, dg, sl, dml, l_own, l_oth, g_own, g_oth):
    _, core = place()
    mine, other = own_cols(core, 256), oth_cols(core, 256)
    left = act[...].T
    l_own[...] = mm(left, dl[:, mine]).astype(bf16)
    l_oth[...] = mm(left, dl[:, other]).astype(bf16)
    g_own[0:512, :] = mm(left, dg[:, mine]).astype(bf16)
    g_oth[0:512, :] = mm(left, dg[:, other]).astype(bf16)
    for ref, cut in ((g_own, slice(0, 256)), (g_oth, slice(256, 512))):
        left = sl[:, cut].T
        for i in range(2):
            ref[512 + 256 * i : 768 + 256 * i, :] = mm(left, dml[:, 256 * i : 256 * (i + 1)]).astype(ref.dtype)


def in_grads(nl, dp, g_own, g_oth):
    left = nl[...].T
    g_own[...] = mm(left, dp[:, :256]).astype(bf16)
    g_oth[...] = mm(left, dp[:, 256:]).astype(bf16)


def turn_kernel(peers, steps, got, comp_in, dk, own, oth, keep, proj, x, nrm, wout_own, wout_oth,
                lin_own, lin_oth, gate_own, gate_oth, perm, cot_own, cot_oth,
                cin, result, d_out, act, dl, dg, sl, dml, skip_row, dst, comp, summ,
                packed, held, gp, sig, qv, y):
    _, core = place()
    states_of(peers, steps, 16, 1, True, got, comp_in, dk, own, oth, keep, proj, cin, sl, packed, held)
    for _ in mix_and_gate(core, x, nrm, sl, wout_own, wout_oth, lin_own, lin_oth, gate_own, gate_oth, gp, act, sig, qv, y):
        pass
    result[...] = y[...].astype(bf16)
    d_out[:, own_cols(core, 256)] = mm(perm[0], flat_rows(cot_own)).astype(bf16)
    d_out[:, oth_cols(core, 256)] = mm(perm[0], flat_rows(cot_oth)).astype(bf16)
    glu_backward(steps, 16, 0, False, core, lambda rows: d_out[rows, :].astype(f32), nrm, x, gp, sig, qv, own, oth, keep, wout_own, wout_oth,
                 lin_own, lin_oth, gate_own, gate_oth, skip_row, dst, comp, summ, packed, dl, dg, dml)


def adjoint_part(peers, steps, base, keep_which, adj_which, adj_reverse, got, comp, dk, own, oth, keep, nl, x, nrm,
                 cin, sl, dst, dml, win_own, win_oth, skip_row, small_own, small_oth, all_rows, packed, held, proj, dp, keep_tile):
    _, core = place()
    device_carry(place()[0], peers, got, held, dk, adj_which, own, oth, base, True, adj_reverse, packed)
    start = entries(comp, packed)
    lams, sc = decay(own, oth, base, 6, conj=True), scales(own, oth, base)
    zero = jnp.zeros((CHUNKS, 128), f32)
    acc = {half: [zero, zero, zero] for half in range(2)}
    proj[:, :256] = mm(nl[...], win_own[...])
    proj[:, 256:] = mm(nl[...], win_oth[...])

    def prior(s, half, im):
        before = s - 1 if adj_reverse else s + 1
        if 0 <= before < steps:
            return sl[before * SLAB : (before + 1) * SLAB, cols(half, im)].astype(f32)
        return cin[:, cols(half, im)]

    def drive(s, row, half):
        return dst[part(s, row), cols(half, 0)], dst[part(s, row), cols(half, 1)]

    def visit(s, state, _):
        for half in range(2):
            prior_re, prior_im = prior(s, half, 0), prior(s, half, 1)
            for row in range(2):
                ar, ai = state[half, row]
                pr, pi = prior_re[part(0, row)], prior_im[part(0, row)]
                keep_here = keep[keep_which, part(s, row), :]
                acc[half][0] = acc[half][0] + keep_here * (ar * pr + ai * pi)
                acc[half][1] = acc[half][1] + keep_here * (ai * pr - ar * pi)
                acc[half][2] = acc[half][2] + (ar * proj[part(s, row), cols(half, 0)] + ai * proj[part(s, row), cols(half, 1)])
            for im in range(2):
                both = jnp.concatenate([sc[half] * state[half, row][im] for row in range(2)], axis=0)
                dp[s * SLAB : (s + 1) * SLAB, cols(half, im)] = both.astype(bf16)

    scan(drive, lams, keep, adj_which, steps, adj_reverse, start, visit)

    bias_row = gain_row = 0.0
    for i in range(0, dp.shape[0], TILE):
        rows = slice(i, i + TILE)
        d_normed = dml[rows, :].astype(f32) * nrm[4:5, :] + mm_nt(dp[rows, :256], win_own[...]) + mm_nt(dp[rows, 256:], win_oth[...])
        xhat, _ = normalized(x[rows, :].astype(f32), nrm)
        bias_row = bias_row + jnp.sum(d_normed, axis=0, keepdims=True)
        gain_row = gain_row + jnp.sum(d_normed * xhat, axis=0, keepdims=True)
        keep_tile(rows, d_normed)
    pack_two(bias_row, gain_row, packed)

    wanted = (skip_row[0:1, :], bias_row, gain_row) if all_rows else (skip_row[0:1, :],)
    for ref, half in ((small_own, 0), (small_oth, 1)):
        ref[...] = jnp.zeros_like(ref)
        at = 0
        for row in wanted:
            pick = jnp.where(core == half, row[:, :256], row[:, 256:])
            ref[at : at + 1, :] = pick[:, :128]
            ref[at + 1 : at + 2, :] = pick[:, 128:]
            at += 2
        for j in range(3):
            ref[at + j : at + j + 1, :] = jnp.sum(acc[half][j], axis=0, keepdims=True)


def adjoint_second_kernel(peers, steps, got, comp, dk, own, oth, keep, nl, x, nrm, cin, sl, dst, dml, win_own, win_oth, skip_row, act, dl, dg,
                          g_own, g_oth, small_own, small_oth, dn, stats, packed, held, proj, dp):
    def keep_tile(rows, d_normed):
        dn[rows, :] = d_normed

    adjoint_part(peers, steps, 16, 1, 0, False, got, comp, dk, own, oth, keep, nl, x, nrm,
                 cin, sl, dst, dml, win_own, win_oth, skip_row, small_own, small_oth, False, packed, held, proj, dp, keep_tile)
    spread(stats, packed)
    mixer_grads(act, dl, dg, sl, dml, g_own.at[:512], g_oth.at[:512], g_own.at[512:1536], g_oth.at[512:1536])
    in_grads(nl, dp, g_own.at[1536:], g_oth.at[1536:])


def back_first_kernel(steps, count, got, dn, x2, nrm2, d_out2, own, oth, keep, x, nrm, gp, sig, qv,
                      wout_own, wout_oth, lin_own, lin_oth, gate_own, gate_oth,
                      act, sl, d_out, dml, totals, l_own, l_oth, g_own, g_oth, skip_row, dst, comp, summ, packed, dl, dg):
    sums = sum_peers(got)
    bias_row, gain_row = row_of_tiles(sums[0:4]), row_of_tiles(sums[4:8])
    totals[...] = jnp.zeros_like(totals)
    totals[0:1, :], totals[1:2, :] = bias_row, gain_row
    mean, inv, gain = nrm2[0:1, :], nrm2[1:2, :], nrm2[2:3, :]
    scaled, shift, slope = inv * gain, inv * gain * bias_row / count, inv * inv * gain * gain_row / count

    def d_in(rows):
        value = d_out2[rows, :].astype(f32) + scaled * dn[rows, :] - shift - slope * (x2[rows, :] - mean)
        d_out[rows, :] = value
        return value

    glu_backward(steps, 0, 1, True, place()[1], d_in, nrm, x, gp, sig, qv, own, oth, keep, wout_own, wout_oth,
                 lin_own, lin_oth, gate_own, gate_oth, skip_row, dst, comp, summ, packed, dl, dg, dml)
    mixer_grads(act, dl, dg, sl, dml, l_own, l_oth, g_own, g_oth)


def adjoint_first_kernel(peers, steps, got, comp, dk, own, oth, keep, nl, x, nrm, cin, sl, dst, dml, win_own, win_oth, skip_row,
                         d_out, small1_own, small1_oth,
                         g_own, g_oth, small_own, partial, packed, held, proj, dp, small_oth):
    _, core = place()
    scaled = nrm[1:2, :] * nrm[2:3, :]

    def keep_tile(rows, d_normed):
        partial[rows, :] = (d_out[rows, :] + scaled * d_normed).astype(bf16)

    adjoint_part(peers, steps, 0, 0, 1, True, got, comp, dk, own, oth, keep, nl, x, nrm,
                 cin, sl, dst, dml, win_own, win_oth, skip_row, small_own, small_oth, True, packed, held, proj, dp, keep_tile)
    small_own[9:14, :] = small1_own[0:5, :]
    small_oth[9:14, :] = small1_oth[0:5, :]
    in_grads(nl, dp, g_own, g_oth.at[:512])
    put_small(g_oth, 512, small_oth[...])


def order_kernel(perm, result, partial, own, oth):
    _, core = place()
    for i, ref in enumerate((result, partial)):
        own[i] = mm(perm[1], ref[:, own_cols(core, 256)]).astype(bf16)
        oth[i] = mm(perm[1], ref[:, oth_cols(core, 256)]).astype(bf16)


def finish_kernel(count, packed, totals1, mine_parts, other_parts, tokens, nrm, raw,
                  block_out, d_in, ngg, bias, skip, rate_grad, angle_grad):
    _, core = place()
    for ref, j in ((skip, 0), (bias, 2), (ngg, 4)):
        ref[0:1, :128], ref[0:1, 128:] = packed[j : j + 1, :], packed[j + 1 : j + 2, :]
    skip[1:2, :128], skip[1:2, 128:] = packed[9:10, :], packed[10:11, :]
    bias[1:2, :] = totals1[0:1, own_cols(core, 256)]
    ngg[1:2, :] = totals1[1:2, own_cols(core, 256)]
    for k, at in ((0, 6), (1, 11)):
        values = raw[k : k + 1, :]
        rate = jnp.exp(values[:, 768:896])
        angle = jnp.exp(values[:, 896:])
        modulus = jnp.exp(-rate)
        scale = jnp.sqrt(1.0 - modulus * modulus)
        cos, sin = jnp.cos(angle), jnp.sin(angle)
        dr, di, ds = (packed[at + j : at + j + 1, :] for j in range(3))
        g_mod = dr * cos + di * sin - ds * modulus / scale
        rate_grad[k : k + 1, :] = -g_mod * modulus * rate
        angle_grad[k : k + 1, :] = modulus * (di * cos - dr * sin) * angle
    mine = nrm[:, own_cols(core, 256)]
    mean, inv, gain = mine[0:1, :], mine[1:2, :], mine[2:3, :]
    bias_row, gain_row = bias[0:1, :], ngg[0:1, :]
    flat = inv * gain / count
    for r in range(4):
        block_out[r] = jnp.where(core == r // 2, mine_parts[0, r % 2], other_parts[0, r % 2])
        held_rows = jnp.where(core == r // 2, mine_parts[1, r % 2].astype(f32), other_parts[1, r % 2].astype(f32))
        xhat = (tokens[r].astype(f32) - mean) * inv
        d_in[r] = held_rows - flat * (bias_row + xhat * gain_row)


def swap(value):
    return lax.ppermute(value, "state", [(0, 1), (1, 0)])


def to_all(value, axes):
    peers = 1
    for a in axes:
        peers *= lax.axis_size(a)
    return lax.all_to_all(jnp.broadcast_to(value[None], (peers,) + value.shape), axes, 0, 0)


def blocking(value, axes, others):
    value, others = lax.optimization_barrier((value, others))
    got, others = lax.optimization_barrier((lax.all_to_all(value, axes, 0, 0), others))
    return (got,), others


def gather_seq(value):
    if lax.axis_size("seq") != 16:
        return (to_all(value, ("seq",)),)
    near = jnp.stack([value] + [partner(value, m) for m in (1, 2, 3)])
    return (near,) + tuple(partner(near, m) for m in (4, 8, 12))


def sum_all(value):
    if lax.axis_size("seq") != 16:
        return (to_all(value, ("seq", "state")),)
    value = value + swap(value)
    near = value + partner(value, 1) + partner(value, 2) + partner(value, 3)
    return (near,) + tuple(partner(near, m) for m in (4, 8, 12))


def partner(value, mask):
    size = lax.axis_size("seq")
    return lax.ppermute(value, "seq", [(i, i ^ mask) for i in range(size)])


def partners(value, masks):
    size = lax.axis_size("seq")
    return lax.ppermute(value, ("seq", "state"), [(2 * i + c, 2 * (i ^ masks[c]) + c) for i in range(size) for c in range(2)])


def tie(value, others):
    return lax.optimization_barrier((value, others))


def bit_of(masks):
    me, core = place()
    return (me // jnp.where(core == 0, masks[0], masks[1])) & 1


def put_small(out, at, value):
    high = value.astype(bf16)
    rest = value - high.astype(f32)
    middle = rest.astype(bf16)
    low = (rest - middle.astype(f32)).astype(bf16)
    out[at : at + 16, :128], out[at : at + 16, 128:] = high, middle
    out[at + 16 : at + 32, :128], out[at + 16 : at + 32, 128:] = low, jnp.zeros_like(low)


def get_small(ref, at):
    return (ref[at : at + 16, :128].astype(f32) + ref[at : at + 16, 128:].astype(f32)) + ref[at + 16 : at + 32, :128].astype(f32)


def first_halves_kernel(masks, pairs, small, mine, other):
    bit, at = bit_of(masks), 0
    for own, got in pairs:
        half = own.shape[0] // 2
        for out, which in ((mine, bit), (other, 1 - bit)):
            rows = pl.ds(pl.multiple_of(which * half, half), half)
            out[at : at + half, :] = (own[rows, :].astype(f32) + got[rows, :].astype(f32)).astype(bf16)
        at += half
    if small is not None:
        total = small[...] + get_small(pairs[-1][1], pairs[-1][0].shape[0])
        put_small(mine, at, total)
        put_small(other, at, total)


def next_halves_kernel(masks, extra, held, got, mine, other):
    bit, half = bit_of(masks), mine.shape[0] - extra
    for out, which in ((mine, bit), (other, 1 - bit)):
        rows = pl.ds(pl.multiple_of(which * half, half), half)
        out[:half, :] = (held[rows, :].astype(f32) + got[rows, :].astype(f32)).astype(bf16)
    if extra:
        total = get_small(held, 2 * half) + get_small(got, 2 * half)
        put_small(mine, half, total)
        put_small(other, half, total)


def add_kernel(extra, held, got, total, *small):
    rows = held.shape[0] - extra
    total[:rows, :] = (held[:rows, :].astype(f32) + got[:rows, :].astype(f32)).astype(bf16)
    if extra:
        value = get_small(held, rows) + get_small(got, rows)
        if small:
            small[0][...] = value
        else:
            put_small(total, rows, value)


def axes_orders(*orders):
    masks, m = [], 1
    while m < lax.axis_size("seq"):
        masks.append(m)
        m *= 2
    return list(zip(*[[masks[i] for i in o] + masks[4:] for o in orders]))


class SeqSum:
    def __init__(self, pairs, masks, small=None):
        self.masks, self.at, self.small, self.extra = masks, 0, (), 0 if small is None else 32
        rows = sum(a.shape[0] for a, _ in pairs) // 2 + self.extra
        shape = ((rows, pairs[0][0].shape[1]), bf16)
        flat = tuple(v for p in pairs for v in p) + (() if small is None else (small,))

        def kernel(refs, mine, other):
            count = 2 * len(pairs)
            first_halves_kernel(masks[0], [(refs[i], refs[i + 1]) for i in range(0, count, 2)],
                                None if small is None else refs[count], mine, other)

        self.mine, self.send = run(kernel, [shape, shape], (flat,))

    def step(self):
        count, i = len(self.masks), self.at
        self.at += 1
        if i < count:
            got = partners(self.send, self.masks[i])
            rows, width = got.shape
            rows -= self.extra
            if i + 2 < count:
                shape = ((rows // 2 + self.extra, width), bf16)
                self.mine, self.send = run(functools.partial(next_halves_kernel, self.masks[i + 1], self.extra), [shape, shape], (self.mine, got))
            elif i + 2 == count:
                (self.send,) = run(functools.partial(add_kernel, self.extra), [((rows + self.extra, width), bf16)], (self.mine, got))
            else:
                outs = [((rows, width), bf16)] + ([((16, 128), f32)] if self.extra else [])
                self.send, *self.small = run(functools.partial(add_kernel, self.extra), outs, (self.send, got))
            return False
        mask = self.masks[2 * count - 2 - i]
        got = partners(self.send, mask)
        if i + 2 == 2 * count:
            self.result = (self.send, got)
            return True
        bit = bit_of(mask)
        self.send = jnp.concatenate([jnp.where(bit == 0, self.send, got), jnp.where(bit == 0, got, self.send)], axis=0)
        return False

    def after(self, values):
        self.send = tie(self.send, values)[0]

    def before(self, value):
        value, self.send = tie(value, self.send)
        return value


class Leaving:
    def __init__(self, sem):
        self.sem, self.copies = sem, []

    def send(self, source, target):
        copy = pltpu.make_async_copy(source, target, self.sem.at[len(self.copies)])
        copy.start()
        self.copies.append(copy)

    def wait(self):
        for copy in self.copies:
            copy.wait()


def put_entry(entry, ref, at, start, rows):
    value = ref[at : at + rows, :].astype(f32)
    entry[pl.ds(2 * start, rows, stride=2), :] = value[:, :128]
    entry[pl.ds(2 * start + 1, rows, stride=2), :] = value[:, 128:]


def on_half(mine, got, masks, half, put):
    bit = bit_of(masks)
    for ref, which in ((mine, bit), (got, 1 - bit)):

        @pl.when(which == half)
        def _():
            put(ref, lambda at, rows: ref[at : at + rows, :].astype(f32))


def unpack_second_kernel(masks, mine, got, lin_out, gate_out, out_out, entry_out, lin, gate, out, entry, sem):
    leaving = Leaving(sem)

    def low(ref, piece):
        lin[1], gate[...], lin[0, :256] = piece(0, 512), piece(512, 512), piece(1024, 256)

    def high(ref, piece):
        out[:, :256], out[:, 256:], lin[0, 256:] = piece(0, 256), piece(256, 256), piece(1024, 256)
        put_entry(entry, ref, 512, 0, 512)

    on_half(mine, got, masks, 0, low)
    leaving.send(gate, gate_out.at[1])
    on_half(mine, got, masks, 1, high)
    leaving.send(lin, lin_out)
    leaving.send(out, out_out.at[1])
    leaving.send(entry, entry_out.at[1])
    leaving.wait()


def unpack_first_kernel(masks, mine, got, gate_in, out_in, entry_in, gate_out, out_out, entry_out, gate, out, entry, sem):
    leaving = Leaving(sem)

    def low(ref, piece):
        gate[...] = piece(0, 512)
        put_entry(entry, ref, 512, 0, 256)

    def high(ref, piece):
        out[:, :256], out[:, 256:] = piece(0, 256), piece(256, 256)
        put_entry(entry, ref, 512, 256, 256)

    on_half(mine, got, masks, 0, low)
    leaving.send(gate, gate_out.at[0])
    on_half(mine, got, masks, 1, high)
    leaving.send(out, out_out.at[0])
    leaving.send(entry, entry_out.at[0])
    leaving.wait()


def unpack(second, second_masks, first, first_masks):
    far, near = pl.BlockSpec(memory_space=pltpu.HBM), pl.BlockSpec(memory_space=pltpu.VMEM)
    lin, gate, out, entry = (jax.ShapeDtypeStruct(s, f32) for s in ((2, 512, 256), (2, 512, 256), (2, 256, 512), (2, 1024, 128)))
    parts = [pltpu.VMEM(a.shape[1:], f32) for a in (gate, out, entry)]
    params = pltpu.CompilerParams(vmem_limit_bytes=24 * 2**20)
    lin_grad, *rest = pl.pallas_call(
        functools.partial(unpack_second_kernel, second_masks),
        out_shape=[lin, gate, out, entry], in_specs=[near] * 2, out_specs=[far] * 4,
        scratch_shapes=[pltpu.VMEM(lin.shape, f32)] + parts + [pltpu.SemaphoreType.DMA((4,))],
        compiler_params=params)(*second)
    rest = pl.pallas_call(
        functools.partial(unpack_first_kernel, first_masks),
        out_shape=[gate, out, entry], in_specs=[near] * 2 + [far] * 3, out_specs=[far] * 3,
        scratch_shapes=parts + [pltpu.SemaphoreType.DMA((3,))],
        input_output_aliases={2: 0, 3: 1, 4: 2},
        compiler_params=params)(*first, *rest)
    return [lin_grad, *rest]


class Far:
    def __init__(self, value, at=None, smem=False):
        self.value, self.at, self.smem = value, at, smem
        self.shape = value.shape if at is None else value.shape[1:] if at != "rows" else (2,) + value.shape[1:]

    def source(self, ref):
        if self.at is None:
            return ref
        return ref.at[pl.ds(lax.axis_index("state") * 2, 2)] if self.at == "rows" else ref.at[self.at]


class Part:
    def __init__(self, value, at):
        self.value, self.at = value, at

    def view(self, ref):
        return ref.at[pl.ds(lax.axis_index("state") * 2, 2)] if self.at == "rows" else ref.at[self.at]


class Held:
    def __init__(self, source, ref, sem):
        self.ref, self.copy, self.shape, self.dtype = ref, pltpu.make_async_copy(source, ref, sem), ref.shape, ref.dtype
        self.copy.start()

    def ready(self):
        if self.copy is not None:
            self.copy.wait()
            self.copy = None

    def __getitem__(self, index):
        self.ready()
        return self.ref[index]


def run(kernel, outs, groups, scratch=(), limit=24, flops=0):
    args = [a for g in groups for a in (g if isinstance(g, tuple) else (g,))]
    far_in = [i for i, a in enumerate(args) if isinstance(a, Far)]
    arrays = [a.value if isinstance(a, (Far, Part)) else a for a in args]
    moved = sum(a.size * a.dtype.itemsize for a in arrays)

    def whole(*refs):
        ins, results = list(refs[: len(args)]), list(refs[len(args) : len(args) + len(outs)])
        rest = refs[len(args) + len(outs) :]
        own = rest[: len(scratch)]
        if far_in:
            buffers, sem = rest[len(scratch) : -1], rest[-1]
        for j, i in enumerate(far_in):
            ins[i] = Held(args[i].source(ins[i]), buffers[j], sem.at[j])
        ins = [a.view(r) if isinstance(a, Part) else r for r, a in zip(ins, args)]
        grouped, at = [], 0
        for g in groups:
            if isinstance(g, tuple):
                grouped.append(tuple(ins[at : at + len(g)]))
                at += len(g)
            else:
                grouped.append(ins[at])
                at += 1
        kernel(*grouped, *results, *own)
        for i in far_in:
            ins[i].ready()

    def space(far):
        return pl.BlockSpec(memory_space=pltpu.HBM if far else pltpu.VMEM)

    held = [(pltpu.SMEM if args[i].smem else pltpu.VMEM)(args[i].shape, args[i].value.dtype) for i in far_in]
    if held:
        held.append(pltpu.SemaphoreType.DMA((len(held),)))
    return pl.pallas_call(
        whole,
        out_shape=[jax.ShapeDtypeStruct(o[0], o[1]) for o in outs],
        in_specs=[space(isinstance(a, Far)) for a in args],
        out_specs=[space(False)] * len(outs),
        scratch_shapes=[pltpu.VMEM(*s) for s in scratch] + held,
        compiler_params=pltpu.CompilerParams(vmem_limit_bytes=limit * 2**20),
        cost_estimate=pl.CostEstimate(flops=flops, bytes_accessed=moved, transcendentals=0),
    )(*arrays)


def body(tokens, gain, bias, in_proj, out_proj, rate_log, angle_log, skip, glu_lin, glu_gate, positions, cotangent):
    peers = lax.axis_size("seq")
    core = lax.axis_index("state")
    rows, span, width = tokens.shape
    steps = span // CHUNKS
    n = 2 * span
    count = float(rows * span * peers)
    packed = ((8, 128), f32)
    one = 2 * n * 512 * 512
    low = ((n, 512), bf16)
    full = ((n, 512), f32)

    (stats,) = run(stats_kernel, [((2 * peers, 4, 128), f32)], (tokens,))
    raw, at = 0.0, 0
    for v in (gain, bias, skip, rate_log, angle_log):
        raw, at = raw + jnp.pad(v.astype(f32), ((0, 0), (at, 1024 - at - v.shape[1]))), at + v.shape[1]
    w_in = in_proj.reshape(2, 512, 256)
    w_out = out_proj.reshape(2, 256, 512)
    x_oth, cot_oth, in_oth, out_oth, lin_oth, gate_oth = (swap(w) for w in (tokens, cotangent, w_in, w_out, glu_lin, glu_gate))
    enter = [(Part(w_in, k), Part(in_oth, k)) for k in range(2)]
    own, keep, dk, perm = run(
        functools.partial(prep_kernel, peers, steps, span),
        [((32, 128), f32), ((2, n, 128), f32), ((2, peers, 8, 128), f32), ((2, n, n), bf16)],
        (Far(positions, smem=True), raw))
    oth = swap(own)
    ordered = ((peers, 8, 128), f32)

    for_seq, for_all = ((peers, 8, 128), f32), ((2 * peers, 8, 128), f32)
    scan_outs = [full, ((16, 8, 128), f32), for_seq, ((8, 512), f32)]
    xp, nl0, proj, comp, summ, nrm0 = run(
        functools.partial(enter_first_kernel, peers, steps, count), [low, low] + scan_outs,
        (lax.all_to_all(stats, ("seq", "state"), 0, 0), Part(tokens, "rows"), Part(x_oth, "rows"), perm, own, oth, keep) + enter[0], [packed], flops=2 * one)
    got, (cot_oth, out_oth, lin_oth, gate_oth) = blocking(summ, "seq", (cot_oth, out_oth, lin_oth, gate_oth))
    glu = [tuple((Part if i % 2 else Part)(w, k) for i, w in enumerate((w_out, out_oth, glu_lin, lin_oth, glu_gate, gate_oth))) for k in range(2)]
    cin0, sl0, gp0, act0, sig0, qv0, y0, stats = run(
        functools.partial(leave_first_kernel, peers, steps),
        [((SLAB, 512), f32), low, low, low, low, low, full, for_all],
        (got, comp, dk, own, oth, keep, proj, xp, nrm0) + glu[0], [packed, ordered], flops=3 * one)
    got, _ = blocking(stats, ("seq", "state"), ())
    nl1, proj, comp, summ, nrm1 = run(
        functools.partial(enter_second_kernel, peers, steps, count), [low] + scan_outs,
        (got, y0, own, oth, keep) + enter[1], [packed], flops=one)
    got, _ = blocking(summ, "seq", ())
    turn_outs = [((8, 512), f32), full, ((16, 8, 128), f32)]
    cin1, result, d_out1, act1, dl1, dg1, sl1, dml1, skip1, dst, comp, summ = run(
        functools.partial(turn_kernel, peers, steps),
        [((SLAB, 512), f32), low, low, low, low, low, low, low] + turn_outs + [for_seq],
        (got, comp, dk, own, oth, keep, proj, y0, nrm1) + glu[1] + (perm, Part(cotangent, "rows"), Part(cot_oth, "rows")),
        [packed, ordered, full, full, full, full], flops=8 * one)
    got, _ = blocking(summ, "seq", ())
    g1_own, g1_oth, s1_own, s1_oth, dn, stats = run(
        functools.partial(adjoint_second_kernel, peers, steps),
        [((2048, 256), bf16), ((2048, 256), bf16), ((8, 128), f32), ((8, 128), f32), full, for_all],
        (got, comp, dk, own, oth, keep, nl1, y0, nrm1, cin1, sl1, dst, dml1) + enter[1] + (skip1, act1, dl1, dg1),
        [packed, ordered, full, low], flops=6 * one)
    got, (g1_oth,) = blocking(stats, ("seq", "state"), (g1_oth,))
    g1_got = swap(g1_oth)
    d_out0, dml0, totals1, l0_own, l0_oth, g0_own, g0_oth, skip0, dst, comp, summ = run(
        functools.partial(back_first_kernel, steps, count),
        [full, low, ((8, 512), f32), ((512, 256), bf16), ((512, 256), bf16), ((1024, 256), bf16), ((1024, 256), bf16)] + turn_outs + [for_seq],
        (got, dn, y0, nrm1, d_out1, own, oth, keep, xp, nrm0, gp0, sig0, qv0) + glu[0] + (act0, sl0),
        [packed, low, low], flops=6 * one)
    got, (l0_oth, g0_oth, g1_got, result) = blocking(summ, "seq", (l0_oth, g0_oth, g1_got, result))
    l0_got, g0_got = swap(l0_oth), swap(g0_oth)
    i0_own, i0_oth, s_own, partial = run(
        functools.partial(adjoint_first_kernel, peers, steps),
        [((512, 256), bf16), ((544, 256), bf16), ((16, 128), f32), low],
        (got, comp, dk, own, oth, keep, nl0, xp, nrm0, cin0, sl0, dst, dml0) + enter[0]
        + (skip0, d_out0, s1_own, s1_oth),
        [packed, ordered, full, low, ((16, 128), f32)], flops=3 * one)
    i0_got = swap(i0_oth)
    bulk1 = SeqSum([(g1_own, g1_got), (l0_own, l0_got)], axes_orders((0, 1, 2, 3), (1, 0, 2, 3)))
    bulk0 = SeqSum([(g0_own, g0_got), (i0_own, i0_got)], axes_orders((2, 1, 0, 3), (2, 0, 1, 3)), s_own)
    own_parts, oth_parts = run(order_kernel, [((2, n, 256), bf16)] * 2, (perm, result, partial), flops=2 * one)
    got_parts = swap(oth_parts)
    for bulk in (bulk1, bulk0):
        while not bulk.step():
            pass
    quad = (2, 2, span, width)
    block_out, d_in, ngg, bias_grad, skip_grad, rate_grad, angle_grad = run(
        functools.partial(finish_kernel, count),
        [((rows, span, width), bf16), ((rows, span, width), f32), ((2, 256), f32), ((2, 256), f32), ((2, 256), f32), ((2, 128), f32), ((2, 128), f32)],
        (bulk0.small[0], totals1, own_parts.reshape(quad), got_parts.reshape(quad), tokens, nrm0, raw))
    lin_grad, gate_grad, out_grad, in_grad = unpack(bulk1.result, bulk1.masks[0], bulk0.result, bulk0.masks[0])
    out_grad, in_grad = out_grad.reshape(2, 2, 128, 512), in_grad.reshape(2, 512, 2, 128)
    return (block_out, d_in, ngg, bias_grad, in_grad, out_grad, rate_grad, angle_grad, skip_grad, lin_grad, gate_grad)


def solution(mesh):
    placed = (
        P(None, "seq", "state"),
        P(None, "state"),
        P(None, "state"),
        P(None, None, None, "state"),
        P(None, None, "state", None),
        P(None, "state"),
        P(None, "state"),
        P(None, "state"),
        P(None, None, "state"),
        P(None, None, "state"),
        P(),
        P(None, "seq", "state"),
    )
    return jax.shard_map(
        body,
        mesh=mesh,
        in_specs=placed,
        out_specs=(
            P(None, "seq", "state"),
            P(None, "seq", "state"),
            P(None, "state"),
            P(None, "state"),
            P(None, None, None, "state"),
            P(None, None, "state", None),
            P(None, "state"),
            P(None, "state"),
            P(None, "state"),
            P(None, None, "state"),
            P(None, None, "state"),
        ),
        check_vma=False,
    )
```

```python
import functools

import jax
import jax.numpy as jnp
from jax import lax
from jax.experimental import pallas as pl
from jax.experimental.pallas import tpu as pltpu
from jax.sharding import PartitionSpec as P

f32, bf16 = jnp.float32, jnp.bfloat16
norm_eps = 1e-05
CHUNKS = 8
SLAB = 2 * CHUNKS
TILE = 512


def mm(a, b):
    return jnp.dot(a, b, preferred_element_type=f32)


def mm_nt(a, b):
    return lax.dot_general(a, b, (((1,), (1,)), ((), ())), preferred_element_type=f32)


def mm_tn(a, b):
    return lax.dot_general(a, b, (((0,), (0,)), ((), ())), preferred_element_type=f32)


def wide(row):
    return jnp.broadcast_to(row, (CHUNKS, 128))


def cmul(ar, ai, br, bi):
    return ar * br - ai * bi, ar * bi + ai * br


def row_of_tiles(tiles):
    return jnp.concatenate([tiles[i : i + 1, :] for i in range(tiles.shape[0])], axis=1)


def channel_row(core, own, oth, at):
    mine, other = own[at : at + 2, :], oth[at : at + 2, :]
    low = jnp.where(core == 0, mine, other)
    high = jnp.where(core == 0, other, mine)
    return jnp.concatenate([low[0:1], low[1:2], high[0:1], high[1:2]], axis=1)


def own_cols(core, width):
    return pl.ds(pl.multiple_of(core * width, width), width)


def oth_cols(core, width):
    return pl.ds(pl.multiple_of((1 - core) * width, width), width)


def scan(drive, lams, keep_ref, which, steps, reverse, start, visit):
    order = range(steps - 1, -1, -1) if reverse else range(steps)
    state = dict(start)
    for s in order:
        for row in range(2):
            at = s * SLAB + row * CHUNKS
            keep = keep_ref[which, at : at + CHUNKS, :]
            for half in range(2):
                lr, li = lams[half]
                hr, hi = state[half, row]
                hr, hi = keep * hr, keep * hi
                dr, di = drive(s, row, half)
                state[half, row] = (lr * hr - li * hi + dr, lr * hi + li * hr + di)
        visit(s, state, keep_ref)
    return state


def keep_products(keep_ref, which, steps):
    out = []
    for row in range(2):
        total = keep_ref[which, row * CHUNKS : (row + 1) * CHUNKS, :]
        for s in range(1, steps):
            at = s * SLAB + row * CHUNKS
            total = total * keep_ref[which, at : at + CHUNKS, :]
        out.append(total)
    return out


def chunk_scan(ends, keeps, powers, reverse, comp_ref, packed):
    index = lax.broadcasted_iota(jnp.int32, (CHUNKS, 128), 0)

    def shifted(value, by, fill):
        turned = pltpu.roll(value, CHUNKS - by if reverse else by, 0)
        valid = index < CHUNKS - by if reverse else index >= by
        return jnp.where(valid, turned, fill)

    for half in range(2):
        for row in range(2):
            er, ei = ends[half, row]
            pr, pi = powers[half][0] * keeps[row], powers[half][1] * keeps[row]
            for by in (1, 2, 4):
                tr, ti = cmul(pr, pi, shifted(er, by, 0.0), shifted(ei, by, 0.0))
                er, ei = er + tr, ei + ti
                pr, pi = cmul(pr, pi, shifted(pr, by, 1.0), shifted(pi, by, 0.0))
            edge = 0 if reverse else CHUNKS - 1
            q = row * 2 + half
            packed[q : q + 1, :] = er[edge : edge + 1, :]
            packed[4 + q : 5 + q, :] = ei[edge : edge + 1, :]
            base = (half * 2 + row) * 4
            comp_ref[base] = shifted(er, 1, 0.0)
            comp_ref[base + 1] = shifted(ei, 1, 0.0)
            comp_ref[base + 2] = shifted(pr, 1, 1.0)
            comp_ref[base + 3] = shifted(pi, 1, 0.0)


def device_carry(me, peers, got, held, dk_ref, which, own, oth, base, conj, reverse, packed):
    got_ref = arrange(got, held)
    index = lax.broadcasted_iota(jnp.int32, (CHUNKS, 128), 0)
    is_own = index % 2 == 0
    sign = jnp.where(index < 4, -1.0, 1.0) * (-1.0 if conj else 1.0)
    ar = jnp.where(is_own, wide(own[base + 11 : base + 12, :]), wide(oth[base + 11 : base + 12, :]))
    ai = jnp.where(is_own, wide(own[base + 12 : base + 13, :]), wide(oth[base + 12 : base + 13, :]))
    ai = ai * sign

    def step(k, held):
        at = peers - 1 - k if reverse else k
        reached = at > me if reverse else at < me
        new = dk_ref[which, at] * (ar * held + ai * pltpu.roll(held, 4, 0)) + got_ref[at]
        return jnp.where(reached, new, held)

    packed[...] = lax.fori_loop(0, peers, step, jnp.zeros((8, 128), f32), unroll=peers <= 16)


def entries(comp_ref, packed):
    start = {}
    for half in range(2):
        for row in range(2):
            base, q = (half * 2 + row) * 4, row * 2 + half
            hr, hi = wide(packed[q : q + 1, :]), wide(packed[4 + q : 5 + q, :])
            tr, ti = cmul(comp_ref[base + 2], comp_ref[base + 3], hr, hi)
            start[half, row] = (comp_ref[base] + tr, comp_ref[base + 1] + ti)
    return start


def decay(own, oth, base, at, conj=False):
    sign = -1.0 if conj else 1.0
    return [(wide(r[base + at : base + at + 1, :]), sign * wide(r[base + at + 1 : base + at + 2, :])) for r in (own, oth)]


def scales(own, oth, base):
    return [wide(r[base + 8 : base + 9, :]) for r in (own, oth)]


def nothing(*_):
    return None


def zeros_start():
    zero = jnp.zeros((CHUNKS, 128), f32)
    return {(half, row): (zero, zero) for half in range(2) for row in range(2)}


def part(s, row):
    at = s * SLAB + row * CHUNKS
    return slice(at, at + CHUNKS)


def cols(half, im):
    at = half * 256 + im * 128
    return slice(at, at + 128)


def flat_rows(ref):
    value = ref[...]
    return value.reshape(value.shape[0] * value.shape[1], value.shape[2])


def spread(out_ref, packed):
    value = packed[...]
    out_ref[...] = value if len(out_ref.shape) == 2 else jnp.broadcast_to(value[None], out_ref.shape)


def arrange(got, held):
    if len(got) == 1:
        return got[0]
    me = place()[0]
    for m, block in enumerate(got):
        for e in range(4):
            held[(((me >> 2) ^ m) << 2) + ((me & 3) ^ e)] = block[e]
    return held


def place():
    return lax.axis_index("seq"), lax.axis_index("state")


def stats_kernel(tokens, stats):
    s1 = s2 = 0.0
    for r in range(tokens.shape[0]):
        x = tokens[r].astype(f32)
        s1 = s1 + jnp.sum(x, axis=0, keepdims=True)
        s2 = s2 + jnp.sum(x * x, axis=0, keepdims=True)
    for i in range(2):
        stats[0, i : i + 1, :] = s1[:, 128 * i : 128 * (i + 1)]
        stats[0, 2 + i : 3 + i, :] = s2[:, 128 * i : 128 * (i + 1)]
    stats[...] = jnp.broadcast_to(stats[0][None], stats.shape)


def prep_kernel(peers, steps, span, pos, raw, small, keep, dk, perm):
    seq, core = place()
    docs = pos.shape[1]

    count = perm.shape[1]
    p = lax.broadcasted_iota(jnp.int32, (count, count), 0)
    q = lax.broadcasted_iota(jnp.int32, (count, count), 1)
    source = ((p >> 3) & 1) * span + (p & 7) * steps + (p >> 4)
    perm[0] = jnp.where(q == source, 1.0, 0.0).astype(bf16)
    source = ((q >> 3) & 1) * span + (q & 7) * steps + (q >> 4)
    perm[1] = jnp.where(p == source, 1.0, 0.0).astype(bf16)

    small[...] = jnp.zeros_like(small)
    for k in range(2):
        at = 16 * k
        values = raw[k : k + 1, :]
        for j in range(6):
            small[at + j : at + j + 1, :] = values[:, 128 * j : 128 * (j + 1)]
        rate = jnp.exp(values[:, 768:896])
        angle = jnp.exp(values[:, 896:])
        modulus = jnp.exp(-rate)
        lr, li = modulus * jnp.cos(angle), modulus * jnp.sin(angle)
        small[at + 6 : at + 7, :] = lr
        small[at + 7 : at + 8, :] = li
        small[at + 8 : at + 9, :] = jnp.sqrt(1.0 - modulus * modulus)
        power = 1
        while power < span:
            lr, li = cmul(lr, li, lr, li)
            power *= 2
            if power == steps:
                small[at + 9 : at + 10, :] = lr
                small[at + 10 : at + 11, :] = li
        small[at + 11 : at + 12, :] = lr
        small[at + 12 : at + 13, :] = li

    chunk = lax.broadcasted_iota(jnp.int32, (CHUNKS, 128), 0) * steps + seq * span
    for row in range(2):
        targets = [pos[core * 2 + row, d] - chunk for d in range(docs)]
        for s in range(steps + 1):
            hit = targets[0] == s
            for t in targets[1:]:
                hit = jnp.logical_or(hit, t == s)
            value = jnp.where(hit, 0.0, 1.0)
            at = s * SLAB + row * CHUNKS
            if s < steps:
                keep[0, at : at + CHUNKS, :] = value
            if s >= 1:
                keep[1, at - SLAB : at - SLAB + CHUNKS, :] = value

    first_row = (lax.broadcasted_iota(jnp.int32, (CHUNKS, 128), 0) // 2) % 2 == 0
    owners = ([], [])
    for d in range(docs):
        a, b = pos[core * 2, d], pos[core * 2 + 1, d]
        owners[0].append(jnp.where(first_row, a // span, b // span))
        owners[1].append(jnp.where(first_row, (a + span - 1) // span - 1, (b + span - 1) // span - 1))

    def mark(j, _):
        for m in range(2):
            hit = owners[m][0] == j
            for o in owners[m][1:]:
                hit = jnp.logical_or(hit, o == j)
            dk[m, j] = jnp.where(hit, 0.0, 1.0)
        return 0

    lax.fori_loop(0, peers, mark, 0)


def norm_rows(total, squares, count, core, own, oth, base, nrm):
    mean = total / count
    inv = lax.rsqrt(squares / count - mean * mean + norm_eps)
    nrm[0:1, :] = mean
    nrm[1:2, :] = inv
    nrm[2:3, :] = channel_row(core, own, oth, base)
    nrm[3:4, :] = channel_row(core, own, oth, base + 2)
    nrm[4:5, :] = channel_row(core, own, oth, base + 4)
    nrm[5:8, :] = jnp.zeros_like(nrm[5:8, :])


def normalized(x, nrm):
    xhat = (x - nrm[0:1, :]) * nrm[1:2, :]
    return xhat, xhat * nrm[2:3, :] + nrm[3:4, :]


def project_and_scan(steps, base, which, reverse, own, oth, keep, win_own, win_oth, nl, proj, comp, summ, packed):
    proj[:, :256] = mm(nl[...], win_own[...])
    proj[:, 256:] = mm(nl[...], win_oth[...])
    lams, sc = decay(own, oth, base, 6), scales(own, oth, base)

    def drive(s, row, half):
        return sc[half] * proj[part(s, row), cols(half, 0)], sc[half] * proj[part(s, row), cols(half, 1)]

    ends = scan(drive, lams, keep, which, steps, reverse, zeros_start(), nothing)
    chunk_scan(ends, keep_products(keep, which, steps), decay(own, oth, base, 9), reverse, comp, packed)
    spread(summ, packed)


def enter_first_kernel(peers, steps, count, got, x_own, x_oth, perm, own, oth, keep, win_own, win_oth,
                       xp, nl, proj, comp, summ, nrm, packed):
    _, core = place()
    sums = got[0:2]
    for j in range(1, peers):
        sums = sums + got[2 * j : 2 * j + 2]
    total = jnp.concatenate([sums[0, 0:1], sums[0, 1:2], sums[1, 0:1], sums[1, 1:2]], axis=1)
    squares = jnp.concatenate([sums[0, 2:3], sums[0, 3:4], sums[1, 2:3], sums[1, 3:4]], axis=1)
    norm_rows(total, squares, count, core, own, oth, 0, nrm)
    xp[:, own_cols(core, 256)] = mm(perm[0], flat_rows(x_own)).astype(bf16)
    xp[:, oth_cols(core, 256)] = mm(perm[0], flat_rows(x_oth)).astype(bf16)
    _, normed = normalized(xp[...].astype(f32), nrm)
    nl[...] = normed.astype(bf16)
    project_and_scan(steps, 0, 0, False, own, oth, keep, win_own, win_oth, nl, proj, comp, summ, packed)


def sum_peers(got):
    if len(got) == 1 and len(got[0].shape) == 3:
        got = [got[0].at[j] for j in range(got[0].shape[0])]
    total = got[0][...]
    for part in got[1:]:
        total = total + part[...]
    return total


def enter_second_kernel(peers, steps, count, got, x, own, oth, keep, win_own, win_oth,
                        nl, proj, comp, summ, nrm, packed):
    _, core = place()
    sums = sum_peers(got)
    norm_rows(row_of_tiles(sums[0:4]), row_of_tiles(sums[4:8]), count, core, own, oth, 16, nrm)
    _, normed = normalized(x[...], nrm)
    nl[...] = normed.astype(bf16)
    project_and_scan(steps, 16, 1, True, own, oth, keep, win_own, win_oth, nl, proj, comp, summ, packed)


def states_of(peers, steps, base, which, reverse, got, comp, dk, own, oth, keep, proj, cin, sl, packed, held):
    device_carry(place()[0], peers, got, held, dk, which, own, oth, base, False, reverse, packed)
    start = entries(comp, packed)
    lams, sc = decay(own, oth, base, 6), scales(own, oth, base)
    for (half, row), (hr, hi) in start.items():
        cin[part(0, row), cols(half, 0)] = hr
        cin[part(0, row), cols(half, 1)] = hi

    def drive(s, row, half):
        return sc[half] * proj[part(s, row), cols(half, 0)], sc[half] * proj[part(s, row), cols(half, 1)]

    def visit(s, state, _):
        for half in range(2):
            for im in range(2):
                both = jnp.concatenate([state[half, row][im] for row in range(2)], axis=0)
                sl[s * SLAB : (s + 1) * SLAB, cols(half, im)] = both.astype(bf16)

    scan(drive, lams, keep, which, steps, reverse, start, visit)


def mix_and_gate(core, x, nrm, sl, wout_own, wout_oth, lin_own, lin_oth, gate_own, gate_oth, gp, act, sig, qv, y):
    c = 0.7978845608028654
    for i in range(0, y.shape[0], TILE):
        rows = slice(i, i + TILE)
        _, normed = normalized(x[rows, :].astype(f32), nrm)
        mixed = mm(sl[rows, :256], wout_own[...]) + mm(sl[rows, 256:], wout_oth[...]) + nrm[4:5, :] * normed
        sq = mixed * mixed
        t = jnp.tanh(mixed * (c + (c * 0.044715) * sq))
        upper = 0.5 + 0.5 * t
        low = (mixed * upper).astype(bf16)
        act[rows, :] = low
        gp[rows, :] = (upper + mixed * (upper * (1.0 - t)) * (c + (3 * c * 0.044715) * sq)).astype(gp.dtype)
        for w_lin, w_gate, at in ((lin_own, gate_own, own_cols(core, 256)), (lin_oth, gate_oth, oth_cols(core, 256))):
            linear = mm(low, w_lin[...])
            gating = mm(low, w_gate[...])
            sg = 0.5 + 0.5 * jnp.tanh(0.5 * gating)
            out = linear * sg
            sig[rows, at] = sg.astype(sig.dtype)
            qv[rows, at] = (out * (1.0 - sg)).astype(qv.dtype)
            y[rows, at] = x[rows, at].astype(f32) + out
        yield rows


def leave_first_kernel(peers, steps, got, comp, dk, own, oth, keep, proj, x, nrm, wout_own, wout_oth,
                       lin_own, lin_oth, gate_own, gate_oth, cin, sl, gp, act, sig, qv, y, stats, packed, held):
    states_of(peers, steps, 0, 0, False, got, comp, dk, own, oth, keep, proj, cin, sl, packed, held)
    s1 = s2 = 0.0
    for rows in mix_and_gate(place()[1], x, nrm, sl, wout_own, wout_oth, lin_own, lin_oth, gate_own, gate_oth, gp, act, sig, qv, y):
        out = y[rows, :]
        s1, s2 = s1 + jnp.sum(out, axis=0, keepdims=True), s2 + jnp.sum(out * out, axis=0, keepdims=True)
    pack_two(s1, s2, packed)
    spread(stats, packed)


def pack_two(a, b, packed):
    for i in range(4):
        packed[i : i + 1, :] = a[:, 128 * i : 128 * (i + 1)]
        packed[4 + i : 5 + i, :] = b[:, 128 * i : 128 * (i + 1)]


def glu_backward(steps, base, adj_which, adj_reverse, core, d_out, nrm, x, gp, sig, qv, own, oth, keep, wout_own, wout_oth,
                 lin_own, lin_oth, gate_own, gate_oth, skip_row, dst, comp, summ, packed, dl, dg, dml):
    mine, other = own_cols(core, 256), oth_cols(core, 256)
    total = 0.0
    for i in range(0, dl.shape[0], TILE):
        rows = slice(i, i + TILE)
        grad = d_out(rows)
        dl[rows, :] = (grad * sig[rows, :].astype(f32)).astype(bf16)
        dg[rows, :] = (grad * qv[rows, :].astype(f32)).astype(bf16)
        d_active = (mm_nt(dl[rows, mine], lin_own[...]) + mm_nt(dg[rows, mine], gate_own[...])
                    + mm_nt(dl[rows, other], lin_oth[...]) + mm_nt(dg[rows, other], gate_oth[...]))
        d_mixed = d_active * gp[rows, :].astype(f32)
        _, normed = normalized(x[rows, :].astype(f32), nrm)
        total = total + jnp.sum(d_mixed * normed, axis=0, keepdims=True)
        low = d_mixed.astype(bf16)
        dml[rows, :] = low
        dst[rows, :256] = mm_nt(low, wout_own[...])
        dst[rows, 256:] = mm_nt(low, wout_oth[...])
    skip_row[0:1, :] = total
    lams = decay(own, oth, base, 6, conj=True)

    def drive(s, row, half):
        return dst[part(s, row), cols(half, 0)], dst[part(s, row), cols(half, 1)]

    ends = scan(drive, lams, keep, adj_which, steps, adj_reverse, zeros_start(), nothing)
    chunk_scan(ends, keep_products(keep, adj_which, steps), decay(own, oth, base, 9, conj=True), adj_reverse, comp, packed)
    spread(summ, packed)


def mixer_grads(act, dl, dg, sl, dml, l_own, l_oth, g_own, g_oth):
    _, core = place()
    mine, other = own_cols(core, 256), oth_cols(core, 256)
    left = act[...].T
    l_own[...] = mm(left, dl[:, mine]).astype(bf16)
    l_oth[...] = mm(left, dl[:, other]).astype(bf16)
    g_own[0:512, :] = mm(left, dg[:, mine]).astype(bf16)
    g_oth[0:512, :] = mm(left, dg[:, other]).astype(bf16)
    for ref, cut in ((g_own, slice(0, 256)), (g_oth, slice(256, 512))):
        left = sl[:, cut].T
        for i in range(2):
            ref[512 + 256 * i : 768 + 256 * i, :] = mm(left, dml[:, 256 * i : 256 * (i + 1)]).astype(ref.dtype)


def in_grads(nl, dp, g_own, g_oth):
    left = nl[...].T
    g_own[...] = mm(left, dp[:, :256]).astype(bf16)
    g_oth[...] = mm(left, dp[:, 256:]).astype(bf16)


def turn_kernel(peers, steps, got, comp_in, dk, own, oth, keep, proj, x, nrm, wout_own, wout_oth,
                lin_own, lin_oth, gate_own, gate_oth, perm, cot_own, cot_oth,
                cin, result, d_out, act, dl, dg, sl, dml, skip_row, dst, comp, summ,
                packed, held, gp, sig, qv, y):
    _, core = place()
    states_of(peers, steps, 16, 1, True, got, comp_in, dk, own, oth, keep, proj, cin, sl, packed, held)
    for _ in mix_and_gate(core, x, nrm, sl, wout_own, wout_oth, lin_own, lin_oth, gate_own, gate_oth, gp, act, sig, qv, y):
        pass
    result[...] = y[...].astype(bf16)
    d_out[:, own_cols(core, 256)] = mm(perm[0], flat_rows(cot_own)).astype(bf16)
    d_out[:, oth_cols(core, 256)] = mm(perm[0], flat_rows(cot_oth)).astype(bf16)
    glu_backward(steps, 16, 0, False, core, lambda rows: d_out[rows, :].astype(f32), nrm, x, gp, sig, qv, own, oth, keep, wout_own, wout_oth,
                 lin_own, lin_oth, gate_own, gate_oth, skip_row, dst, comp, summ, packed, dl, dg, dml)


def adjoint_part(peers, steps, base, keep_which, adj_which, adj_reverse, got, comp, dk, own, oth, keep, nl, x, nrm,
                 cin, sl, dst, dml, win_own, win_oth, skip_row, small_own, small_oth, all_rows, packed, held, proj, dp, keep_tile):
    _, core = place()
    device_carry(place()[0], peers, got, held, dk, adj_which, own, oth, base, True, adj_reverse, packed)
    start = entries(comp, packed)
    lams, sc = decay(own, oth, base, 6, conj=True), scales(own, oth, base)
    zero = jnp.zeros((CHUNKS, 128), f32)
    acc = {half: [zero, zero, zero] for half in range(2)}
    proj[:, :256] = mm(nl[...], win_own[...])
    proj[:, 256:] = mm(nl[...], win_oth[...])

    def prior(s, half, im):
        before = s - 1 if adj_reverse else s + 1
        if 0 <= before < steps:
            return sl[before * SLAB : (before + 1) * SLAB, cols(half, im)].astype(f32)
        return cin[:, cols(half, im)]

    def drive(s, row, half):
        return dst[part(s, row), cols(half, 0)], dst[part(s, row), cols(half, 1)]

    def visit(s, state, _):
        for half in range(2):
            prior_re, prior_im = prior(s, half, 0), prior(s, half, 1)
            for row in range(2):
                ar, ai = state[half, row]
                pr, pi = prior_re[part(0, row)], prior_im[part(0, row)]
                keep_here = keep[keep_which, part(s, row), :]
                acc[half][0] = acc[half][0] + keep_here * (ar * pr + ai * pi)
                acc[half][1] = acc[half][1] + keep_here * (ai * pr - ar * pi)
                acc[half][2] = acc[half][2] + (ar * proj[part(s, row), cols(half, 0)] + ai * proj[part(s, row), cols(half, 1)])
            for im in range(2):
                both = jnp.concatenate([sc[half] * state[half, row][im] for row in range(2)], axis=0)
                dp[s * SLAB : (s + 1) * SLAB, cols(half, im)] = both.astype(bf16)

    scan(drive, lams, keep, adj_which, steps, adj_reverse, start, visit)

    bias_row = gain_row = 0.0
    for i in range(0, dp.shape[0], TILE):
        rows = slice(i, i + TILE)
        d_normed = dml[rows, :].astype(f32) * nrm[4:5, :] + mm_nt(dp[rows, :256], win_own[...]) + mm_nt(dp[rows, 256:], win_oth[...])
        xhat, _ = normalized(x[rows, :].astype(f32), nrm)
        bias_row = bias_row + jnp.sum(d_normed, axis=0, keepdims=True)
        gain_row = gain_row + jnp.sum(d_normed * xhat, axis=0, keepdims=True)
        keep_tile(rows, d_normed)
    pack_two(bias_row, gain_row, packed)

    wanted = (skip_row[0:1, :], bias_row, gain_row) if all_rows else (skip_row[0:1, :],)
    for ref, half in ((small_own, 0), (small_oth, 1)):
        ref[...] = jnp.zeros_like(ref)
        at = 0
        for row in wanted:
            pick = jnp.where(core == half, row[:, :256], row[:, 256:])
            ref[at : at + 1, :] = pick[:, :128]
            ref[at + 1 : at + 2, :] = pick[:, 128:]
            at += 2
        for j in range(3):
            ref[at + j : at + j + 1, :] = jnp.sum(acc[half][j], axis=0, keepdims=True)


def adjoint_second_kernel(peers, steps, got, comp, dk, own, oth, keep, nl, x, nrm, cin, sl, dst, dml, win_own, win_oth, skip_row, act, dl, dg,
                          g_own, g_oth, small_own, small_oth, dn, stats, packed, held, proj, dp):
    def keep_tile(rows, d_normed):
        dn[rows, :] = d_normed

    adjoint_part(peers, steps, 16, 1, 0, False, got, comp, dk, own, oth, keep, nl, x, nrm,
                 cin, sl, dst, dml, win_own, win_oth, skip_row, small_own, small_oth, False, packed, held, proj, dp, keep_tile)
    spread(stats, packed)
    mixer_grads(act, dl, dg, sl, dml, g_own.at[:512], g_oth.at[:512], g_own.at[512:1536], g_oth.at[512:1536])
    in_grads(nl, dp, g_own.at[1536:], g_oth.at[1536:])


def back_first_kernel(steps, count, got, dn, x2, nrm2, d_out2, own, oth, keep, x, nrm, gp, sig, qv,
                      wout_own, wout_oth, lin_own, lin_oth, gate_own, gate_oth,
                      act, sl, d_out, dml, totals, l_own, l_oth, g_own, g_oth, skip_row, dst, comp, summ, packed, dl, dg):
    sums = sum_peers(got)
    bias_row, gain_row = row_of_tiles(sums[0:4]), row_of_tiles(sums[4:8])
    totals[...] = jnp.zeros_like(totals)
    totals[0:1, :], totals[1:2, :] = bias_row, gain_row
    mean, inv, gain = nrm2[0:1, :], nrm2[1:2, :], nrm2[2:3, :]
    scaled, shift, slope = inv * gain, inv * gain * bias_row / count, inv * inv * gain * gain_row / count

    def d_in(rows):
        value = d_out2[rows, :].astype(f32) + scaled * dn[rows, :] - shift - slope * (x2[rows, :] - mean)
        d_out[rows, :] = value
        return value

    glu_backward(steps, 0, 1, True, place()[1], d_in, nrm, x, gp, sig, qv, own, oth, keep, wout_own, wout_oth,
                 lin_own, lin_oth, gate_own, gate_oth, skip_row, dst, comp, summ, packed, dl, dg, dml)
    mixer_grads(act, dl, dg, sl, dml, l_own, l_oth, g_own, g_oth)


def adjoint_first_kernel(peers, steps, got, comp, dk, own, oth, keep, nl, x, nrm, cin, sl, dst, dml, win_own, win_oth, skip_row,
                         d_out, small1_own, small1_oth,
                         g_own, g_oth, small_own, partial, packed, held, proj, dp, small_oth):
    _, core = place()
    scaled = nrm[1:2, :] * nrm[2:3, :]

    def keep_tile(rows, d_normed):
        partial[rows, :] = (d_out[rows, :] + scaled * d_normed).astype(bf16)

    adjoint_part(peers, steps, 0, 0, 1, True, got, comp, dk, own, oth, keep, nl, x, nrm,
                 cin, sl, dst, dml, win_own, win_oth, skip_row, small_own, small_oth, True, packed, held, proj, dp, keep_tile)
    small_own[9:14, :] = small1_own[0:5, :]
    small_oth[9:14, :] = small1_oth[0:5, :]
    in_grads(nl, dp, g_own, g_oth.at[:512])
    put_small(g_oth, 512, small_oth[...])


def order_kernel(perm, result, partial, own, oth):
    _, core = place()
    for i, ref in enumerate((result, partial)):
        own[i] = mm(perm[1], ref[:, own_cols(core, 256)]).astype(bf16)
        oth[i] = mm(perm[1], ref[:, oth_cols(core, 256)]).astype(bf16)


def finish_kernel(count, packed, totals1, mine_parts, other_parts, tokens, nrm, raw,
                  block_out, d_in, ngg, bias, skip, rate_grad, angle_grad):
    _, core = place()
    for ref, j in ((skip, 0), (bias, 2), (ngg, 4)):
        ref[0:1, :128], ref[0:1, 128:] = packed[j : j + 1, :], packed[j + 1 : j + 2, :]
    skip[1:2, :128], skip[1:2, 128:] = packed[9:10, :], packed[10:11, :]
    bias[1:2, :] = totals1[0:1, own_cols(core, 256)]
    ngg[1:2, :] = totals1[1:2, own_cols(core, 256)]
    for k, at in ((0, 6), (1, 11)):
        values = raw[k : k + 1, :]
        rate = jnp.exp(values[:, 768:896])
        angle = jnp.exp(values[:, 896:])
        modulus = jnp.exp(-rate)
        scale = jnp.sqrt(1.0 - modulus * modulus)
        cos, sin = jnp.cos(angle), jnp.sin(angle)
        dr, di, ds = (packed[at + j : at + j + 1, :] for j in range(3))
        g_mod = dr * cos + di * sin - ds * modulus / scale
        rate_grad[k : k + 1, :] = -g_mod * modulus * rate
        angle_grad[k : k + 1, :] = modulus * (di * cos - dr * sin) * angle
    mine = nrm[:, own_cols(core, 256)]
    mean, inv, gain = mine[0:1, :], mine[1:2, :], mine[2:3, :]
    bias_row, gain_row = bias[0:1, :], ngg[0:1, :]
    flat = inv * gain / count
    for r in range(4):
        block_out[r] = jnp.where(core == r // 2, mine_parts[0, r % 2], other_parts[0, r % 2])
        held_rows = jnp.where(core == r // 2, mine_parts[1, r % 2].astype(f32), other_parts[1, r % 2].astype(f32))
        xhat = (tokens[r].astype(f32) - mean) * inv
        d_in[r] = held_rows - flat * (bias_row + xhat * gain_row)


def swap(value):
    return lax.ppermute(value, "state", [(0, 1), (1, 0)])


def to_all(value, axes):
    peers = 1
    for a in axes:
        peers *= lax.axis_size(a)
    return lax.all_to_all(jnp.broadcast_to(value[None], (peers,) + value.shape), axes, 0, 0)


def blocking(value, axes, others):
    value, others = lax.optimization_barrier((value, others))
    got, others = lax.optimization_barrier((lax.all_to_all(value, axes, 0, 0), others))
    return (got,), others


def gather_seq(value):
    if lax.axis_size("seq") != 16:
        return (to_all(value, ("seq",)),)
    near = jnp.stack([value] + [partner(value, m) for m in (1, 2, 3)])
    return (near,) + tuple(partner(near, m) for m in (4, 8, 12))


def sum_all(value):
    if lax.axis_size("seq") != 16:
        return (to_all(value, ("seq", "state")),)
    value = value + swap(value)
    near = value + partner(value, 1) + partner(value, 2) + partner(value, 3)
    return (near,) + tuple(partner(near, m) for m in (4, 8, 12))


def partner(value, mask):
    size = lax.axis_size("seq")
    return lax.ppermute(value, "seq", [(i, i ^ mask) for i in range(size)])


def partners(value, masks):
    size = lax.axis_size("seq")
    return lax.ppermute(value, ("seq", "state"), [(2 * i + c, 2 * (i ^ masks[c]) + c) for i in range(size) for c in range(2)])


def tie(value, others):
    return lax.optimization_barrier((value, others))


def bit_of(masks):
    me, core = place()
    return (me // jnp.where(core == 0, masks[0], masks[1])) & 1


def put_small(out, at, value):
    high = value.astype(bf16)
    rest = value - high.astype(f32)
    middle = rest.astype(bf16)
    low = (rest - middle.astype(f32)).astype(bf16)
    out[at : at + 16, :128], out[at : at + 16, 128:] = high, middle
    out[at + 16 : at + 32, :128], out[at + 16 : at + 32, 128:] = low, jnp.zeros_like(low)


def get_small(ref, at):
    return (ref[at : at + 16, :128].astype(f32) + ref[at : at + 16, 128:].astype(f32)) + ref[at + 16 : at + 32, :128].astype(f32)


def first_halves_kernel(masks, pairs, small, mine, other):
    bit, at = bit_of(masks), 0
    for own, got in pairs:
        half = own.shape[0] // 2
        for out, which in ((mine, bit), (other, 1 - bit)):
            rows = pl.ds(pl.multiple_of(which * half, half), half)
            out[at : at + half, :] = (own[rows, :].astype(f32) + got[rows, :].astype(f32)).astype(bf16)
        at += half
    if small is not None:
        total = small[...] + get_small(pairs[-1][1], pairs[-1][0].shape[0])
        put_small(mine, at, total)
        put_small(other, at, total)


def next_halves_kernel(masks, extra, held, got, mine, other):
    bit, half = bit_of(masks), mine.shape[0] - extra
    for out, which in ((mine, bit), (other, 1 - bit)):
        rows = pl.ds(pl.multiple_of(which * half, half), half)
        out[:half, :] = (held[rows, :].astype(f32) + got[rows, :].astype(f32)).astype(bf16)
    if extra:
        total = get_small(held, 2 * half) + get_small(got, 2 * half)
        put_small(mine, half, total)
        put_small(other, half, total)


def add_kernel(extra, held, got, total, *small):
    rows = held.shape[0] - extra
    total[:rows, :] = (held[:rows, :].astype(f32) + got[:rows, :].astype(f32)).astype(bf16)
    if extra:
        value = get_small(held, rows) + get_small(got, rows)
        if small:
            small[0][...] = value
        else:
            put_small(total, rows, value)


def axes_orders(*orders):
    masks, m = [], 1
    while m < lax.axis_size("seq"):
        masks.append(m)
        m *= 2
    return list(zip(*[[masks[i] for i in o] + masks[4:] for o in orders]))


class SeqSum:
    def __init__(self, pairs, masks, small=None):
        self.masks, self.at, self.small, self.extra = masks, 0, (), 0 if small is None else 32
        rows = sum(a.shape[0] for a, _ in pairs) // 2 + self.extra
        shape = ((rows, pairs[0][0].shape[1]), bf16)
        flat = tuple(v for p in pairs for v in p) + (() if small is None else (small,))

        def kernel(refs, mine, other):
            count = 2 * len(pairs)
            first_halves_kernel(masks[0], [(refs[i], refs[i + 1]) for i in range(0, count, 2)],
                                None if small is None else refs[count], mine, other)

        self.mine, self.send = run(kernel, [shape, shape], (flat,))

    def step(self):
        count, i = len(self.masks), self.at
        self.at += 1
        if i < count:
            got = partners(self.send, self.masks[i])
            rows, width = got.shape
            rows -= self.extra
            if i + 2 < count:
                shape = ((rows // 2 + self.extra, width), bf16)
                self.mine, self.send = run(functools.partial(next_halves_kernel, self.masks[i + 1], self.extra), [shape, shape], (self.mine, got))
            elif i + 2 == count:
                (self.send,) = run(functools.partial(add_kernel, self.extra), [((rows + self.extra, width), bf16)], (self.mine, got))
            else:
                outs = [((rows, width), bf16)] + ([((16, 128), f32)] if self.extra else [])
                self.send, *self.small = run(functools.partial(add_kernel, self.extra), outs, (self.send, got))
            return False
        mask = self.masks[2 * count - 2 - i]
        got = partners(self.send, mask)
        if i + 2 == 2 * count:
            self.result = (self.send, got)
            return True
        bit = bit_of(mask)
        self.send = jnp.concatenate([jnp.where(bit == 0, self.send, got), jnp.where(bit == 0, got, self.send)], axis=0)
        return False

    def after(self, values):
        self.send = tie(self.send, values)[0]

    def before(self, value):
        value, self.send = tie(value, self.send)
        return value


class Leaving:
    def __init__(self, sem):
        self.sem, self.copies = sem, []

    def send(self, source, target):
        copy = pltpu.make_async_copy(source, target, self.sem.at[len(self.copies)])
        copy.start()
        self.copies.append(copy)

    def wait(self):
        for copy in self.copies:
            copy.wait()


def put_entry(entry, ref, at, start, rows):
    value = ref[at : at + rows, :].astype(f32)
    entry[pl.ds(2 * start, rows, stride=2), :] = value[:, :128]
    entry[pl.ds(2 * start + 1, rows, stride=2), :] = value[:, 128:]


def on_half(mine, got, masks, half, put):
    bit = bit_of(masks)
    for ref, which in ((mine, bit), (got, 1 - bit)):

        @pl.when(which == half)
        def _():
            put(ref, lambda at, rows: ref[at : at + rows, :].astype(f32))


def unpack_second_kernel(masks, mine, got, lin_out, gate_out, out_out, entry_out, lin, gate, out, entry, sem):
    leaving = Leaving(sem)

    def low(ref, piece):
        lin[1], gate[...], lin[0, :256] = piece(0, 512), piece(512, 512), piece(1024, 256)

    def high(ref, piece):
        out[:, :256], out[:, 256:], lin[0, 256:] = piece(0, 256), piece(256, 256), piece(1024, 256)
        put_entry(entry, ref, 512, 0, 512)

    on_half(mine, got, masks, 0, low)
    leaving.send(gate, gate_out.at[1])
    on_half(mine, got, masks, 1, high)
    leaving.send(lin, lin_out)
    leaving.send(out, out_out.at[1])
    leaving.send(entry, entry_out.at[1])
    leaving.wait()


def unpack_first_kernel(masks, mine, got, gate_in, out_in, entry_in, gate_out, out_out, entry_out, gate, out, entry, sem):
    leaving = Leaving(sem)

    def low(ref, piece):
        gate[...] = piece(0, 512)
        put_entry(entry, ref, 512, 0, 256)

    def high(ref, piece):
        out[:, :256], out[:, 256:] = piece(0, 256), piece(256, 256)
        put_entry(entry, ref, 512, 256, 256)

    on_half(mine, got, masks, 0, low)
    leaving.send(gate, gate_out.at[0])
    on_half(mine, got, masks, 1, high)
    leaving.send(out, out_out.at[0])
    leaving.send(entry, entry_out.at[0])
    leaving.wait()


def unpack(second, second_masks, first, first_masks):
    far, near = pl.BlockSpec(memory_space=pltpu.HBM), pl.BlockSpec(memory_space=pltpu.VMEM)
    lin, gate, out, entry = (jax.ShapeDtypeStruct(s, f32) for s in ((2, 512, 256), (2, 512, 256), (2, 256, 512), (2, 1024, 128)))
    parts = [pltpu.VMEM(a.shape[1:], f32) for a in (gate, out, entry)]
    params = pltpu.CompilerParams(vmem_limit_bytes=24 * 2**20)
    lin_grad, *rest = pl.pallas_call(
        functools.partial(unpack_second_kernel, second_masks),
        out_shape=[lin, gate, out, entry], in_specs=[near] * 2, out_specs=[far] * 4,
        scratch_shapes=[pltpu.VMEM(lin.shape, f32)] + parts + [pltpu.SemaphoreType.DMA((4,))],
        compiler_params=params)(*second)
    rest = pl.pallas_call(
        functools.partial(unpack_first_kernel, first_masks),
        out_shape=[gate, out, entry], in_specs=[near] * 2 + [far] * 3, out_specs=[far] * 3,
        scratch_shapes=parts + [pltpu.SemaphoreType.DMA((3,))],
        input_output_aliases={2: 0, 3: 1, 4: 2},
        compiler_params=params)(*first, *rest)
    return [lin_grad, *rest]


class Far:
    def __init__(self, value, at=None, smem=False):
        self.value, self.at, self.smem = value, at, smem
        self.shape = value.shape if at is None else value.shape[1:] if at != "rows" else (2,) + value.shape[1:]

    def source(self, ref):
        if self.at is None:
            return ref
        return ref.at[pl.ds(lax.axis_index("state") * 2, 2)] if self.at == "rows" else ref.at[self.at]


class Part:
    def __init__(self, value, at):
        self.value, self.at = value, at

    def view(self, ref):
        return ref.at[pl.ds(lax.axis_index("state") * 2, 2)] if self.at == "rows" else ref.at[self.at]


class Held:
    def __init__(self, source, ref, sem):
        self.ref, self.copy, self.shape, self.dtype = ref, pltpu.make_async_copy(source, ref, sem), ref.shape, ref.dtype
        self.copy.start()

    def ready(self):
        if self.copy is not None:
            self.copy.wait()
            self.copy = None

    def __getitem__(self, index):
        self.ready()
        return self.ref[index]


def run(kernel, outs, groups, scratch=(), limit=24, flops=0):
    args = [a for g in groups for a in (g if isinstance(g, tuple) else (g,))]
    far_in = [i for i, a in enumerate(args) if isinstance(a, Far)]
    arrays = [a.value if isinstance(a, (Far, Part)) else a for a in args]
    moved = sum(a.size * a.dtype.itemsize for a in arrays)

    def whole(*refs):
        ins, results = list(refs[: len(args)]), list(refs[len(args) : len(args) + len(outs)])
        rest = refs[len(args) + len(outs) :]
        own = rest[: len(scratch)]
        if far_in:
            buffers, sem = rest[len(scratch) : -1], rest[-1]
        for j, i in enumerate(far_in):
            ins[i] = Held(args[i].source(ins[i]), buffers[j], sem.at[j])
        ins = [a.view(r) if isinstance(a, Part) else r for r, a in zip(ins, args)]
        grouped, at = [], 0
        for g in groups:
            if isinstance(g, tuple):
                grouped.append(tuple(ins[at : at + len(g)]))
                at += len(g)
            else:
                grouped.append(ins[at])
                at += 1
        kernel(*grouped, *results, *own)
        for i in far_in:
            ins[i].ready()

    def space(far):
        return pl.BlockSpec(memory_space=pltpu.HBM if far else pltpu.VMEM)

    held = [(pltpu.SMEM if args[i].smem else pltpu.VMEM)(args[i].shape, args[i].value.dtype) for i in far_in]
    if held:
        held.append(pltpu.SemaphoreType.DMA((len(held),)))
    return pl.pallas_call(
        whole,
        out_shape=[jax.ShapeDtypeStruct(o[0], o[1]) for o in outs],
        in_specs=[space(isinstance(a, Far)) for a in args],
        out_specs=[space(False)] * len(outs),
        scratch_shapes=[pltpu.VMEM(*s) for s in scratch] + held,
        compiler_params=pltpu.CompilerParams(vmem_limit_bytes=limit * 2**20),
        cost_estimate=pl.CostEstimate(flops=flops, bytes_accessed=moved, transcendentals=0),
    )(*arrays)


def body(tokens, gain, bias, in_proj, out_proj, rate_log, angle_log, skip, glu_lin, glu_gate, positions, cotangent):
    peers = lax.axis_size("seq")
    core = lax.axis_index("state")
    rows, span, width = tokens.shape
    steps = span // CHUNKS
    n = 2 * span
    count = float(rows * span * peers)
    packed = ((8, 128), f32)
    one = 2 * n * 512 * 512
    low = ((n, 512), bf16)
    full = ((n, 512), f32)

    (stats,) = run(stats_kernel, [((2 * peers, 4, 128), f32)], (tokens,))
    raw, at = 0.0, 0
    for v in (gain, bias, skip, rate_log, angle_log):
        raw, at = raw + jnp.pad(v.astype(f32), ((0, 0), (at, 1024 - at - v.shape[1]))), at + v.shape[1]
    w_in = in_proj.reshape(2, 512, 256)
    w_out = out_proj.reshape(2, 256, 512)
    x_oth, cot_oth, in_oth, out_oth, lin_oth, gate_oth = (swap(w) for w in (tokens, cotangent, w_in, w_out, glu_lin, glu_gate))
    enter = [(Part(w_in, k), Part(in_oth, k)) for k in range(2)]
    own, keep, dk, perm = run(
        functools.partial(prep_kernel, peers, steps, span),
        [((32, 128), f32), ((2, n, 128), f32), ((2, peers, 8, 128), f32), ((2, n, n), bf16)],
        (Far(positions, smem=True), raw))
    oth = swap(own)
    ordered = ((peers, 8, 128), f32)

    for_seq, for_all = ((peers, 8, 128), f32), ((2 * peers, 8, 128), f32)
    scan_outs = [full, ((16, 8, 128), f32), for_seq, ((8, 512), f32)]
    xp, nl0, proj, comp, summ, nrm0 = run(
        functools.partial(enter_first_kernel, peers, steps, count), [low, low] + scan_outs,
        (lax.all_to_all(stats, ("seq", "state"), 0, 0), Part(tokens, "rows"), Part(x_oth, "rows"), perm, own, oth, keep) + enter[0], [packed], flops=2 * one)
    got, (cot_oth, out_oth, lin_oth, gate_oth) = blocking(summ, "seq", (cot_oth, out_oth, lin_oth, gate_oth))
    glu = [tuple((Part if i % 2 else Part)(w, k) for i, w in enumerate((w_out, out_oth, glu_lin, lin_oth, glu_gate, gate_oth))) for k in range(2)]
    cin0, sl0, gp0, act0, sig0, qv0, y0, stats = run(
        functools.partial(leave_first_kernel, peers, steps),
        [((SLAB, 512), f32), low, low, low, low, low, full, for_all],
        (got, comp, dk, own, oth, keep, proj, xp, nrm0) + glu[0], [packed, ordered], flops=3 * one)
    got, _ = blocking(stats, ("seq", "state"), ())
    nl1, proj, comp, summ, nrm1 = run(
        functools.partial(enter_second_kernel, peers, steps, count), [low] + scan_outs,
        (got, y0, own, oth, keep) + enter[1], [packed], flops=one)
    got, _ = blocking(summ, "seq", ())
    turn_outs = [((8, 512), f32), full, ((16, 8, 128), f32)]
    cin1, result, d_out1, act1, dl1, dg1, sl1, dml1, skip1, dst, comp, summ = run(
        functools.partial(turn_kernel, peers, steps),
        [((SLAB, 512), f32), low, low, low, low, low, low, low] + turn_outs + [for_seq],
        (got, comp, dk, own, oth, keep, proj, y0, nrm1) + glu[1] + (perm, Part(cotangent, "rows"), Part(cot_oth, "rows")),
        [packed, ordered, full, full, full, full], flops=8 * one)
    got, _ = blocking(summ, "seq", ())
    g1_own, g1_oth, s1_own, s1_oth, dn, stats = run(
        functools.partial(adjoint_second_kernel, peers, steps),
        [((2048, 256), bf16), ((2048, 256), bf16), ((8, 128), f32), ((8, 128), f32), full, for_all],
        (got, comp, dk, own, oth, keep, nl1, y0, nrm1, cin1, sl1, dst, dml1) + enter[1] + (skip1, act1, dl1, dg1),
        [packed, ordered, full, low], flops=6 * one)
    got, (g1_oth,) = blocking(stats, ("seq", "state"), (g1_oth,))
    g1_got = swap(g1_oth)
    d_out0, dml0, totals1, l0_own, l0_oth, g0_own, g0_oth, skip0, dst, comp, summ = run(
        functools.partial(back_first_kernel, steps, count),
        [full, low, ((8, 512), f32), ((512, 256), bf16), ((512, 256), bf16), ((1024, 256), bf16), ((1024, 256), bf16)] + turn_outs + [for_seq],
        (got, dn, y0, nrm1, d_out1, own, oth, keep, xp, nrm0, gp0, sig0, qv0) + glu[0] + (act0, sl0),
        [packed, low, low], flops=6 * one)
    got, (l0_oth, g0_oth, g1_got, result) = blocking(summ, "seq", (l0_oth, g0_oth, g1_got, result))
    l0_got, g0_got = swap(l0_oth), swap(g0_oth)
    i0_own, i0_oth, s_own, partial = run(
        functools.partial(adjoint_first_kernel, peers, steps),
        [((512, 256), bf16), ((544, 256), bf16), ((16, 128), f32), low],
        (got, comp, dk, own, oth, keep, nl0, xp, nrm0, cin0, sl0, dst, dml0) + enter[0]
        + (skip0, d_out0, s1_own, s1_oth),
        [packed, ordered, full, low, ((16, 128), f32)], flops=3 * one)
    i0_got = swap(i0_oth)
    bulk1 = SeqSum([(g1_own, g1_got), (l0_own, l0_got)], axes_orders((0, 1, 2, 3), (1, 0, 2, 3)))
    bulk0 = SeqSum([(g0_own, g0_got), (i0_own, i0_got)], axes_orders((2, 1, 0, 3), (2, 0, 1, 3)), s_own)
    own_parts, oth_parts = run(order_kernel, [((2, n, 256), bf16)] * 2, (perm, result, partial), flops=2 * one)
    got_parts = swap(oth_parts)
    for bulk in (bulk1, bulk0):
        while not bulk.step():
            pass
    quad = (2, 2, span, width)
    block_out, d_in, ngg, bias_grad, skip_grad, rate_grad, angle_grad = run(
        functools.partial(finish_kernel, count),
        [((rows, span, width), bf16), ((rows, span, width), f32), ((2, 256), f32), ((2, 256), f32), ((2, 256), f32), ((2, 128), f32), ((2, 128), f32)],
        (bulk0.small[0], totals1, own_parts.reshape(quad), got_parts.reshape(quad), tokens, nrm0, raw))
    lin_grad, gate_grad, out_grad, in_grad = unpack(bulk1.result, bulk1.masks[0], bulk0.result, bulk0.masks[0])
    out_grad, in_grad = out_grad.reshape(2, 2, 128, 512), in_grad.reshape(2, 512, 2, 128)
    return (block_out, d_in, ngg, bias_grad, in_grad, out_grad, rate_grad, angle_grad, skip_grad, lin_grad, gate_grad)


def solution(mesh):
    placed = (
        P(None, "seq", "state"),
        P(None, "state"),
        P(None, "state"),
        P(None, None, None, "state"),
        P(None, None, "state", None),
        P(None, "state"),
        P(None, "state"),
        P(None, "state"),
        P(None, None, "state"),
        P(None, None, "state"),
        P(),
        P(None, "seq", "state"),
    )
    return jax.shard_map(
        body,
        mesh=mesh,
        in_specs=placed,
        out_specs=(
            P(None, "seq", "state"),
            P(None, "seq", "state"),
            P(None, "state"),
            P(None, "state"),
            P(None, None, None, "state"),
            P(None, None, "state", None),
            P(None, "state"),
            P(None, "state"),
            P(None, "state"),
            P(None, None, "state"),
            P(None, None, "state"),
        ),
        check_vma=False,
    )
```

```python
import functools

import jax
import jax.numpy as jnp
from jax import lax
from jax.experimental import pallas as pl
from jax.experimental.pallas import tpu as pltpu
from jax.sharding import PartitionSpec as P

f32, bf16 = jnp.float32, jnp.bfloat16
norm_eps = 1e-05
CHUNKS = 8
SLAB = 2 * CHUNKS
TILE = 512


def mm(a, b):
    return jnp.dot(a, b, preferred_element_type=f32)


def mm_nt(a, b):
    return lax.dot_general(a, b, (((1,), (1,)), ((), ())), preferred_element_type=f32)


def mm_tn(a, b):
    return lax.dot_general(a, b, (((0,), (0,)), ((), ())), preferred_element_type=f32)


def wide(row):
    return jnp.broadcast_to(row, (CHUNKS, 128))


def cmul(ar, ai, br, bi):
    return ar * br - ai * bi, ar * bi + ai * br


def row_of_tiles(tiles):
    return jnp.concatenate([tiles[i : i + 1, :] for i in range(tiles.shape[0])], axis=1)


def channel_row(core, own, oth, at):
    mine, other = own[at : at + 2, :], oth[at : at + 2, :]
    low = jnp.where(core == 0, mine, other)
    high = jnp.where(core == 0, other, mine)
    return jnp.concatenate([low[0:1], low[1:2], high[0:1], high[1:2]], axis=1)


def own_cols(core, width):
    return pl.ds(pl.multiple_of(core * width, width), width)


def oth_cols(core, width):
    return pl.ds(pl.multiple_of((1 - core) * width, width), width)


def scan(drive, lams, keep_ref, which, steps, reverse, start, visit):
    order = range(steps - 1, -1, -1) if reverse else range(steps)
    state = dict(start)
    for s in order:
        for row in range(2):
            at = s * SLAB + row * CHUNKS
            keep = keep_ref[which, at : at + CHUNKS, :]
            for half in range(2):
                lr, li = lams[half]
                hr, hi = state[half, row]
                hr, hi = keep * hr, keep * hi
                dr, di = drive(s, row, half)
                state[half, row] = (lr * hr - li * hi + dr, lr * hi + li * hr + di)
        visit(s, state, keep_ref)
    return state


def keep_products(keep_ref, which, steps):
    out = []
    for row in range(2):
        total = keep_ref[which, row * CHUNKS : (row + 1) * CHUNKS, :]
        for s in range(1, steps):
            at = s * SLAB + row * CHUNKS
            total = total * keep_ref[which, at : at + CHUNKS, :]
        out.append(total)
    return out


def chunk_scan(ends, keeps, powers, reverse, comp_ref, packed):
    index = lax.broadcasted_iota(jnp.int32, (CHUNKS, 128), 0)

    def shifted(value, by, fill):
        turned = pltpu.roll(value, CHUNKS - by if reverse else by, 0)
        valid = index < CHUNKS - by if reverse else index >= by
        return jnp.where(valid, turned, fill)

    for half in range(2):
        for row in range(2):
            er, ei = ends[half, row]
            pr, pi = powers[half][0] * keeps[row], powers[half][1] * keeps[row]
            for by in (1, 2, 4):
                tr, ti = cmul(pr, pi, shifted(er, by, 0.0), shifted(ei, by, 0.0))
                er, ei = er + tr, ei + ti
                pr, pi = cmul(pr, pi, shifted(pr, by, 1.0), shifted(pi, by, 0.0))
            edge = 0 if reverse else CHUNKS - 1
            q = row * 2 + half
            packed[q : q + 1, :] = er[edge : edge + 1, :]
            packed[4 + q : 5 + q, :] = ei[edge : edge + 1, :]
            base = (half * 2 + row) * 4
            comp_ref[base] = shifted(er, 1, 0.0)
            comp_ref[base + 1] = shifted(ei, 1, 0.0)
            comp_ref[base + 2] = shifted(pr, 1, 1.0)
            comp_ref[base + 3] = shifted(pi, 1, 0.0)


def device_carry(me, peers, got, held, dk_ref, which, own, oth, base, conj, reverse, packed):
    got_ref = arrange(got, held)
    index = lax.broadcasted_iota(jnp.int32, (CHUNKS, 128), 0)
    is_own = index % 2 == 0
    sign = jnp.where(index < 4, -1.0, 1.0) * (-1.0 if conj else 1.0)
    ar = jnp.where(is_own, wide(own[base + 11 : base + 12, :]), wide(oth[base + 11 : base + 12, :]))
    ai = jnp.where(is_own, wide(own[base + 12 : base + 13, :]), wide(oth[base + 12 : base + 13, :]))
    ai = ai * sign

    def step(k, held):
        at = peers - 1 - k if reverse else k
        reached = at > me if reverse else at < me
        new = dk_ref[which, at] * (ar * held + ai * pltpu.roll(held, 4, 0)) + got_ref[at]
        return jnp.where(reached, new, held)

    packed[...] = lax.fori_loop(0, peers, step, jnp.zeros((8, 128), f32), unroll=peers <= 16)


def entries(comp_ref, packed):
    start = {}
    for half in range(2):
        for row in range(2):
            base, q = (half * 2 + row) * 4, row * 2 + half
            hr, hi = wide(packed[q : q + 1, :]), wide(packed[4 + q : 5 + q, :])
            tr, ti = cmul(comp_ref[base + 2], comp_ref[base + 3], hr, hi)
            start[half, row] = (comp_ref[base] + tr, comp_ref[base + 1] + ti)
    return start


def decay(own, oth, base, at, conj=False):
    sign = -1.0 if conj else 1.0
    return [(wide(r[base + at : base + at + 1, :]), sign * wide(r[base + at + 1 : base + at + 2, :])) for r in (own, oth)]


def scales(own, oth, base):
    return [wide(r[base + 8 : base + 9, :]) for r in (own, oth)]


def nothing(*_):
    return None


def zeros_start():
    zero = jnp.zeros((CHUNKS, 128), f32)
    return {(half, row): (zero, zero) for half in range(2) for row in range(2)}


def part(s, row):
    at = s * SLAB + row * CHUNKS
    return slice(at, at + CHUNKS)


def cols(half, im):
    at = half * 256 + im * 128
    return slice(at, at + 128)


def flat_rows(ref):
    value = ref[...]
    return value.reshape(value.shape[0] * value.shape[1], value.shape[2])


def spread(out_ref, packed):
    value = packed[...]
    out_ref[...] = value if len(out_ref.shape) == 2 else jnp.broadcast_to(value[None], out_ref.shape)


def arrange(got, held):
    if len(got) == 1:
        return got[0]
    me = place()[0]
    for m, block in enumerate(got):
        for e in range(4):
            held[(((me >> 2) ^ m) << 2) + ((me & 3) ^ e)] = block[e]
    return held


def place():
    return lax.axis_index("seq"), lax.axis_index("state")


def stats_kernel(tokens, stats):
    s1 = s2 = 0.0
    for r in range(tokens.shape[0]):
        x = tokens[r].astype(f32)
        s1 = s1 + jnp.sum(x, axis=0, keepdims=True)
        s2 = s2 + jnp.sum(x * x, axis=0, keepdims=True)
    for i in range(2):
        stats[0, i : i + 1, :] = s1[:, 128 * i : 128 * (i + 1)]
        stats[0, 2 + i : 3 + i, :] = s2[:, 128 * i : 128 * (i + 1)]
    stats[...] = jnp.broadcast_to(stats[0][None], stats.shape)


def prep_kernel(peers, steps, span, pos, raw, small, keep, dk, perm):
    seq, core = place()
    docs = pos.shape[1]

    count = perm.shape[1]
    p = lax.broadcasted_iota(jnp.int32, (count, count), 0)
    q = lax.broadcasted_iota(jnp.int32, (count, count), 1)
    source = ((p >> 3) & 1) * span + (p & 7) * steps + (p >> 4)
    perm[0] = jnp.where(q == source, 1.0, 0.0).astype(bf16)
    source = ((q >> 3) & 1) * span + (q & 7) * steps + (q >> 4)
    perm[1] = jnp.where(p == source, 1.0, 0.0).astype(bf16)

    small[...] = jnp.zeros_like(small)
    for k in range(2):
        at = 16 * k
        values = raw[k : k + 1, :]
        for j in range(6):
            small[at + j : at + j + 1, :] = values[:, 128 * j : 128 * (j + 1)]
        rate = jnp.exp(values[:, 768:896])
        angle = jnp.exp(values[:, 896:])
        modulus = jnp.exp(-rate)
        lr, li = modulus * jnp.cos(angle), modulus * jnp.sin(angle)
        small[at + 6 : at + 7, :] = lr
        small[at + 7 : at + 8, :] = li
        small[at + 8 : at + 9, :] = jnp.sqrt(1.0 - modulus * modulus)
        power = 1
        while power < span:
            lr, li = cmul(lr, li, lr, li)
            power *= 2
            if power == steps:
                small[at + 9 : at + 10, :] = lr
                small[at + 10 : at + 11, :] = li
        small[at + 11 : at + 12, :] = lr
        small[at + 12 : at + 13, :] = li

    chunk = lax.broadcasted_iota(jnp.int32, (CHUNKS, 128), 0) * steps + seq * span
    for row in range(2):
        targets = [pos[core * 2 + row, d] - chunk for d in range(docs)]
        for s in range(steps + 1):
            hit = targets[0] == s
            for t in targets[1:]:
                hit = jnp.logical_or(hit, t == s)
            value = jnp.where(hit, 0.0, 1.0)
            at = s * SLAB + row * CHUNKS
            if s < steps:
                keep[0, at : at + CHUNKS, :] = value
            if s >= 1:
                keep[1, at - SLAB : at - SLAB + CHUNKS, :] = value

    first_row = (lax.broadcasted_iota(jnp.int32, (CHUNKS, 128), 0) // 2) % 2 == 0
    owners = ([], [])
    for d in range(docs):
        a, b = pos[core * 2, d], pos[core * 2 + 1, d]
        owners[0].append(jnp.where(first_row, a // span, b // span))
        owners[1].append(jnp.where(first_row, (a + span - 1) // span - 1, (b + span - 1) // span - 1))

    def mark(j, _):
        for m in range(2):
            hit = owners[m][0] == j
            for o in owners[m][1:]:
                hit = jnp.logical_or(hit, o == j)
            dk[m, j] = jnp.where(hit, 0.0, 1.0)
        return 0

    lax.fori_loop(0, peers, mark, 0)


def norm_rows(total, squares, count, core, own, oth, base, nrm):
    mean = total / count
    inv = lax.rsqrt(squares / count - mean * mean + norm_eps)
    nrm[0:1, :] = mean
    nrm[1:2, :] = inv
    nrm[2:3, :] = channel_row(core, own, oth, base)
    nrm[3:4, :] = channel_row(core, own, oth, base + 2)
    nrm[4:5, :] = channel_row(core, own, oth, base + 4)
    nrm[5:8, :] = jnp.zeros_like(nrm[5:8, :])


def normalized(x, nrm):
    xhat = (x - nrm[0:1, :]) * nrm[1:2, :]
    return xhat, xhat * nrm[2:3, :] + nrm[3:4, :]


def project_and_scan(steps, base, which, reverse, own, oth, keep, win_own, win_oth, nl, proj, comp, summ, packed):
    proj[:, :256] = mm(nl[...], win_own[...])
    proj[:, 256:] = mm(nl[...], win_oth[...])
    lams, sc = decay(own, oth, base, 6), scales(own, oth, base)

    def drive(s, row, half):
        return sc[half] * proj[part(s, row), cols(half, 0)], sc[half] * proj[part(s, row), cols(half, 1)]

    ends = scan(drive, lams, keep, which, steps, reverse, zeros_start(), nothing)
    chunk_scan(ends, keep_products(keep, which, steps), decay(own, oth, base, 9), reverse, comp, packed)
    spread(summ, packed)


def enter_first_kernel(peers, steps, count, got, x_own, x_oth, perm, own, oth, keep, win_own, win_oth,
                       xp, nl, proj, comp, summ, nrm, packed):
    _, core = place()
    sums = got[0:2]
    for j in range(1, peers):
        sums = sums + got[2 * j : 2 * j + 2]
    total = jnp.concatenate([sums[0, 0:1], sums[0, 1:2], sums[1, 0:1], sums[1, 1:2]], axis=1)
    squares = jnp.concatenate([sums[0, 2:3], sums[0, 3:4], sums[1, 2:3], sums[1, 3:4]], axis=1)
    norm_rows(total, squares, count, core, own, oth, 0, nrm)
    xp[:, own_cols(core, 256)] = mm(perm[0], flat_rows(x_own)).astype(bf16)
    xp[:, oth_cols(core, 256)] = mm(perm[0], flat_rows(x_oth)).astype(bf16)
    _, normed = normalized(xp[...].astype(f32), nrm)
    nl[...] = normed.astype(bf16)
    project_and_scan(steps, 0, 0, False, own, oth, keep, win_own, win_oth, nl, proj, comp, summ, packed)


def sum_peers(got):
    if len(got) == 1 and len(got[0].shape) == 3:
        got = [got[0].at[j] for j in range(got[0].shape[0])]
    total = got[0][...]
    for part in got[1:]:
        total = total + part[...]
    return total


def enter_second_kernel(peers, steps, count, got, x, own, oth, keep, win_own, win_oth,
                        nl, proj, comp, summ, nrm, packed):
    _, core = place()
    sums = sum_peers(got)
    norm_rows(row_of_tiles(sums[0:4]), row_of_tiles(sums[4:8]), count, core, own, oth, 16, nrm)
    _, normed = normalized(x[...], nrm)
    nl[...] = normed.astype(bf16)
    project_and_scan(steps, 16, 1, True, own, oth, keep, win_own, win_oth, nl, proj, comp, summ, packed)


def states_of(peers, steps, base, which, reverse, got, comp, dk, own, oth, keep, proj, cin, sl, packed, held):
    device_carry(place()[0], peers, got, held, dk, which, own, oth, base, False, reverse, packed)
    start = entries(comp, packed)
    lams, sc = decay(own, oth, base, 6), scales(own, oth, base)
    for (half, row), (hr, hi) in start.items():
        cin[part(0, row), cols(half, 0)] = hr
        cin[part(0, row), cols(half, 1)] = hi

    def drive(s, row, half):
        return sc[half] * proj[part(s, row), cols(half, 0)], sc[half] * proj[part(s, row), cols(half, 1)]

    def visit(s, state, _):
        for half in range(2):
            for im in range(2):
                both = jnp.concatenate([state[half, row][im] for row in range(2)], axis=0)
                sl[s * SLAB : (s + 1) * SLAB, cols(half, im)] = both.astype(bf16)

    scan(drive, lams, keep, which, steps, reverse, start, visit)


def mix_and_gate(core, x, nrm, sl, wout_own, wout_oth, lin_own, lin_oth, gate_own, gate_oth, gp, act, sig, qv, y):
    c = 0.7978845608028654
    for i in range(0, y.shape[0], TILE):
        rows = slice(i, i + TILE)
        _, normed = normalized(x[rows, :].astype(f32), nrm)
        mixed = mm(sl[rows, :256], wout_own[...]) + mm(sl[rows, 256:], wout_oth[...]) + nrm[4:5, :] * normed
        sq = mixed * mixed
        t = jnp.tanh(mixed * (c + (c * 0.044715) * sq))
        upper = 0.5 + 0.5 * t
        low = (mixed * upper).astype(bf16)
        act[rows, :] = low
        gp[rows, :] = (upper + mixed * (upper * (1.0 - t)) * (c + (3 * c * 0.044715) * sq)).astype(gp.dtype)
        for w_lin, w_gate, at in ((lin_own, gate_own, own_cols(core, 256)), (lin_oth, gate_oth, oth_cols(core, 256))):
            linear = mm(low, w_lin[...])
            gating = mm(low, w_gate[...])
            sg = 0.5 + 0.5 * jnp.tanh(0.5 * gating)
            out = linear * sg
            sig[rows, at] = sg.astype(sig.dtype)
            qv[rows, at] = (out * (1.0 - sg)).astype(qv.dtype)
            y[rows, at] = x[rows, at].astype(f32) + out
        yield rows


def leave_first_kernel(peers, steps, got, comp, dk, own, oth, keep, proj, x, nrm, wout_own, wout_oth,
                       lin_own, lin_oth, gate_own, gate_oth, cin, sl, gp, act, sig, qv, y, stats, packed, held):
    states_of(peers, steps, 0, 0, False, got, comp, dk, own, oth, keep, proj, cin, sl, packed, held)
    s1 = s2 = 0.0
    for rows in mix_and_gate(place()[1], x, nrm, sl, wout_own, wout_oth, lin_own, lin_oth, gate_own, gate_oth, gp, act, sig, qv, y):
        out = y[rows, :]
        s1, s2 = s1 + jnp.sum(out, axis=0, keepdims=True), s2 + jnp.sum(out * out, axis=0, keepdims=True)
    pack_two(s1, s2, packed)
    spread(stats, packed)


def pack_two(a, b, packed):
    for i in range(4):
        packed[i : i + 1, :] = a[:, 128 * i : 128 * (i + 1)]
        packed[4 + i : 5 + i, :] = b[:, 128 * i : 128 * (i + 1)]


def glu_backward(steps, base, adj_which, adj_reverse, core, d_out, nrm, x, gp, sig, qv, own, oth, keep, wout_own, wout_oth,
                 lin_own, lin_oth, gate_own, gate_oth, skip_row, dst, comp, summ, packed, dl, dg, dml):
    mine, other = own_cols(core, 256), oth_cols(core, 256)
    total = 0.0
    for i in range(0, dl.shape[0], TILE):
        rows = slice(i, i + TILE)
        grad = d_out(rows)
        dl[rows, :] = (grad * sig[rows, :].astype(f32)).astype(bf16)
        dg[rows, :] = (grad * qv[rows, :].astype(f32)).astype(bf16)
        d_active = (mm_nt(dl[rows, mine], lin_own[...]) + mm_nt(dg[rows, mine], gate_own[...])
                    + mm_nt(dl[rows, other], lin_oth[...]) + mm_nt(dg[rows, other], gate_oth[...]))
        d_mixed = d_active * gp[rows, :].astype(f32)
        _, normed = normalized(x[rows, :].astype(f32), nrm)
        total = total + jnp.sum(d_mixed * normed, axis=0, keepdims=True)
        low = d_mixed.astype(bf16)
        dml[rows, :] = low
        dst[rows, :256] = mm_nt(low, wout_own[...])
        dst[rows, 256:] = mm_nt(low, wout_oth[...])
    skip_row[0:1, :] = total
    lams = decay(own, oth, base, 6, conj=True)

    def drive(s, row, half):
        return dst[part(s, row), cols(half, 0)], dst[part(s, row), cols(half, 1)]

    ends = scan(drive, lams, keep, adj_which, steps, adj_reverse, zeros_start(), nothing)
    chunk_scan(ends, keep_products(keep, adj_which, steps), decay(own, oth, base, 9, conj=True), adj_reverse, comp, packed)
    spread(summ, packed)


def mixer_grads(act, dl, dg, sl, dml, l_own, l_oth, g_own, g_oth):
    _, core = place()
    mine, other = own_cols(core, 256), oth_cols(core, 256)
    left = act[...].T
    l_own[...] = mm(left, dl[:, mine]).astype(bf16)
    l_oth[...] = mm(left, dl[:, other]).astype(bf16)
    g_own[0:512, :] = mm(left, dg[:, mine]).astype(bf16)
    g_oth[0:512, :] = mm(left, dg[:, other]).astype(bf16)
    for ref, cut in ((g_own, slice(0, 256)), (g_oth, slice(256, 512))):
        left = sl[:, cut].T
        for i in range(2):
            ref[512 + 256 * i : 768 + 256 * i, :] = mm(left, dml[:, 256 * i : 256 * (i + 1)]).astype(ref.dtype)


def in_grads(nl, dp, g_own, g_oth):
    left = nl[...].T
    g_own[...] = mm(left, dp[:, :256]).astype(bf16)
    g_oth[...] = mm(left, dp[:, 256:]).astype(bf16)


def turn_kernel(peers, steps, got, comp_in, dk, own, oth, keep, proj, x, nrm, wout_own, wout_oth,
                lin_own, lin_oth, gate_own, gate_oth, perm, cot_own, cot_oth,
                cin, result, d_out, act, dl, dg, sl, dml, skip_row, dst, comp, summ,
                packed, held, gp, sig, qv, y):
    _, core = place()
    states_of(peers, steps, 16, 1, True, got, comp_in, dk, own, oth, keep, proj, cin, sl, packed, held)
    for _ in mix_and_gate(core, x, nrm, sl, wout_own, wout_oth, lin_own, lin_oth, gate_own, gate_oth, gp, act, sig, qv, y):
        pass
    result[...] = y[...].astype(bf16)
    d_out[:, own_cols(core, 256)] = mm(perm[0], flat_rows(cot_own)).astype(bf16)
    d_out[:, oth_cols(core, 256)] = mm(perm[0], flat_rows(cot_oth)).astype(bf16)
    glu_backward(steps, 16, 0, False, core, lambda rows: d_out[rows, :].astype(f32), nrm, x, gp, sig, qv, own, oth, keep, wout_own, wout_oth,
                 lin_own, lin_oth, gate_own, gate_oth, skip_row, dst, comp, summ, packed, dl, dg, dml)


def adjoint_part(peers, steps, base, keep_which, adj_which, adj_reverse, got, comp, dk, own, oth, keep, nl, x, nrm,
                 cin, sl, dst, dml, win_own, win_oth, skip_row, small_own, small_oth, all_rows, packed, held, proj, dp, keep_tile):
    _, core = place()
    device_carry(place()[0], peers, got, held, dk, adj_which, own, oth, base, True, adj_reverse, packed)
    start = entries(comp, packed)
    lams, sc = decay(own, oth, base, 6, conj=True), scales(own, oth, base)
    zero = jnp.zeros((CHUNKS, 128), f32)
    acc = {half: [zero, zero, zero] for half in range(2)}
    proj[:, :256] = mm(nl[...], win_own[...])
    proj[:, 256:] = mm(nl[...], win_oth[...])

    def prior(s, half, im):
        before = s - 1 if adj_reverse else s + 1
        if 0 <= before < steps:
            return sl[before * SLAB : (before + 1) * SLAB, cols(half, im)].astype(f32)
        return cin[:, cols(half, im)]

    def drive(s, row, half):
        return dst[part(s, row), cols(half, 0)], dst[part(s, row), cols(half, 1)]

    def visit(s, state, _):
        for half in range(2):
            prior_re, prior_im = prior(s, half, 0), prior(s, half, 1)
            for row in range(2):
                ar, ai = state[half, row]
                pr, pi = prior_re[part(0, row)], prior_im[part(0, row)]
                keep_here = keep[keep_which, part(s, row), :]
                acc[half][0] = acc[half][0] + keep_here * (ar * pr + ai * pi)
                acc[half][1] = acc[half][1] + keep_here * (ai * pr - ar * pi)
                acc[half][2] = acc[half][2] + (ar * proj[part(s, row), cols(half, 0)] + ai * proj[part(s, row), cols(half, 1)])
            for im in range(2):
                both = jnp.concatenate([sc[half] * state[half, row][im] for row in range(2)], axis=0)
                dp[s * SLAB : (s + 1) * SLAB, cols(half, im)] = both.astype(bf16)

    scan(drive, lams, keep, adj_which, steps, adj_reverse, start, visit)

    bias_row = gain_row = 0.0
    for i in range(0, dp.shape[0], TILE):
        rows = slice(i, i + TILE)
        d_normed = dml[rows, :].astype(f32) * nrm[4:5, :] + mm_nt(dp[rows, :256], win_own[...]) + mm_nt(dp[rows, 256:], win_oth[...])
        xhat, _ = normalized(x[rows, :].astype(f32), nrm)
        bias_row = bias_row + jnp.sum(d_normed, axis=0, keepdims=True)
        gain_row = gain_row + jnp.sum(d_normed * xhat, axis=0, keepdims=True)
        keep_tile(rows, d_normed)
    pack_two(bias_row, gain_row, packed)

    wanted = (skip_row[0:1, :], bias_row, gain_row) if all_rows else (skip_row[0:1, :],)
    for ref, half in ((small_own, 0), (small_oth, 1)):
        ref[...] = jnp.zeros_like(ref)
        at = 0
        for row in wanted:
            pick = jnp.where(core == half, row[:, :256], row[:, 256:])
            ref[at : at + 1, :] = pick[:, :128]
            ref[at + 1 : at + 2, :] = pick[:, 128:]
            at += 2
        for j in range(3):
            ref[at + j : at + j + 1, :] = jnp.sum(acc[half][j], axis=0, keepdims=True)


def adjoint_second_kernel(peers, steps, got, comp, dk, own, oth, keep, nl, x, nrm, cin, sl, dst, dml, win_own, win_oth, skip_row, act, dl, dg,
                          g_own, g_oth, small_own, small_oth, dn, stats, packed, held, proj, dp):
    def keep_tile(rows, d_normed):
        dn[rows, :] = d_normed

    adjoint_part(peers, steps, 16, 1, 0, False, got, comp, dk, own, oth, keep, nl, x, nrm,
                 cin, sl, dst, dml, win_own, win_oth, skip_row, small_own, small_oth, False, packed, held, proj, dp, keep_tile)
    spread(stats, packed)
    mixer_grads(act, dl, dg, sl, dml, g_own.at[:512], g_oth.at[:512], g_own.at[512:1536], g_oth.at[512:1536])
    in_grads(nl, dp, g_own.at[1536:], g_oth.at[1536:])


def back_first_kernel(steps, count, got, dn, x2, nrm2, d_out2, own, oth, keep, x, nrm, gp, sig, qv,
                      wout_own, wout_oth, lin_own, lin_oth, gate_own, gate_oth,
                      act, sl, d_out, dml, totals, l_own, l_oth, g_own, g_oth, skip_row, dst, comp, summ, packed, dl, dg):
    sums = sum_peers(got)
    bias_row, gain_row = row_of_tiles(sums[0:4]), row_of_tiles(sums[4:8])
    totals[...] = jnp.zeros_like(totals)
    totals[0:1, :], totals[1:2, :] = bias_row, gain_row
    mean, inv, gain = nrm2[0:1, :], nrm2[1:2, :], nrm2[2:3, :]
    scaled, shift, slope = inv * gain, inv * gain * bias_row / count, inv * inv * gain * gain_row / count

    def d_in(rows):
        value = d_out2[rows, :].astype(f32) + scaled * dn[rows, :] - shift - slope * (x2[rows, :] - mean)
        d_out[rows, :] = value
        return value

    glu_backward(steps, 0, 1, True, place()[1], d_in, nrm, x, gp, sig, qv, own, oth, keep, wout_own, wout_oth,
                 lin_own, lin_oth, gate_own, gate_oth, skip_row, dst, comp, summ, packed, dl, dg, dml)
    mixer_grads(act, dl, dg, sl, dml, l_own, l_oth, g_own, g_oth)


def adjoint_first_kernel(peers, steps, got, comp, dk, own, oth, keep, nl, x, nrm, cin, sl, dst, dml, win_own, win_oth, skip_row,
                         d_out, small1_own, small1_oth,
                         g_own, g_oth, small_own, partial, packed, held, proj, dp, small_oth):
    _, core = place()
    scaled = nrm[1:2, :] * nrm[2:3, :]

    def keep_tile(rows, d_normed):
        partial[rows, :] = (d_out[rows, :] + scaled * d_normed).astype(bf16)

    adjoint_part(peers, steps, 0, 0, 1, True, got, comp, dk, own, oth, keep, nl, x, nrm,
                 cin, sl, dst, dml, win_own, win_oth, skip_row, small_own, small_oth, True, packed, held, proj, dp, keep_tile)
    small_own[9:14, :] = small1_own[0:5, :]
    small_oth[9:14, :] = small1_oth[0:5, :]
    in_grads(nl, dp, g_own, g_oth.at[:512])
    put_small(g_oth, 512, small_oth[...])


def order_kernel(perm, result, partial, own, oth):
    _, core = place()
    for i, ref in enumerate((result, partial)):
        own[i] = mm(perm[1], ref[:, own_cols(core, 256)]).astype(bf16)
        oth[i] = mm(perm[1], ref[:, oth_cols(core, 256)]).astype(bf16)


def finish_kernel(count, packed, totals1, mine_parts, other_parts, tokens, nrm, raw,
                  block_out, d_in, ngg, bias, skip, rate_grad, angle_grad):
    _, core = place()
    for ref, j in ((skip, 0), (bias, 2), (ngg, 4)):
        ref[0:1, :128], ref[0:1, 128:] = packed[j : j + 1, :], packed[j + 1 : j + 2, :]
    skip[1:2, :128], skip[1:2, 128:] = packed[9:10, :], packed[10:11, :]
    bias[1:2, :] = totals1[0:1, own_cols(core, 256)]
    ngg[1:2, :] = totals1[1:2, own_cols(core, 256)]
    for k, at in ((0, 6), (1, 11)):
        values = raw[k : k + 1, :]
        rate = jnp.exp(values[:, 768:896])
        angle = jnp.exp(values[:, 896:])
        modulus = jnp.exp(-rate)
        scale = jnp.sqrt(1.0 - modulus * modulus)
        cos, sin = jnp.cos(angle), jnp.sin(angle)
        dr, di, ds = (packed[at + j : at + j + 1, :] for j in range(3))
        g_mod = dr * cos + di * sin - ds * modulus / scale
        rate_grad[k : k + 1, :] = -g_mod * modulus * rate
        angle_grad[k : k + 1, :] = modulus * (di * cos - dr * sin) * angle
    mine = nrm[:, own_cols(core, 256)]
    mean, inv, gain = mine[0:1, :], mine[1:2, :], mine[2:3, :]
    bias_row, gain_row = bias[0:1, :], ngg[0:1, :]
    flat = inv * gain / count
    for r in range(4):
        block_out[r] = jnp.where(core == r // 2, mine_parts[0, r % 2], other_parts[0, r % 2])
        held_rows = jnp.where(core == r // 2, mine_parts[1, r % 2].astype(f32), other_parts[1, r % 2].astype(f32))
        xhat = (tokens[r].astype(f32) - mean) * inv
        d_in[r] = held_rows - flat * (bias_row + xhat * gain_row)


def swap(value):
    return lax.ppermute(value, "state", [(0, 1), (1, 0)])


def to_all(value, axes):
    peers = 1
    for a in axes:
        peers *= lax.axis_size(a)
    return lax.all_to_all(jnp.broadcast_to(value[None], (peers,) + value.shape), axes, 0, 0)


def blocking(value, axes, others):
    value, others = lax.optimization_barrier((value, others))
    got, others = lax.optimization_barrier((lax.all_to_all(value, axes, 0, 0), others))
    return (got,), others


def gather_seq(value):
    if lax.axis_size("seq") != 16:
        return (to_all(value, ("seq",)),)
    near = jnp.stack([value] + [partner(value, m) for m in (1, 2, 3)])
    return (near,) + tuple(partner(near, m) for m in (4, 8, 12))


def sum_all(value):
    if lax.axis_size("seq") != 16:
        return (to_all(value, ("seq", "state")),)
    value = value + swap(value)
    near = value + partner(value, 1) + partner(value, 2) + partner(value, 3)
    return (near,) + tuple(partner(near, m) for m in (4, 8, 12))


def partner(value, mask):
    size = lax.axis_size("seq")
    return lax.ppermute(value, "seq", [(i, i ^ mask) for i in range(size)])


def partners(value, masks):
    size = lax.axis_size("seq")
    return lax.ppermute(value, ("seq", "state"), [(2 * i + c, 2 * (i ^ masks[c]) + c) for i in range(size) for c in range(2)])


def tie(value, others):
    return lax.optimization_barrier((value, others))


def bit_of(masks):
    me, core = place()
    return (me // jnp.where(core == 0, masks[0], masks[1])) & 1


def put_small(out, at, value):
    high = value.astype(bf16)
    rest = value - high.astype(f32)
    middle = rest.astype(bf16)
    low = (rest - middle.astype(f32)).astype(bf16)
    out[at : at + 16, :128], out[at : at + 16, 128:] = high, middle
    out[at + 16 : at + 32, :128], out[at + 16 : at + 32, 128:] = low, jnp.zeros_like(low)


def get_small(ref, at):
    return (ref[at : at + 16, :128].astype(f32) + ref[at : at + 16, 128:].astype(f32)) + ref[at + 16 : at + 32, :128].astype(f32)


def first_halves_kernel(masks, pairs, small, mine, other):
    bit, at = bit_of(masks), 0
    for own, got in pairs:
        half = own.shape[0] // 2
        for out, which in ((mine, bit), (other, 1 - bit)):
            rows = pl.ds(pl.multiple_of(which * half, half), half)
            out[at : at + half, :] = (own[rows, :].astype(f32) + got[rows, :].astype(f32)).astype(bf16)
        at += half
    if small is not None:
        total = small[...] + get_small(pairs[-1][1], pairs[-1][0].shape[0])
        put_small(mine, at, total)
        put_small(other, at, total)


def next_halves_kernel(masks, extra, held, got, mine, other):
    bit, half = bit_of(masks), mine.shape[0] - extra
    for out, which in ((mine, bit), (other, 1 - bit)):
        rows = pl.ds(pl.multiple_of(which * half, half), half)
        out[:half, :] = (held[rows, :].astype(f32) + got[rows, :].astype(f32)).astype(bf16)
    if extra:
        total = get_small(held, 2 * half) + get_small(got, 2 * half)
        put_small(mine, half, total)
        put_small(other, half, total)


def add_kernel(extra, held, got, total, *small):
    rows = held.shape[0] - extra
    total[:rows, :] = (held[:rows, :].astype(f32) + got[:rows, :].astype(f32)).astype(bf16)
    if extra:
        value = get_small(held, rows) + get_small(got, rows)
        if small:
            small[0][...] = value
        else:
            put_small(total, rows, value)


def axes_orders(*orders):
    masks, m = [], 1
    while m < lax.axis_size("seq"):
        masks.append(m)
        m *= 2
    return list(zip(*[[masks[i] for i in o] + masks[4:] for o in orders]))


class SeqSum:
    def __init__(self, pairs, masks, small=None):
        self.masks, self.at, self.small, self.extra = masks, 0, (), 0 if small is None else 32
        rows = sum(a.shape[0] for a, _ in pairs) // 2 + self.extra
        shape = ((rows, pairs[0][0].shape[1]), bf16)
        flat = tuple(v for p in pairs for v in p) + (() if small is None else (small,))

        def kernel(refs, mine, other):
            count = 2 * len(pairs)
            first_halves_kernel(masks[0], [(refs[i], refs[i + 1]) for i in range(0, count, 2)],
                                None if small is None else refs[count], mine, other)

        self.mine, self.send = run(kernel, [shape, shape], (flat,))

    def step(self):
        count, i = len(self.masks), self.at
        self.at += 1
        if i < count:
            got = partners(self.send, self.masks[i])
            rows, width = got.shape
            rows -= self.extra
            if i + 2 < count:
                shape = ((rows // 2 + self.extra, width), bf16)
                self.mine, self.send = run(functools.partial(next_halves_kernel, self.masks[i + 1], self.extra), [shape, shape], (self.mine, got))
            elif i + 2 == count:
                (self.send,) = run(functools.partial(add_kernel, self.extra), [((rows + self.extra, width), bf16)], (self.mine, got))
            else:
                outs = [((rows, width), bf16)] + ([((16, 128), f32)] if self.extra else [])
                self.send, *self.small = run(functools.partial(add_kernel, self.extra), outs, (self.send, got))
            return False
        mask = self.masks[2 * count - 2 - i]
        got = partners(self.send, mask)
        if i + 2 == 2 * count:
            self.result = (self.send, got)
            return True
        bit = bit_of(mask)
        self.send = jnp.concatenate([jnp.where(bit == 0, self.send, got), jnp.where(bit == 0, got, self.send)], axis=0)
        return False

    def after(self, values):
        self.send = tie(self.send, values)[0]

    def before(self, value):
        value, self.send = tie(value, self.send)
        return value


class Leaving:
    def __init__(self, sem):
        self.sem, self.copies = sem, []

    def send(self, source, target):
        copy = pltpu.make_async_copy(source, target, self.sem.at[len(self.copies)])
        copy.start()
        self.copies.append(copy)

    def wait(self):
        for copy in self.copies:
            copy.wait()


def put_entry(entry, ref, at, start, rows):
    value = ref[at : at + rows, :].astype(f32)
    entry[pl.ds(2 * start, rows, stride=2), :] = value[:, :128]
    entry[pl.ds(2 * start + 1, rows, stride=2), :] = value[:, 128:]


def on_half(mine, got, masks, half, put):
    bit = bit_of(masks)
    for ref, which in ((mine, bit), (got, 1 - bit)):

        @pl.when(which == half)
        def _():
            put(ref, lambda at, rows: ref[at : at + rows, :].astype(f32))


def unpack_second_kernel(masks, mine, got, lin_out, gate_out, out_out, entry_out, lin, gate, out, entry, sem):
    leaving = Leaving(sem)

    def low(ref, piece):
        lin[1], gate[...], lin[0, :256] = piece(0, 512), piece(512, 512), piece(1024, 256)

    def high(ref, piece):
        out[:, :256], out[:, 256:], lin[0, 256:] = piece(0, 256), piece(256, 256), piece(1024, 256)
        put_entry(entry, ref, 512, 0, 512)

    on_half(mine, got, masks, 0, low)
    leaving.send(gate, gate_out.at[1])
    on_half(mine, got, masks, 1, high)
    leaving.send(lin, lin_out)
    leaving.send(out, out_out.at[1])
    leaving.send(entry, entry_out.at[1])
    leaving.wait()


def unpack_first_kernel(masks, mine, got, gate_in, out_in, entry_in, gate_out, out_out, entry_out, gate, out, entry, sem):
    leaving = Leaving(sem)

    def low(ref, piece):
        gate[...] = piece(0, 512)
        put_entry(entry, ref, 512, 0, 256)

    def high(ref, piece):
        out[:, :256], out[:, 256:] = piece(0, 256), piece(256, 256)
        put_entry(entry, ref, 512, 256, 256)

    on_half(mine, got, masks, 0, low)
    leaving.send(gate, gate_out.at[0])
    on_half(mine, got, masks, 1, high)
    leaving.send(out, out_out.at[0])
    leaving.send(entry, entry_out.at[0])
    leaving.wait()


def unpack(second, second_masks, first, first_masks):
    far, near = pl.BlockSpec(memory_space=pltpu.HBM), pl.BlockSpec(memory_space=pltpu.VMEM)
    lin, gate, out, entry = (jax.ShapeDtypeStruct(s, f32) for s in ((2, 512, 256), (2, 512, 256), (2, 256, 512), (2, 1024, 128)))
    parts = [pltpu.VMEM(a.shape[1:], f32) for a in (gate, out, entry)]
    params = pltpu.CompilerParams(vmem_limit_bytes=24 * 2**20)
    lin_grad, *rest = pl.pallas_call(
        functools.partial(unpack_second_kernel, second_masks),
        out_shape=[lin, gate, out, entry], in_specs=[near] * 2, out_specs=[far] * 4,
        scratch_shapes=[pltpu.VMEM(lin.shape, f32)] + parts + [pltpu.SemaphoreType.DMA((4,))],
        compiler_params=params)(*second)
    rest = pl.pallas_call(
        functools.partial(unpack_first_kernel, first_masks),
        out_shape=[gate, out, entry], in_specs=[near] * 2 + [far] * 3, out_specs=[far] * 3,
        scratch_shapes=parts + [pltpu.SemaphoreType.DMA((3,))],
        input_output_aliases={2: 0, 3: 1, 4: 2},
        compiler_params=params)(*first, *rest)
    return [lin_grad, *rest]


class Far:
    def __init__(self, value, at=None, smem=False):
        self.value, self.at, self.smem = value, at, smem
        self.shape = value.shape if at is None else value.shape[1:] if at != "rows" else (2,) + value.shape[1:]

    def source(self, ref):
        if self.at is None:
            return ref
        return ref.at[pl.ds(lax.axis_index("state") * 2, 2)] if self.at == "rows" else ref.at[self.at]


class Part:
    def __init__(self, value, at):
        self.value, self.at = value, at

    def view(self, ref):
        return ref.at[pl.ds(lax.axis_index("state") * 2, 2)] if self.at == "rows" else ref.at[self.at]


class Held:
    def __init__(self, source, ref, sem):
        self.ref, self.copy, self.shape, self.dtype = ref, pltpu.make_async_copy(source, ref, sem), ref.shape, ref.dtype
        self.copy.start()

    def ready(self):
        if self.copy is not None:
            self.copy.wait()
            self.copy = None

    def __getitem__(self, index):
        self.ready()
        return self.ref[index]


def run(kernel, outs, groups, scratch=(), limit=24, flops=0, smem=None):
    args = [a for g in groups for a in (g if isinstance(g, tuple) else (g,))]
    far_in = [i for i, a in enumerate(args) if isinstance(a, Far)]
    arrays = [a.value if isinstance(a, (Far, Part)) else a for a in args]
    moved = sum(a.size * a.dtype.itemsize for a in arrays)

    def whole(*refs):
        ins, results = list(refs[: len(args)]), list(refs[len(args) : len(args) + len(outs)])
        rest = refs[len(args) + len(outs) :]
        own = rest[: len(scratch)]
        if far_in:
            buffers, sem = rest[len(scratch) : -1], rest[-1]
        for j, i in enumerate(far_in):
            ins[i] = Held(args[i].source(ins[i]), buffers[j], sem.at[j])
        ins = [a.view(r) if isinstance(a, Part) else r for r, a in zip(ins, args)]
        grouped, at = [], 0
        for g in groups:
            if isinstance(g, tuple):
                grouped.append(tuple(ins[at : at + len(g)]))
                at += len(g)
            else:
                grouped.append(ins[at])
                at += 1
        kernel(*grouped, *results, *own)
        for i in far_in:
            ins[i].ready()

    def space(far):
        return pl.BlockSpec(memory_space=pltpu.HBM if far else pltpu.VMEM)

    held = [(pltpu.SMEM if args[i].smem else pltpu.VMEM)(args[i].shape, args[i].value.dtype) for i in far_in]
    if held:
        held.append(pltpu.SemaphoreType.DMA((len(held),)))
    return pl.pallas_call(
        whole,
        out_shape=[jax.ShapeDtypeStruct(o[0], o[1]) for o in outs],
        in_specs=[pl.BlockSpec(memory_space=pltpu.SMEM) if a is smem else space(isinstance(a, Far)) for a in args],
        out_specs=[space(False)] * len(outs),
        scratch_shapes=[pltpu.VMEM(*s) for s in scratch] + held,
        compiler_params=pltpu.CompilerParams(vmem_limit_bytes=limit * 2**20),
        cost_estimate=pl.CostEstimate(flops=flops, bytes_accessed=moved, transcendentals=0),
    )(*arrays)


def body(tokens, gain, bias, in_proj, out_proj, rate_log, angle_log, skip, glu_lin, glu_gate, positions, cotangent):
    peers = lax.axis_size("seq")
    core = lax.axis_index("state")
    rows, span, width = tokens.shape
    steps = span // CHUNKS
    n = 2 * span
    count = float(rows * span * peers)
    packed = ((8, 128), f32)
    one = 2 * n * 512 * 512
    low = ((n, 512), bf16)
    full = ((n, 512), f32)

    (stats,) = run(stats_kernel, [((2 * peers, 4, 128), f32)], (tokens,))
    raw, at = 0.0, 0
    for v in (gain, bias, skip, rate_log, angle_log):
        raw, at = raw + jnp.pad(v.astype(f32), ((0, 0), (at, 1024 - at - v.shape[1]))), at + v.shape[1]
    w_in = in_proj.reshape(2, 512, 256)
    w_out = out_proj.reshape(2, 256, 512)
    x_oth, cot_oth, in_oth, out_oth, lin_oth, gate_oth = (swap(w) for w in (tokens, cotangent, w_in, w_out, glu_lin, glu_gate))
    enter = [(Part(w_in, k), Part(in_oth, k)) for k in range(2)]
    own, keep, dk, perm = run(
        functools.partial(prep_kernel, peers, steps, span),
        [((32, 128), f32), ((2, n, 128), f32), ((2, peers, 8, 128), f32), ((2, n, n), bf16)],
        (positions, raw), smem=positions)
    oth = swap(own)
    ordered = ((peers, 8, 128), f32)

    for_seq, for_all = ((peers, 8, 128), f32), ((2 * peers, 8, 128), f32)
    scan_outs = [full, ((16, 8, 128), f32), for_seq, ((8, 512), f32)]
    xp, nl0, proj, comp, summ, nrm0 = run(
        functools.partial(enter_first_kernel, peers, steps, count), [low, low] + scan_outs,
        (lax.all_to_all(stats, ("seq", "state"), 0, 0), Part(tokens, "rows"), Part(x_oth, "rows"), perm, own, oth, keep) + enter[0], [packed], flops=2 * one)
    got, (cot_oth, out_oth, lin_oth, gate_oth) = blocking(summ, "seq", (cot_oth, out_oth, lin_oth, gate_oth))
    glu = [tuple((Part if i % 2 else Part)(w, k) for i, w in enumerate((w_out, out_oth, glu_lin, lin_oth, glu_gate, gate_oth))) for k in range(2)]
    cin0, sl0, gp0, act0, sig0, qv0, y0, stats = run(
        functools.partial(leave_first_kernel, peers, steps),
        [((SLAB, 512), f32), low, low, low, low, low, full, for_all],
        (got, comp, dk, own, oth, keep, proj, xp, nrm0) + glu[0], [packed, ordered], flops=3 * one)
    got, _ = blocking(stats, ("seq", "state"), ())
    nl1, proj, comp, summ, nrm1 = run(
        functools.partial(enter_second_kernel, peers, steps, count), [low] + scan_outs,
        (got, y0, own, oth, keep) + enter[1], [packed], flops=one)
    got, _ = blocking(summ, "seq", ())
    turn_outs = [((8, 512), f32), full, ((16, 8, 128), f32)]
    cin1, result, d_out1, act1, dl1, dg1, sl1, dml1, skip1, dst, comp, summ = run(
        functools.partial(turn_kernel, peers, steps),
        [((SLAB, 512), f32), low, low, low, low, low, low, low] + turn_outs + [for_seq],
        (got, comp, dk, own, oth, keep, proj, y0, nrm1) + glu[1] + (perm, Part(cotangent, "rows"), Part(cot_oth, "rows")),
        [packed, ordered, full, full, full, full], flops=8 * one)
    got, _ = blocking(summ, "seq", ())
    g1_own, g1_oth, s1_own, s1_oth, dn, stats = run(
        functools.partial(adjoint_second_kernel, peers, steps),
        [((2048, 256), bf16), ((2048, 256), bf16), ((8, 128), f32), ((8, 128), f32), full, for_all],
        (got, comp, dk, own, oth, keep, nl1, y0, nrm1, cin1, sl1, dst, dml1) + enter[1] + (skip1, act1, dl1, dg1),
        [packed, ordered, full, low], flops=6 * one)
    got, (g1_oth,) = blocking(stats, ("seq", "state"), (g1_oth,))
    g1_got = swap(g1_oth)
    d_out0, dml0, totals1, l0_own, l0_oth, g0_own, g0_oth, skip0, dst, comp, summ = run(
        functools.partial(back_first_kernel, steps, count),
        [full, low, ((8, 512), f32), ((512, 256), bf16), ((512, 256), bf16), ((1024, 256), bf16), ((1024, 256), bf16)] + turn_outs + [for_seq],
        (got, dn, y0, nrm1, d_out1, own, oth, keep, xp, nrm0, gp0, sig0, qv0) + glu[0] + (act0, sl0),
        [packed, low, low], flops=6 * one)
    got, (l0_oth, g0_oth, g1_got, result) = blocking(summ, "seq", (l0_oth, g0_oth, g1_got, result))
    l0_got, g0_got = swap(l0_oth), swap(g0_oth)
    i0_own, i0_oth, s_own, partial = run(
        functools.partial(adjoint_first_kernel, peers, steps),
        [((512, 256), bf16), ((544, 256), bf16), ((16, 128), f32), low],
        (got, comp, dk, own, oth, keep, nl0, xp, nrm0, cin0, sl0, dst, dml0) + enter[0]
        + (skip0, d_out0, s1_own, s1_oth),
        [packed, ordered, full, low, ((16, 128), f32)], flops=3 * one)
    i0_got = swap(i0_oth)
    bulk1 = SeqSum([(g1_own, g1_got), (l0_own, l0_got)], axes_orders((0, 1, 2, 3), (1, 0, 2, 3)))
    bulk0 = SeqSum([(g0_own, g0_got), (i0_own, i0_got)], axes_orders((2, 1, 0, 3), (2, 0, 1, 3)), s_own)
    own_parts, oth_parts = run(order_kernel, [((2, n, 256), bf16)] * 2, (perm, result, partial), flops=2 * one)
    got_parts = swap(oth_parts)
    for bulk in (bulk1, bulk0):
        while not bulk.step():
            pass
    quad = (2, 2, span, width)
    block_out, d_in, ngg, bias_grad, skip_grad, rate_grad, angle_grad = run(
        functools.partial(finish_kernel, count),
        [((rows, span, width), bf16), ((rows, span, width), f32), ((2, 256), f32), ((2, 256), f32), ((2, 256), f32), ((2, 128), f32), ((2, 128), f32)],
        (bulk0.small[0], totals1, own_parts.reshape(quad), got_parts.reshape(quad), tokens, nrm0, raw))
    lin_grad, gate_grad, out_grad, in_grad = unpack(bulk1.result, bulk1.masks[0], bulk0.result, bulk0.masks[0])
    out_grad, in_grad = out_grad.reshape(2, 2, 128, 512), in_grad.reshape(2, 512, 2, 128)
    return (block_out, d_in, ngg, bias_grad, in_grad, out_grad, rate_grad, angle_grad, skip_grad, lin_grad, gate_grad)


def solution(mesh):
    placed = (
        P(None, "seq", "state"),
        P(None, "state"),
        P(None, "state"),
        P(None, None, None, "state"),
        P(None, None, "state", None),
        P(None, "state"),
        P(None, "state"),
        P(None, "state"),
        P(None, None, "state"),
        P(None, None, "state"),
        P(),
        P(None, "seq", "state"),
    )
    return jax.shard_map(
        body,
        mesh=mesh,
        in_specs=placed,
        out_specs=(
            P(None, "seq", "state"),
            P(None, "seq", "state"),
            P(None, "state"),
            P(None, "state"),
            P(None, None, None, "state"),
            P(None, None, "state", None),
            P(None, "state"),
            P(None, "state"),
            P(None, "state"),
            P(None, None, "state"),
            P(None, None, "state"),
        ),
        check_vma=False,
    )
```
